128 devices in a mesh: row: 8 (over x, z_lo), col: 16 (over y, z_hi, core).
Axes of the slice: x: 4, y: 4, z: 4 (z_hi: 2, z_lo: 2; z = z_hi * 2 + z_lo), core: 2. Of those that a mesh axis runs over, the one named last changes fastest.
Arguments:
- hidden_in: bfloat16 [2048, 16384], P('col', 'row'), may hold values from -4 to 4
- segment_ids: int32 [2048], replicated, may hold values from 0 to 7, never falling along the last dimension, each value on 1 to 512 neighbouring positions
- q_weight: bfloat16 [16384, 16384], P(('row', 'col')), may hold values from -1 to 1
- k_weight: bfloat16 [16384, 1024], P(('row', 'col')), may hold values from -0.03203125 to 0.03203125
- value_weight: bfloat16 [16384, 1024], P(('row', 'col')), may hold values from -0.046875 to 0.046875
- out_weight: bfloat16 [16384, 16384], P(('row', 'col')), may hold values from -0.046875 to 0.046875
Outputs:
- mixed: bfloat16 [2048, 16384], P('col', 'row')
The draws below stay inside these ranges and needn't reach their ends.
All inputs are finite; a program needn't handle non-finite values.
Results may differ from the reference program's by a relative error of at most 0.039.
Values may be sent and summed in bfloat16 or wider, within the bound.
A program may use at most 128 MiB of HBM per device.

```python
import math
import jax
import jax.numpy as jnp
import numpy as np
from jax import lax

MODEL_WIDTH = 16384
QUERY_HEADS = 128
KEY_VALUE_HEADS = 8
HEAD_SIZE = 128
TOKENS = 2048
N_ROW = 8
N_COL = 16


def shared_keys(key):
    return jax.random.truncated_normal(key, -4.0, 4.0, (MODEL_WIDTH, KEY_VALUE_HEADS * HEAD_SIZE), jnp.float32) * MODEL_WIDTH ** (-0.5)


def draw_k_weight(key, part):
    base_offset = shared_keys(key)
    return base_offset.astype(jnp.bfloat16)


def draw_q_weight(key, part):
    key = jax.random.fold_in(key, 3)
    own = jax.random.truncated_normal(jax.random.fold_in(key, 1), -4.0, 4.0, (MODEL_WIDTH, QUERY_HEADS * HEAD_SIZE), jnp.float32) * MODEL_WIDTH ** (-0.5)
    return own.astype(jnp.bfloat16)


def draw_hidden_in(key, part):
    key = jax.random.fold_in(key, 1)
    return jax.random.truncated_normal(key, -4.0, 4.0, (TOKENS, MODEL_WIDTH), jnp.float32).astype(jnp.bfloat16)


def shard_levels(own_key, shape, cuts, smallest, top_value):
    level = 1.0
    for dim, parts in cuts:
        steps = jax.random.uniform(jax.random.fold_in(jax.random.fold_in(own_key, 6), dim), (parts,), jnp.float32, smallest / len(cuts), top_value / len(cuts))
        level = level * jnp.repeat(jnp.exp(steps), shape[dim] // parts).reshape((-1,) + (1,) * (len(shape) - 1 - dim))
    return level


def profile(amount, total, most, slope):
    loads = [(1 << 20) // math.isqrt(grade ** slope) + 1 for grade in range(2, amount + 1)]
    spare, counts = total - most - (amount - 1), [1] * (amount - 1)
    while spare > 0:
        free = [i for i in range(amount - 1) if counts[i] < most]
        pool, remaining = sum([loads[i] for i in free]), spare
        for i in free:
            more = min(most - counts[i], max(1, remaining * loads[i] // pool), spare)
            counts[i] = counts[i] + more
            spare = spare - more
    return np.array([most] + counts)


def uneven_parts(key, amount, total, bound, slope):
    if amount == 2:
        one = jax.random.randint(key, (), max(1, total - bound), min(bound, total - 1) + 1)
        return jnp.stack([one, total - one])
    tallies = jnp.asarray(profile(amount, total, bound, slope), jnp.int32)
    pairs = (amount - 1) // 2
    donor, sink = tallies[1:1 + 2 * pairs:2], tallies[2:2 + 2 * pairs:2]
    slack = jnp.minimum(donor - 1, bound - sink)
    shifted = jax.random.randint(jax.random.fold_in(key, 1), (pairs,), 0, 1 << 20) % (slack + 1)
    tallies = tallies.at[1:1 + 2 * pairs:2].set(donor - shifted).at[2:2 + 2 * pairs:2].set(sink + shifted)
    return tallies[jax.random.permutation(jax.random.fold_in(key, 2), amount)]


def noise(stream_key, extent, scale, reach, split=(), kind=jnp.bfloat16):
    values = jax.random.normal(stream_key, extent, jnp.float32) * scale
    if len(split) > 0:
        values = shard_levels(stream_key, extent, split, -0.22, 0.18) * values
    return jnp.clip(values, min=-reach, max=reach).astype(kind)


def setup_inputs(seed: int = 0) -> dict:
    keys = jax.random.split(jax.random.key(seed), 7)
    hidden_in = draw_hidden_in(jax.random.fold_in(keys[6], 71), 0)
    segment_ids = jnp.searchsorted(jnp.cumsum(uneven_parts(keys[1], 8, TOKENS, TOKENS // 4, 0)), jnp.arange(TOKENS), side="right").astype(jnp.int32)
    q_weight = draw_q_weight(jax.random.fold_in(keys[6], 71), 0)
    k_weight = draw_k_weight(jax.random.fold_in(keys[6], 71), 0)
    value_weight = noise(keys[4], (MODEL_WIDTH, KEY_VALUE_HEADS * HEAD_SIZE), MODEL_WIDTH ** -0.5, 0.046875, ((0, 128),))
    out_weight = noise(keys[5], (MODEL_WIDTH, QUERY_HEADS * HEAD_SIZE), (QUERY_HEADS * HEAD_SIZE) ** -0.5, 0.046875, ((0, 128),))
    return dict(hidden_in=hidden_in, segment_ids=segment_ids, q_weight=q_weight, k_weight=k_weight, value_weight=value_weight, out_weight=out_weight)


THETA = 500000.0
NEGATIVE = -1e+30

def apply_rotation(vectors, token_positions):
    half_width = vectors.shape[-1] // 2
    indices = jnp.arange(half_width, dtype=jnp.float32)
    inverse = jnp.power(jnp.float32(THETA), -2.0 * indices / (2 * half_width))
    angles = token_positions.astype(jnp.float32)[:, None] * inverse[None, :]
    cosine = jnp.cos(angles)[:, None, :]
    sine_part = jnp.sin(angles)[:, None, :]
    front_half = vectors[..., :half_width]
    back_half = vectors[..., half_width:]
    return jnp.concatenate([front_half * cosine - back_half * sine_part, back_half * cosine + front_half * sine_part], axis=-1)

def reference(hidden_in, segment_ids, q_weight, k_weight, value_weight, out_weight):
    token_total = hidden_in.shape[0]
    block_width = MODEL_WIDTH // N_ROW
    width_of_queries = QUERY_HEADS * HEAD_SIZE
    key_value_width = KEY_VALUE_HEADS * HEAD_SIZE
    projected_rows = jnp.zeros((token_total, width_of_queries + 2 * key_value_width), jnp.float32)
    for block in range(N_ROW):
        lower = block * block_width
        inputs_block = hidden_in[:, lower:lower + block_width]
        partial_value = jnp.concatenate([jnp.dot(inputs_block, q_weight[lower:lower + block_width], preferred_element_type=jnp.float32), jnp.dot(inputs_block, k_weight[lower:lower + block_width], preferred_element_type=jnp.float32), jnp.dot(inputs_block, value_weight[lower:lower + block_width], preferred_element_type=jnp.float32)], axis=1)
        projected_rows = projected_rows + lax.optimization_barrier(partial_value.astype(jnp.bfloat16)).astype(jnp.float32)
    token_positions = jnp.arange(token_total, dtype=jnp.int32)
    queries = apply_rotation(projected_rows[:, :width_of_queries].reshape(token_total, QUERY_HEADS, HEAD_SIZE), token_positions).astype(jnp.bfloat16)
    block_of_keys = apply_rotation(projected_rows[:, width_of_queries:width_of_queries + key_value_width].reshape(token_total, KEY_VALUE_HEADS, HEAD_SIZE), token_positions).astype(jnp.bfloat16)
    block_of_values = projected_rows[:, width_of_queries + key_value_width:].reshape(token_total, KEY_VALUE_HEADS, HEAD_SIZE).astype(jnp.bfloat16)
    head_major = jnp.transpose(queries, (1, 0, 2))
    keys_major = jnp.transpose(block_of_keys, (1, 0, 2))
    values_major = jnp.transpose(block_of_values, (1, 0, 2))
    index_in_group = jnp.arange(QUERY_HEADS, dtype=jnp.int32) // (QUERY_HEADS // KEY_VALUE_HEADS)
    allowed = (token_positions[None, :] <= token_positions[:, None]) & (segment_ids[None, :] == segment_ids[:, None])
    scale = 1.0 / math.sqrt(HEAD_SIZE)

    def one_head(carried):
        query_head, group = carried
        key_head = keys_major[group]
        value_head = values_major[group]
        scores = jnp.dot(query_head, key_head.T, preferred_element_type=jnp.float32) * scale
        scores = jnp.where(allowed, scores, NEGATIVE)
        largest = lax.optimization_barrier(jnp.max(scores, axis=-1, keepdims=True))
        exponent = jnp.exp(scores - largest)
        denominator = lax.optimization_barrier(jnp.sum(exponent, axis=-1, keepdims=True))
        probabilities = (exponent / denominator).astype(jnp.bfloat16)
        return jnp.dot(probabilities, value_head, preferred_element_type=jnp.float32).astype(jnp.bfloat16)
    attended = lax.map(one_head, (head_major, index_in_group))
    attended = jnp.transpose(attended, (1, 0, 2)).reshape(token_total, width_of_queries)
    out_width = width_of_queries // N_COL
    mixed = jnp.zeros((token_total, MODEL_WIDTH), jnp.float32)
    for block in range(N_COL):
        lower = block * out_width
        partial_value = lax.dot_general(attended[:, lower:lower + out_width], out_weight[:, lower:lower + out_width], (((1,), (1,)), ((), ())), preferred_element_type=jnp.float32)
        mixed = mixed + lax.optimization_barrier(partial_value.astype(jnp.bfloat16)).astype(jnp.float32)
    return mixed.astype(jnp.bfloat16)
```

```python
import math

import jax
import jax.numpy as jnp
import numpy as np
from jax import lax
from jax.experimental import pallas as pl
from jax.experimental.pallas import tpu as pltpu
from jax.sharding import PartitionSpec as P

HEAD = 128
BLOCK = 128
THETA = 500000.0
NEGATIVE = -1e30
SEMAPHORES = 300
WINDOW = 5
F32 = jnp.float32
BF16 = jnp.bfloat16
MESH = pl.DeviceIdType.MESH


class Place:
    def __init__(self):
        row, col = lax.axis_index("row"), lax.axis_index("col")
        self.x, self.zl = lax.div(row, 2), lax.rem(row, 2)
        self.y, self.zh, self.c = lax.div(col, 4), lax.rem(lax.div(col, 2), 2), lax.rem(col, 2)
        self.col = col
        self.oc = 1 - self.c
        x, y, zl, zh = self.x, self.y, self.zl, self.zh
        self.ya, self.yb = y + 1 - 2 * lax.rem(y, 2), 3 - y
        self.yab = 3 - self.ya
        self.xa, self.xb = x + 1 - 2 * lax.rem(x, 2), 3 - x
        self.bits = (lax.div(x, 2), lax.rem(x + lax.div(x, 2), 2), zh, lax.rem(zl + zh, 2))
        self.partners = (
            self.dev(x=self.xb),
            self.dev(x=self.xa),
            self.dev(zh=1 - zh, zl=1 - zl),
            self.dev(zl=1 - zl),
        )
        self.token_block = (
            8 * self.bits[0] + 4 * self.bits[1] + 2 * self.bits[2] + self.bits[3]
        )

    def dev(self, **k):
        g = lambda n: k.get(n, getattr(self, n))
        return (2 * g("x") + g("zl"), 4 * g("y") + 2 * g("zh") + g("c"))

    def ycore_partners(self):
        return [
            self.dev(c=self.oc),
            self.dev(y=self.ya),
            self.dev(y=self.ya, c=self.oc),
            self.dev(y=self.yb),
            self.dev(y=self.yb, c=self.oc),
        ]

    def block_dev(self, t):
        t = lax.rem(t + 16, 16)
        n0, n1 = lax.div(t, 8), lax.rem(lax.div(t, 4), 2)
        n2, n3 = lax.rem(lax.div(t, 2), 2), lax.rem(t, 2)
        return self.dev(x=2 * n0 + lax.rem(n0 + n1, 2), zh=n2, zl=lax.rem(n2 + n3, 2))

    def all_partners(self):
        window = [self.block_dev(self.token_block + d) for i in range(1, WINDOW) for d in (i, -i)]
        return (
            self.ycore_partners() + [self.dev(zh=1 - self.zh)] + list(self.partners) + window
        )


def order(s):
    return [(s + k) % 4 for k in range(4)]


def barrier(devices):
    sem = pltpu.get_barrier_semaphore()
    for d in devices:
        pl.semaphore_signal(sem, inc=1, device_id=d, device_id_type=MESH)
    pl.semaphore_wait(sem, len(devices))


class Net:
    def __init__(self, send, recv):
        self.send, self.recv, self.n, self.open = send, recv, 0, []

    def remote(self, src, dst, dev):
        i = self.n
        self.n += 1
        cp = pltpu.make_async_remote_copy(
            src, dst, self.send.at[i], self.recv.at[i], device_id=dev, device_id_type=MESH
        )
        cp.start()
        self.open.append(cp)
        return cp

    def local(self, src, dst):
        i = self.n
        self.n += 1
        cp = pltpu.make_async_copy(src, dst, self.recv.at[i])
        cp.start()
        return cp

    def finish(self):
        for cp in self.open:
            cp.wait_send()
        self.open = []


def rows(i, n=1):
    return pl.ds(pl.multiple_of(i * BLOCK, BLOCK), n * BLOCK)


class Relay:
    def __init__(self, net, p, src, dst, rel):
        self.net, self.p, self.dst, self.rel = net, p, dst, rel
        y, c, oc = p.y, p.c, p.oc
        mine = dst.at[rows(2 * y + c)]
        self.ra = net.remote(src(2 * p.yab + c), rel.at[0], p.dev(y=p.ya))
        self.rb = net.remote(src(2 * p.yab + oc), rel.at[1], p.dev(y=p.yb))
        self.waits = [
            net.remote(src(2 * p.ya + c), mine, p.dev(y=p.ya)),
            net.remote(src(2 * p.yb + c), mine, p.dev(y=p.yb)),
            net.remote(src(2 * p.ya + oc), mine, p.dev(y=p.ya, c=oc)),
            net.remote(src(2 * p.yb + oc), mine, p.dev(y=p.yb, c=oc)),
            net.remote(src(2 * y + oc), mine, p.dev(c=oc)),
        ]
        self.own = net.local(src(2 * y + c), mine)

    def forward(self):
        p, net = self.p, self.net
        self.ra.wait_recv()
        self.waits.append(
            net.remote(self.rel.at[0], self.dst.at[rows(2 * p.ya + p.c)], p.dev(y=p.yb))
        )
        self.rb.wait_recv()
        self.waits.append(
            net.remote(
                self.rel.at[1], self.dst.at[rows(2 * p.yb + p.c)], p.dev(y=p.ya, c=p.oc)
            )
        )

    def wait(self):
        self.own.wait()
        for cp in self.waits:
            cp.wait_recv()


def prefix(bits, o, k):
    total = 0
    for i in range(k):
        total = total + bits[o[i]] * (8 >> i)
    return total


def tables():
    inverse = np.power(np.float32(THETA), -2.0 * np.arange(64, dtype=np.float32) / HEAD)
    angles = np.arange(2048, dtype=np.float32)[:, None] * inverse.astype(np.float32)[None, :]
    angles = angles.astype(np.float64)
    cos, sin = np.cos(angles), np.sin(angles)
    cos = np.concatenate([cos, cos], axis=1).astype(np.float32)
    sin = np.concatenate([-sin, sin], axis=1).astype(np.float32)
    return cos, sin


def kernel(
    h_ref, seg_ref, cos_ref, sin_ref, q_ref, k_ref, v_ref, o_ref,
    out_ref,
    hx, xs, wkv, wq, relkv, relq, part, r0, r1, r2, r3, cos, sin, kv, bias,
    att, wo, relo, acc, po, rc, ry1, ry2, fin, send, recv,
):
    p = Place()
    net = Net(send, recv)
    recvs = (r0, r1, r2, r3)
    for z in range(2):
        for yy in range(4):
            hx[z, :, yy * 256 : (yy + 1) * 256] = h_ref[
                :, yy * 512 + z * 256 : yy * 512 + z * 256 + 256
            ]
    xs[rows(p.col)] = hx[p.zh]
    barrier(p.all_partners())

    def columns(ref, width, j=0, chunk=None):
        chunk = chunk or width
        return lambda d: ref.at[:, pl.ds(pl.multiple_of(d * width + j * chunk, chunk), chunk)]

    weights = {}

    def start_weights(t):
        if t == 0:
            weights[t] = [
                Relay(net, p, columns(k_ref, HEAD), wkv.at[0], relkv.at[0]),
                Relay(net, p, columns(v_ref, HEAD), wkv.at[1], relkv.at[1]),
            ]
        elif t < 5:
            j = t - 1
            weights[t] = [Relay(net, p, columns(q_ref, 2048, j, 512), wq.at[j], relq.at[j])]
        else:
            j = t - 5
            weights[t] = [Relay(net, p, columns(o_ref, 2048, j, 512), wo.at[j], relo.at[j])]

    def forward_weights(t):
        for w in weights[t]:
            w.forward()

    def wait_weights(t):
        for w in weights[t]:
            w.wait()

    def xrows(y, zh, c):
        return xs.at[rows(4 * y + 2 * zh + c)]

    def push(block, dev):
        return net.remote(block, block, dev)

    to_a, to_b, to_core = p.dev(y=p.ya), p.dev(y=p.yb), p.dev(c=p.oc)
    oz = 1 - p.zh
    swap = net.remote(hx.at[oz], xs.at[rows(p.col)], p.dev(zh=oz))
    first = xrows(p.y, p.zh, p.c)
    a1, b1, c1 = push(first, to_a), push(first, to_b), push(first, to_core)
    table_copies = [
        net.local(cos_ref.at[rows(p.token_block)], cos),
        net.local(sin_ref.at[rows(p.token_block)], sin),
    ]
    start_weights(0)
    seg_q = jnp.transpose(
        jnp.broadcast_to(seg_ref[pl.ds(p.token_block, 1), :], (BLOCK, BLOCK))
    )
    lane = lax.broadcasted_iota(jnp.int32, (BLOCK, BLOCK), 1)
    query = p.token_block * BLOCK + lax.broadcasted_iota(jnp.int32, (BLOCK, BLOCK), 0)
    for i in range(WINDOW):
        b = lax.rem(p.token_block + 16 - (WINDOW - 1) + i, 16)
        allowed = (b * BLOCK + lane <= query) & (seg_ref[pl.ds(b, 1), :] == seg_q)
        bias[:, i * BLOCK : (i + 1) * BLOCK] = jnp.where(allowed, F32(0), F32(NEGATIVE))
    core = [c1]
    a1.wait_recv()
    f1 = push(xrows(p.ya, p.zh, p.c), to_b)
    core.append(push(xrows(p.ya, p.zh, p.c), to_core))
    b1.wait_recv()
    core.append(push(xrows(p.yb, p.zh, p.c), to_core))
    swap.wait_recv()
    second = xrows(p.y, oz, p.c)
    a2, b2 = push(second, to_a), push(second, to_b)
    core.append(push(second, to_core))
    start_weights(1)
    b2.wait_recv()
    f2 = push(xrows(p.yb, oz, p.c), to_a)
    core.append(push(xrows(p.yb, oz, p.c), to_core))
    a2.wait_recv()
    core.append(push(xrows(p.ya, oz, p.c), to_core))
    forward_weights(0)
    f1.wait_recv()
    core.append(push(xrows(p.yab, p.zh, p.c), to_core))
    start_weights(2)
    f2.wait_recv()
    core.append(push(xrows(p.yab, oz, p.c), to_core))
    for cp in table_copies:
        cp.wait()
    for cp in core:
        cp.wait_recv()

    def streams(t):
        if t == 0:
            return [(16, order(0)), (17, order(2))]
        return [((t - 1) * 4 + s, order(s)) for s in range(4)]

    def place_in(o, nat):
        return 8 * nat[o[0]] + 4 * nat[o[1]] + 2 * nat[o[2]] + nat[o[3]]

    def product(t):
        def step(m, carry):
            x = xs[pl.ds(pl.multiple_of(m * 512, 512), 512), :]
            if t == 0:
                w = jnp.concatenate([wkv[0], wkv[1]], axis=1)
            else:
                w = wq[t - 1]
            y = jnp.dot(x, w, preferred_element_type=F32).astype(BF16)
            n0, n1 = lax.div(m, 2), lax.rem(m, 2)
            for i in range(4):
                nat = (n0, n1, i // 2, i % 2)
                for g, (slot, o) in enumerate(streams(t)):
                    part[slot, place_in(o, nat)] = y[
                        i * BLOCK : (i + 1) * BLOCK, g * HEAD : (g + 1) * HEAD
                    ]
            return carry

        lax.fori_loop(0, 4, step, 0)

    pending = {}

    def scatter(t, k):
        for slot, o in streams(t):
            n = 8 >> k
            at = prefix(p.bits, o, k) + (1 - p.bits[o[k]]) * n
            pending[slot, k] = net.remote(
                part.at[slot, pl.ds(at, n)], recvs[k].at[slot], p.partners[o[k]]
            )

    def rope(u):
        return u * cos[...] + pltpu.roll(u, 64, 1) * sin[...]

    def combine(t, k):
        done = []
        for slot, o in streams(t):
            pending[slot, k].wait_recv()
            n = 8 >> k
            at = prefix(p.bits, o, k + 1)
            for i in range(n):
                total = part[slot, at + i].astype(F32) + recvs[k][slot, i].astype(F32)
                if k < 3:
                    part[slot, at + i] = total.astype(BF16)
                else:
                    done.append((total if slot == 17 else rope(total)).astype(BF16))
        return done

    window = []

    def send_window(keys, values):
        kv[WINDOW - 1, 0] = keys
        kv[WINDOW - 1, 1] = values
        for d in range(1, WINDOW):
            window.append(
                net.remote(
                    kv.at[WINDOW - 1], kv.at[WINDOW - 1 - d], p.block_dev(p.token_block + d)
                )
            )

    gathers = {}

    def gather(u, i):
        for s in range(4):
            o, k = order(s), 3 - i
            blocks = att.at[4 * u + s, pl.ds(prefix(p.bits, o, k + 1), 1 << i)]
            gathers[u, i, s] = net.remote(blocks, blocks, p.partners[o[k]])

    def attention(u, heads):
        scale = 1.0 / math.sqrt(HEAD)
        keys = jnp.concatenate([kv[i, 0] for i in range(WINDOW)], axis=0)
        values = jnp.concatenate([kv[i, 1] for i in range(WINDOW)], axis=0)
        for s, q in enumerate(heads):
            scores = lax.dot_general(
                q, keys, (((1,), (1,)), ((), ())), preferred_element_type=F32
            )
            scores = scores * scale + bias[...]
            largest = jnp.max(scores, axis=-1, keepdims=True)
            exponent = jnp.exp(scores - largest)
            denominator = jnp.sum(exponent, axis=-1, keepdims=True)
            probabilities = (exponent * (1.0 / denominator)).astype(BF16)
            att[4 * u + s, prefix(p.bits, order(s), 4)] = jnp.dot(
                probabilities, values, preferred_element_type=F32
            ).astype(BF16)
        gather(u, 0)

    def attended_rows(u, m):
        n0, n1 = lax.div(m, 2), lax.rem(m, 2)
        blocks = []
        for i in range(4):
            nat = (n0, n1, i // 2, i % 2)
            blocks.append(
                jnp.concatenate(
                    [att[4 * u + s, place_in(order(s), nat)] for s in range(4)], axis=1
                )
            )
        return jnp.concatenate(blocks, axis=0)

    def out_product(u):
        def step(m, carry):
            y = lax.dot_general(
                attended_rows(u, m), wo[u], (((1,), (1,)), ((), ())),
                preferred_element_type=F32,
            )
            for n in range(4):
                at = (n, pl.ds(pl.multiple_of(m * 512, 512), 512))
                term = y[:, n * 256 : (n + 1) * 256]
                acc[at] = term if u == 0 else acc[at] + term
            return carry

        lax.fori_loop(0, 4, step, 0)

    def last_product(n):
        def step(m, carry):
            y = lax.dot_general(
                attended_rows(3, m), wo[3, n * 256 : (n + 1) * 256],
                (((1,), (1,)), ((), ())), preferred_element_type=F32,
            )
            total = (acc[n, pl.ds(pl.multiple_of(m * 512, 512), 512)] + y).astype(BF16)
            for i in range(4):
                po[n, i % 2, 2 * m + i // 2] = total[i * BLOCK : (i + 1) * BLOCK]
            return carry

        lax.fori_loop(0, 4, step, 0)

    for t in range(13):
        for u in range(4):
            i = t - (u + 5) - 1
            if 0 <= i < 4:
                for s in range(4):
                    gathers[u, i, s].wait_recv()
                if i < 3:
                    gather(u, i + 1)
        finished = []
        for u in range(5):
            k = t - u - 1
            if 0 <= k < 4:
                done = combine(u, k)
                if k < 3:
                    scatter(u, k + 1)
                elif u == 0:
                    send_window(*done)
                else:
                    finished.append((u - 1, done))
        if t + 1 < 9:
            forward_weights(t + 1)
        if t < 5:
            wait_weights(t)
            if t + 3 < 5:
                start_weights(t + 3)
            if 5 <= t + 2:
                start_weights(t + 2)
            product(t)
            scatter(t, 0)
        elif t + 2 < 9:
            start_weights(t + 2)
        if t == 5:
            for cp in window:
                cp.wait_recv()
        for u, heads in finished:
            attention(u, heads)
        u = t - 9
        if 0 <= u < 3:
            wait_weights(5 + u)
            out_product(u)
    wait_weights(8)

    y, ya, yb, yab = p.y, p.ya, p.yb, p.yab
    step1, step2, step3, step4 = {}, {}, {}, {}

    def add(n, at, other):
        po[n, p.c, at] = (po[n, p.c, at].astype(F32) + other.astype(F32)).astype(BF16)

    def sum_cores(n):
        step1[n].wait_recv()
        for i in range(8):
            add(n, i, rc[n, i])
        mine = po.at[n, p.c]
        step2[n] = [
            net.remote(mine.at[2 * yab], ry1.at[n, 0, 0], to_a),
            net.remote(mine.at[2 * yab + 1], ry1.at[n, 1, 0], to_b),
            net.remote(mine.at[2 * ya], ry1.at[n, 0, 1], to_a),
            net.remote(mine.at[2 * yb + 1], ry1.at[n, 1, 1], to_b),
        ]

    def sum_first(n):
        for cp in step2[n]:
            cp.wait_recv()
        add(n, 2 * yb, ry1[n, 0, 0])
        add(n, 2 * ya + 1, ry1[n, 1, 0])
        mine = po.at[n, p.c]
        step3[n] = [
            net.remote(mine.at[2 * yb], ry2.at[n, 0], to_b),
            net.remote(mine.at[2 * ya + 1], ry2.at[n, 1], to_a),
        ]
        add(n, 2 * y, ry1[n, 0, 1])
        add(n, 2 * y + 1, ry1[n, 1, 1])

    def sum_second(n):
        for cp in step3[n]:
            cp.wait_recv()
        add(n, 2 * y, ry2[n, 0])
        add(n, 2 * y + 1, ry2[n, 1])
        step4[n] = net.remote(
            po.at[n, p.c, 2 * y + oz], fin.at[n, p.zh], p.dev(zh=oz)
        )
        fin[n, p.zh] = po[n, p.c, 2 * y + p.zh]

    def finish(n):
        step4[n].wait_recv()
        for z in range(2):
            out_ref[:, n * 512 + z * 256 : n * 512 + z * 256 + 256] = fin[n, z]

    for n in range(8):
        if n < 4:
            last_product(n)
            step1[n] = net.remote(po.at[n, p.oc], rc.at[n], to_core)
        if 0 <= n - 3 < 4:
            sum_second(n - 3)
        if 0 <= n - 2 < 4:
            sum_first(n - 2)
        if 0 <= n - 1 < 4:
            sum_cores(n - 1)
        if 0 <= n - 4 < 4:
            finish(n - 4)
    net.finish()


def body(hidden_in, segment_ids, q_weight, k_weight, value_weight, out_weight):
    vmem = pl.BlockSpec(memory_space=pltpu.VMEM)
    hbm = pl.BlockSpec(memory_space=pl.ANY)
    cos, sin = tables()
    blocks = lambda *shape: pltpu.VMEM(shape, BF16)
    return pl.pallas_call(
        kernel,
        out_shape=jax.ShapeDtypeStruct((BLOCK, 2048), BF16),
        in_specs=[vmem, vmem, hbm, hbm, hbm, hbm, hbm, hbm],
        out_specs=vmem,
        scratch_shapes=[
            blocks(2, BLOCK, 1024),
            blocks(2048, 1024),
            blocks(2, 1024, HEAD),
            blocks(4, 1024, 512),
            blocks(2, 2, BLOCK, HEAD),
            blocks(4, 2, BLOCK, 512),
            blocks(18, 16, BLOCK, HEAD),
            blocks(18, 8, BLOCK, HEAD),
            blocks(18, 4, BLOCK, HEAD),
            blocks(18, 2, BLOCK, HEAD),
            blocks(18, 1, BLOCK, HEAD),
            pltpu.VMEM((BLOCK, HEAD), F32),
            pltpu.VMEM((BLOCK, HEAD), F32),
            blocks(WINDOW, 2, BLOCK, HEAD),
            pltpu.VMEM((BLOCK, WINDOW * BLOCK), F32),
            blocks(16, 16, BLOCK, HEAD),
            blocks(4, 1024, 512),
            blocks(4, 2, BLOCK, 512),
            pltpu.VMEM((4, 2048, 256), F32),
            blocks(4, 2, 8, BLOCK, 256),
            blocks(4, 8, BLOCK, 256),
            blocks(4, 2, 2, BLOCK, 256),
            blocks(4, 2, BLOCK, 256),
            blocks(4, 2, BLOCK, 256),
            pltpu.SemaphoreType.DMA((SEMAPHORES,)),
            pltpu.SemaphoreType.DMA((SEMAPHORES,)),
        ],
        compiler_params=pltpu.CompilerParams(
            collective_id=0, has_side_effects=True, vmem_limit_bytes=63 << 20
        ),
    )(hidden_in, segment_ids.reshape(16, BLOCK), cos, sin, q_weight, k_weight, value_weight,
      out_weight)


def solution(mesh):
    placed = (
        P("col", "row"),
        P(),
        P(("row", "col"), None),
        P(("row", "col"), None),
        P(("row", "col"), None),
        P(("row", "col"), None),
    )
    return jax.shard_map(
        body, mesh=mesh, in_specs=placed, out_specs=P("col", "row"), check_vma=False
    )
```

```python
import math

import jax
import jax.numpy as jnp
import numpy as np
from jax import lax
from jax.experimental import pallas as pl
from jax.experimental.pallas import tpu as pltpu
from jax.sharding import PartitionSpec as P

HEAD = 128
BLOCK = 128
HALF = 64
THETA = 500000.0
NEGATIVE = -1e30
SEMAPHORES = 400
WINDOW = 5
F32 = jnp.float32
BF16 = jnp.bfloat16
MESH = pl.DeviceIdType.MESH


class Place:
    def __init__(self):
        row, col = lax.axis_index("row"), lax.axis_index("col")
        self.x, self.zl = lax.div(row, 2), lax.rem(row, 2)
        self.y, self.zh, self.c = lax.div(col, 4), lax.rem(lax.div(col, 2), 2), lax.rem(col, 2)
        self.col = col
        self.oc = 1 - self.c
        x, y, zl, zh = self.x, self.y, self.zl, self.zh
        self.ya, self.yb = y + 1 - 2 * lax.rem(y, 2), 3 - y
        self.yab = 3 - self.ya
        self.xa, self.xb = x + 1 - 2 * lax.rem(x, 2), 3 - x
        self.bits = (lax.div(x, 2), lax.rem(x + lax.div(x, 2), 2), zh, lax.rem(zl + zh, 2))
        self.partners = (
            self.dev(x=self.xb),
            self.dev(x=self.xa),
            self.dev(zh=1 - zh, zl=1 - zl),
            self.dev(zl=1 - zl),
        )
        self.token_block = (
            8 * self.bits[0] + 4 * self.bits[1] + 2 * self.bits[2] + self.bits[3]
        )

    def dev(self, **k):
        g = lambda n: k.get(n, getattr(self, n))
        return (2 * g("x") + g("zl"), 4 * g("y") + 2 * g("zh") + g("c"))

    def ycore_partners(self):
        return [
            self.dev(c=self.oc),
            self.dev(y=self.ya),
            self.dev(y=self.ya, c=self.oc),
            self.dev(y=self.yb),
            self.dev(y=self.yb, c=self.oc),
        ]

    def block_dev(self, t):
        t = lax.rem(t + 16, 16)
        n0, n1 = lax.div(t, 8), lax.rem(lax.div(t, 4), 2)
        n2, n3 = lax.rem(lax.div(t, 2), 2), lax.rem(t, 2)
        return self.dev(x=2 * n0 + lax.rem(n0 + n1, 2), zh=n2, zl=lax.rem(n2 + n3, 2))

    def all_partners(self):
        window = [self.block_dev(self.token_block + d) for i in range(1, WINDOW) for d in (i, -i)]
        return (
            self.ycore_partners()
            + [self.dev(y=y, zh=1 - self.zh) for y in (self.y, self.ya, self.yb)]
            + list(self.partners)
            + window
        )


def order(s):
    return [(s + k) % 4 for k in range(4)]


def barrier(devices):
    sem = pltpu.get_barrier_semaphore()
    for d in devices:
        pl.semaphore_signal(sem, inc=1, device_id=d, device_id_type=MESH)
    pl.semaphore_wait(sem, len(devices))


class Net:
    def __init__(self, send, recv):
        self.send, self.recv, self.n, self.open = send, recv, 0, []

    def remote(self, src, dst, dev):
        i = self.n
        self.n += 1
        cp = pltpu.make_async_remote_copy(
            src, dst, self.send.at[i], self.recv.at[i], device_id=dev, device_id_type=MESH
        )
        cp.start()
        self.open.append(cp)
        return cp

    def local(self, src, dst):
        i = self.n
        self.n += 1
        cp = pltpu.make_async_copy(src, dst, self.recv.at[i])
        cp.start()
        return cp

    def finish(self):
        for cp in self.open:
            cp.wait_send()
        self.open = []


def rows(i, n=1):
    return pl.ds(pl.multiple_of(i * BLOCK, BLOCK), n * BLOCK)


class Relay:
    def __init__(self, net, p, src, dst, rel):
        self.net, self.p, self.dst, self.rel = net, p, dst, rel
        y, c, oc = p.y, p.c, p.oc
        mine = dst.at[rows(2 * y + c)]
        self.ra = net.remote(src(2 * p.yab + c), rel.at[0], p.dev(y=p.ya))
        self.rb = net.remote(src(2 * p.yab + oc), rel.at[1], p.dev(y=p.yb))
        self.waits = [
            net.remote(src(2 * p.ya + c), mine, p.dev(y=p.ya)),
            net.remote(src(2 * p.yb + c), mine, p.dev(y=p.yb)),
            net.remote(src(2 * p.ya + oc), mine, p.dev(y=p.ya, c=oc)),
            net.remote(src(2 * p.yb + oc), mine, p.dev(y=p.yb, c=oc)),
            net.remote(src(2 * y + oc), mine, p.dev(c=oc)),
        ]
        self.own = net.local(src(2 * y + c), mine)

    def forward(self, way):
        p = self.p
        (self.ra, self.rb)[way].wait_recv()
        origin = (p.ya, p.yb)[way]
        to = (p.dev(y=p.yb), p.dev(y=p.ya, c=p.oc))[way]
        self.waits.append(
            self.net.remote(self.rel.at[way], self.dst.at[rows(2 * origin + p.c)], to)
        )

    def wait(self):
        self.own.wait()
        for cp in self.waits:
            cp.wait_recv()


def prefix(bits, o, k):
    total = 0
    for i in range(k):
        total = total + bits[o[i]] * (8 >> i)
    return total


def tables():
    inverse = np.power(np.float32(THETA), -2.0 * np.arange(64, dtype=np.float32) / HEAD)
    angles = np.arange(2048, dtype=np.float32)[:, None] * inverse.astype(np.float32)[None, :]
    angles = angles.astype(np.float64)
    cos, sin = np.cos(angles), np.sin(angles)
    cos = np.concatenate([cos, cos], axis=1).astype(np.float32)
    sin = np.concatenate([-sin, sin], axis=1).astype(np.float32)
    return cos, sin


ORDER = (
    ("H","swap"), ("H","a1"), ("S",0), ("F",0,0), ("S",1), ("H","b2"), ("F",1,0),
    ("H","f1"), ("H","f2"), ("F",0,1), ("F",1,1), ("H","b1"), ("S",2), ("H","a2"), ("P",0),
    ("P",1), ("F",2,0), ("F",2,1), ("S",3), ("C",17,0), ("C",16,0), ("C",3,0), ("C",1,0),
    ("C",2,0), ("C",0,0), ("F",3,0), ("F",3,1), ("C",16,1), ("C",17,1), ("P",2), ("C",16,2),
    ("C",0,1), ("C",1,1), ("C",3,1), ("C",2,1), ("S",4), ("C",17,2), ("P",3), ("C",7,0),
    ("C",5,0), ("F",4,1), ("F",4,0), ("S",5), ("C",2,2), ("C",4,0), ("C",1,2), ("C",6,0),
    ("S",6), ("C",16,3), ("S",7), ("C",3,2), ("C",0,2), ("S",8), ("C",17,3), ("C",11,0),
    ("C",9,0), ("C",2,3), ("C",10,0), ("C",8,0), ("F",5,0), ("C",7,1), ("C",5,1), ("C",6,1),
    ("C",4,1), ("P",4), ("C",3,3), ("C",4,2), ("C",11,1), ("C",0,3), ("C",10,1), ("C",1,3),
    ("A",0), ("C",5,2), ("C",7,2), ("C",9,1), ("C",8,1), ("C",6,2), ("C",12,0), ("C",13,0),
    ("C",15,0), ("G",3,0,0), ("C",14,0), ("G",3,0,1), ("C",10,2), ("C",11,2), ("G",2,0,0),
    ("G",1,0,1), ("C",4,3), ("G",0,0,1), ("G",1,0,0), ("C",7,3), ("C",5,3), ("G",0,0,0),
    ("C",9,2), ("C",6,3), ("G",2,0,1), ("A",1), ("C",8,2), ("G",2,1,0), ("C",14,1),
    ("G",1,1,1), ("C",15,1), ("C",13,1), ("G",3,1,1), ("C",10,3), ("C",12,1), ("G",3,1,0),
    ("G",2,1,1), ("G",5,0,0), ("G",0,1,1), ("G",0,1,0), ("G",4,0,1), ("C",9,3), ("G",1,1,0),
    ("G",4,0,0), ("C",11,3), ("C",8,3), ("G",6,0,0), ("G",7,0,1), ("A",2), ("G",5,0,1),
    ("G",4,1,1), ("C",13,2), ("C",12,2), ("G",0,2,0), ("C",15,2), ("C",14,2), ("G",3,2,1),
    ("F",7,0), ("G",1,2,0), ("G",6,1,0), ("G",2,2,1), ("F",8,0), ("G",3,2,0), ("G",9,0,1),
    ("G",8,0,1), ("F",5,1), ("G",10,0,1), ("G",11,0,1), ("G",6,0,1), ("G",7,0,0),
    ("G",5,1,1), ("G",2,2,0), ("C",13,3), ("G",0,2,1), ("C",15,3), ("C",12,3), ("G",7,1,1),
    ("G",1,2,1), ("C",14,3), ("A",3), ("G",6,1,1), ("F",7,1), ("G",11,0,0), ("G",10,0,0),
    ("G",5,1,0), ("G",11,1,1), ("G",10,1,1), ("G",8,1,1), ("F",8,1), ("G",8,0,0),
    ("G",4,1,0), ("F",6,1), ("G",9,0,0), ("G",7,1,0), ("F",6,0), ("G",9,1,1), ("G",13,0,1),
    ("G",12,0,1), ("G",14,0,1), ("G",15,0,1), ("G",14,0,0), ("G",5,2,1), ("G",7,2,1),
    ("G",4,2,1), ("G",15,0,0), ("G",6,2,1), ("O",0,1), ("G",14,1,1), ("G",12,1,1),
    ("G",11,2,1), ("G",13,1,1), ("G",12,0,0), ("G",15,1,1), ("G",8,2,1), ("G",10,2,1),
    ("G",13,0,0), ("G",9,2,1), ("O",0,0), ("G",13,2,1), ("G",14,2,1), ("G",12,2,1),
    ("G",15,2,1), ("G",14,1,0), ("O",1,1), ("G",11,1,0), ("G",10,1,0), ("G",15,1,0),
    ("G",8,1,0), ("G",7,2,0), ("G",4,2,0), ("G",12,1,0), ("G",9,1,0), ("G",13,1,0),
    ("O",2,1), ("G",5,2,0), ("G",6,2,0), ("L",1,0), ("G",9,2,0), ("L",1,1), ("G",10,2,0),
    ("G",11,2,0), ("G",14,2,0), ("G",8,2,0), ("G",13,2,0), ("G",12,2,0), ("G",15,2,0),
    ("U",0,1,0), ("O",1,0), ("U",0,1,1), ("O",2,0), ("U",1,1,0), ("L",0,1), ("L",0,0),
    ("U",1,1,1), ("U",0,0,1), ("U",0,0,0), ("U",1,0,1), ("U",2,1,1), ("U",1,0,0),
    ("U",2,1,0), ("U",2,0,1), ("U",2,0,0),
)


def kernel(
    h_ref, seg_ref, cos_ref, sin_ref, q_ref, k_ref, v_ref, o_ref,
    out_ref,
    hx, xs, wkv, wq, relkv, relq, part, r0, r1, r2, r3, cos, sin, kv, bias,
    att, wo, relo, acc, po, rc, ry1, ry2, fin, send, recv,
):
    p = Place()
    net = Net(send, recv)
    recvs = (r0, r1, r2, r3)
    for z in range(2):
        for yy in range(4):
            hx[z, :, yy * 256 : (yy + 1) * 256] = h_ref[
                :, yy * 512 + z * 256 : yy * 512 + z * 256 + 256
            ]
    xs[rows(p.col)] = hx[p.zh]
    barrier(p.all_partners())

    flying = {}

    def arrive(*keys):
        for key in keys:
            flying.pop(key).wait_recv()

    def arrive_once(*keys):
        arrive(*[key for key in keys if key in flying])

    to_a, to_b, to_core = p.dev(y=p.ya), p.dev(y=p.yb), p.dev(c=p.oc)
    oz = 1 - p.zh

    def push(key, y, zh, dev):
        block = xs.at[rows(4 * y + 2 * zh + p.c)]
        flying[key] = net.remote(block, block, dev)

    def swap(key, y):
        flying[key] = net.remote(hx.at[oz], xs.at[rows(p.col)], p.dev(y=y, zh=oz))

    swap("swap", p.y)
    push("a1", p.y, p.zh, to_a)
    push("b1", p.y, p.zh, to_b)
    push("c1", p.y, p.zh, to_core)
    swap("a2", p.ya)
    swap("b2", p.yb)
    table_copies = [
        net.local(cos_ref.at[rows(p.token_block)], cos),
        net.local(sin_ref.at[rows(p.token_block)], sin),
    ]

    def act_h(name):
        arrive(name)
        if name == "a1":
            push("f1", p.ya, p.zh, to_b)
            push("h1", p.ya, p.zh, to_core)
        elif name == "b1":
            push("h2", p.yb, p.zh, to_core)
        elif name == "swap":
            push("c2", p.y, oz, to_core)
        elif name == "b2":
            push("f2", p.yb, oz, to_a)
            push("h3", p.yb, oz, to_core)
        elif name == "a2":
            push("h4", p.ya, oz, to_core)
        elif name == "f1":
            push("h5", p.yab, p.zh, to_core)
        elif name == "f2":
            push("h6", p.yab, oz, to_core)

    def columns(ref, width, j=0, chunk=None):
        chunk = chunk or width
        return lambda d: ref.at[:, pl.ds(pl.multiple_of(d * width + j * chunk, chunk), chunk)]

    weights = {}

    def act_s(t):
        if t == 0:
            weights[t] = [
                Relay(net, p, columns(k_ref, HEAD), wkv.at[0], relkv.at[0]),
                Relay(net, p, columns(v_ref, HEAD), wkv.at[1], relkv.at[1]),
            ]
        elif t < 5:
            j = t - 1
            weights[t] = [Relay(net, p, columns(q_ref, 2048, j, 512), wq.at[j], relq.at[j])]
        else:
            j = t - 5
            weights[t] = [Relay(net, p, columns(o_ref, 2048, j, 512), wo.at[j], relo.at[j])]

    def act_f(t, way):
        for w in weights[t]:
            w.forward(way)

    def wait_weights(t):
        for w in weights.pop(t, ()):
            w.wait()

    def slot_order(slot):
        return order((0, 2)[slot - 16] if slot >= 16 else slot % 4)

    def place_in(o, nat):
        return 8 * nat[o[0]] + 4 * nat[o[1]] + 2 * nat[o[2]] + nat[o[3]]

    def scatter(slot, k):
        o, n = slot_order(slot), 8 >> k
        at = prefix(p.bits, o, k) + (1 - p.bits[o[k]]) * n
        flying["r", slot, k] = net.remote(
            part.at[slot, pl.ds(at, n)], recvs[k].at[slot], p.partners[o[k]]
        )

    def act_p(t):
        arrive_once("c1", "c2", "h1", "h2", "h3", "h4", "h5", "h6")
        wait_weights(t)
        slots = (16, 17) if t == 0 else range(4 * t - 4, 4 * t)

        def step(m, carry):
            x = xs[pl.ds(pl.multiple_of(m * 512, 512), 512), :]
            if t == 0:
                w = jnp.concatenate([wkv[0], wkv[1]], axis=1)
            else:
                w = wq[t - 1]
            y = jnp.dot(x, w, preferred_element_type=F32).astype(BF16)
            n0, n1 = lax.div(m, 2), lax.rem(m, 2)
            for i in range(4):
                nat = (n0, n1, i // 2, i % 2)
                for g, slot in enumerate(slots):
                    part[slot, place_in(slot_order(slot), nat)] = y[
                        i * BLOCK : (i + 1) * BLOCK, g * HEAD : (g + 1) * HEAD
                    ]
            return carry

        lax.fori_loop(0, 4, step, 0)
        for slot in slots:
            scatter(slot, 0)

    def rope(u):
        while table_copies:
            table_copies.pop().wait()
        return u * cos[...] + pltpu.roll(u, 64, 1) * sin[...]

    queries = {}

    def act_c(slot, k):
        arrive(("r", slot, k))
        o, n = slot_order(slot), 8 >> k
        at = prefix(p.bits, o, k + 1)
        if k < 3:
            for i in range(n):
                part[slot, at + i] = part[slot, at + i] + recvs[k][slot, i]
            scatter(slot, k + 1)
            return
        total = part[slot, at].astype(F32) + recvs[k][slot, 0].astype(F32)
        if slot < 16:
            queries[slot] = (rope(total) * (math.log2(math.e) / math.sqrt(HEAD))).astype(BF16)
        else:
            which = slot - 16
            kv[which, WINDOW - 1] = (total if which else rope(total)).astype(BF16)
            for d in range(1, WINDOW):
                flying["window", which, d] = net.remote(
                    kv.at[which, WINDOW - 1],
                    kv.at[which, WINDOW - 1 - d],
                    p.block_dev(p.token_block + d),
                )

    def gather(slot, i, half):
        o, k = slot_order(slot), 3 - i
        blocks = att.at[half, slot, pl.ds(prefix(p.bits, o, k + 1), 1 << i)]
        flying["g", slot, i, half] = net.remote(blocks, blocks, p.partners[o[k]])

    def act_a(u):
        arrive_once(*[("window", which, d) for which in range(2) for d in range(1, WINDOW)])
        slots = range(4 * u, 4 * u + 4)
        scores = lax.dot_general(
            jnp.concatenate([queries.pop(slot) for slot in slots], axis=0),
            kv[0].reshape(WINDOW * BLOCK, HEAD),
            (((1,), (1,)), ((), ())),
            preferred_element_type=F32,
        )
        scores = scores.reshape(4, BLOCK, WINDOW * BLOCK) + bias[...][None]
        scores = scores.reshape(4 * BLOCK, WINDOW * BLOCK)
        exponent = jnp.exp2(scores - jnp.max(scores, axis=-1, keepdims=True))
        denominator = jnp.sum(exponent, axis=-1, keepdims=True)
        attended = jnp.dot(
            exponent.astype(BF16),
            kv[1].reshape(WINDOW * BLOCK, HEAD),
            preferred_element_type=F32,
        )
        attended = (attended * (1.0 / denominator)).astype(BF16)
        for s, slot in enumerate(slots):
            at = prefix(p.bits, order(s), 4)
            for half in range(2):
                low = s * BLOCK + half * HALF
                att[half, slot, at] = attended[low : low + HALF]
                gather(slot, 0, half)

    def act_g(slot, i, half):
        arrive(("g", slot, i, half))
        gather(slot, i + 1, half)

    def attended_rows(u, half, m):
        blocks = []
        for i in range(8):
            nat = (m, i // 4, i // 2 % 2, i % 2)
            blocks.append(
                jnp.concatenate(
                    [att[half, 4 * u + s, place_in(order(s), nat)] for s in range(4)], axis=1
                )
            )
        return jnp.concatenate(blocks, axis=0)

    def act_o(u, half):
        wait_weights(5 + u)
        arrive(*[("g", 4 * u + s, 3, half) for s in range(4)])

        def step(m, carry):
            y = lax.dot_general(
                attended_rows(u, half, m), wo[u], (((1,), (1,)), ((), ())),
                preferred_element_type=F32,
            )
            for f in range(2):
                at = (half, f, pl.ds(pl.multiple_of(m * 512, 512), 512))
                term = y[:, f * 512 : (f + 1) * 512]
                acc[at] = term if u == 0 else acc[at] + term
            return carry

        lax.fori_loop(0, 2, step, 0)

    y, ya, yb, yab = p.y, p.ya, p.yb, p.yab

    def act_l(half, f):
        wait_weights(8)
        arrive_once(*[("g", 12 + s, 3, half) for s in range(4)])

        def step(m, carry):
            term = lax.dot_general(
                attended_rows(3, half, m), wo[3, f * 512 : (f + 1) * 512],
                (((1,), (1,)), ((), ())), preferred_element_type=F32,
            )
            total = acc[half, f, pl.ds(pl.multiple_of(m * 512, 512), 512)] + term
            total = total.astype(BF16)
            for i in range(8):
                po[half, f, i % 2, 4 * m + i // 2] = total[i * HALF : (i + 1) * HALF]
            return carry

        lax.fori_loop(0, 2, step, 0)
        flying["c", half, f] = net.remote(po.at[half, f, p.oc], rc.at[half, f], to_core)

    def act_u(stage, half, f):
        mine, key = po.at[half, f, p.c], ("u", stage, half, f)
        one, two = ry1.at[half, f], ry2.at[half, f]

        def add(at, other):
            mine[at] = mine[at] + other

        def hand(block, dst, dev):
            flying["u", stage + 1, half, f, len(flying)] = net.remote(mine.at[block], dst, dev)

        if stage == 0:
            arrive(("c", half, f))
            for i in range(8):
                add(i, rc[half, f, i])
            hand(2 * yab + p.zh, one.at[0, 0], to_a)
            hand(2 * yab + oz, one.at[1, 0], to_b)
            hand(2 * ya + p.zh, one.at[0, 1], to_a)
            hand(2 * yb + oz, one.at[1, 1], to_b)
            return
        arrive(*[k for k in flying if k[:4] == key])
        if stage == 1:
            add(2 * yb + p.zh, one[0, 0])
            hand(2 * yb + p.zh, two.at[0], to_b)
            add(2 * ya + oz, one[1, 0])
            hand(2 * ya + oz, two.at[1], p.dev(y=ya, zh=oz))
            add(2 * y + oz, one[1, 1])
            hand(2 * y + oz, two.at[2], p.dev(zh=oz))
            add(2 * y + p.zh, one[0, 1])
            return
        fin[half, f, p.zh] = mine[2 * y + p.zh] + two[0]
        fin[half, f, oz] = two[1] + two[2]
        for z in range(2):
            for e in range(2):
                at = (2 * f + e) * 512 + z * 256
                out_ref[half * HALF : (half + 1) * HALF, at : at + 256] = fin[
                    half, f, z, :, e * 256 : (e + 1) * 256
                ]

    seg_q = jnp.transpose(
        jnp.broadcast_to(seg_ref[pl.ds(p.token_block, 1), :], (BLOCK, BLOCK))
    )
    lane = lax.broadcasted_iota(jnp.int32, (BLOCK, BLOCK), 1)
    query = p.token_block * BLOCK + lax.broadcasted_iota(jnp.int32, (BLOCK, BLOCK), 0)
    for i in range(WINDOW):
        b = lax.rem(p.token_block + 16 - (WINDOW - 1) + i, 16)
        allowed = (b * BLOCK + lane <= query) & (seg_ref[pl.ds(b, 1), :] == seg_q)
        bias[:, i * BLOCK : (i + 1) * BLOCK] = jnp.where(allowed, F32(0), F32(NEGATIVE))

    actions = dict(
        H=act_h, S=act_s, F=act_f, P=act_p, C=act_c, A=act_a, G=act_g, O=act_o, L=act_l, U=act_u
    )
    for name, *arguments in ORDER:
        actions[name](*arguments)
    net.finish()


def body(hidden_in, segment_ids, q_weight, k_weight, value_weight, out_weight):
    vmem = pl.BlockSpec(memory_space=pltpu.VMEM)
    hbm = pl.BlockSpec(memory_space=pl.ANY)
    cos, sin = tables()
    blocks = lambda *shape: pltpu.VMEM(shape, BF16)
    return pl.pallas_call(
        kernel,
        out_shape=jax.ShapeDtypeStruct((BLOCK, 2048), BF16),
        in_specs=[vmem, vmem, hbm, hbm, hbm, hbm, hbm, hbm],
        out_specs=vmem,
        scratch_shapes=[
            blocks(2, BLOCK, 1024),
            blocks(2048, 1024),
            blocks(2, 1024, HEAD),
            blocks(4, 1024, 512),
            blocks(2, 2, BLOCK, HEAD),
            blocks(4, 2, BLOCK, 512),
            blocks(18, 16, BLOCK, HEAD),
            blocks(18, 8, BLOCK, HEAD),
            blocks(18, 4, BLOCK, HEAD),
            blocks(18, 2, BLOCK, HEAD),
            blocks(18, 1, BLOCK, HEAD),
            pltpu.VMEM((BLOCK, HEAD), F32),
            pltpu.VMEM((BLOCK, HEAD), F32),
            blocks(2, WINDOW, BLOCK, HEAD),
            pltpu.VMEM((BLOCK, WINDOW * BLOCK), F32),
            blocks(2, 16, 16, HALF, HEAD),
            blocks(4, 1024, 512),
            blocks(4, 2, BLOCK, 512),
            pltpu.VMEM((2, 2, 1024, 512), F32),
            blocks(2, 2, 2, 8, HALF, 512),
            blocks(2, 2, 8, HALF, 512),
            blocks(2, 2, 2, 2, HALF, 512),
            blocks(2, 2, 3, HALF, 512),
            blocks(2, 2, 2, HALF, 512),
            pltpu.SemaphoreType.DMA((SEMAPHORES,)),
            pltpu.SemaphoreType.DMA((SEMAPHORES,)),
        ],
        compiler_params=pltpu.CompilerParams(
            collective_id=0, has_side_effects=True, vmem_limit_bytes=63 << 20
        ),
    )(hidden_in, segment_ids.reshape(16, BLOCK), cos, sin, q_weight, k_weight, value_weight,
      out_weight)


def solution(mesh):
    placed = (
        P("col", "row"),
        P(),
        P(("row", "col"), None),
        P(("row", "col"), None),
        P(("row", "col"), None),
        P(("row", "col"), None),
    )
    return jax.shard_map(
        body, mesh=mesh, in_specs=placed, out_specs=P("col", "row"), check_vma=False
    )
```

```python
import math

import jax
import jax.numpy as jnp
import numpy as np
from jax import lax
from jax.experimental import pallas as pl
from jax.experimental.pallas import tpu as pltpu
from jax.sharding import PartitionSpec as P

HEAD = 128
BLOCK = 128
HALF = 64
THETA = 500000.0
NEGATIVE = -1e30
SEMAPHORES = 400
WINDOW = 5
F32 = jnp.float32
BF16 = jnp.bfloat16
MESH = pl.DeviceIdType.MESH


class Place:
    def __init__(self):
        row, col = lax.axis_index("row"), lax.axis_index("col")
        self.x, self.zl = lax.div(row, 2), lax.rem(row, 2)
        self.y, self.zh, self.c = lax.div(col, 4), lax.rem(lax.div(col, 2), 2), lax.rem(col, 2)
        self.col = col
        self.oc = 1 - self.c
        x, y, zl, zh = self.x, self.y, self.zl, self.zh
        self.ya, self.yb = y + 1 - 2 * lax.rem(y, 2), 3 - y
        self.yab = 3 - self.ya
        self.xa, self.xb = x + 1 - 2 * lax.rem(x, 2), 3 - x
        self.bits = (lax.div(x, 2), lax.rem(x + lax.div(x, 2), 2), zh, lax.rem(zl + zh, 2))
        self.partners = (
            self.dev(x=self.xb),
            self.dev(x=self.xa),
            self.dev(zh=1 - zh, zl=1 - zl),
            self.dev(zl=1 - zl),
        )
        self.token_block = (
            8 * self.bits[0] + 4 * self.bits[1] + 2 * self.bits[2] + self.bits[3]
        )

    def dev(self, **k):
        g = lambda n: k.get(n, getattr(self, n))
        return (2 * g("x") + g("zl"), 4 * g("y") + 2 * g("zh") + g("c"))

    def ycore_partners(self):
        return [
            self.dev(c=self.oc),
            self.dev(y=self.ya),
            self.dev(y=self.ya, c=self.oc),
            self.dev(y=self.yb),
            self.dev(y=self.yb, c=self.oc),
        ]

    def block_dev(self, t):
        t = lax.rem(t + 16, 16)
        n0, n1 = lax.div(t, 8), lax.rem(lax.div(t, 4), 2)
        n2, n3 = lax.rem(lax.div(t, 2), 2), lax.rem(t, 2)
        return self.dev(x=2 * n0 + lax.rem(n0 + n1, 2), zh=n2, zl=lax.rem(n2 + n3, 2))

    def all_partners(self):
        window = [self.block_dev(self.token_block + d) for i in range(1, WINDOW) for d in (i, -i)]
        return (
            self.ycore_partners()
            + [self.dev(y=y, zh=1 - self.zh) for y in (self.y, self.ya, self.yb)]
            + list(self.partners)
            + window
        )


def order(s):
    return [(s + k) % 4 for k in range(4)]


def barrier(devices):
    sem = pltpu.get_barrier_semaphore()
    for d in devices:
        pl.semaphore_signal(sem, inc=1, device_id=d, device_id_type=MESH)
    pl.semaphore_wait(sem, len(devices))


class Net:
    def __init__(self, send, recv):
        self.send, self.recv, self.n, self.open = send, recv, 0, []

    def remote(self, src, dst, dev):
        i = self.n
        self.n += 1
        cp = pltpu.make_async_remote_copy(
            src, dst, self.send.at[i], self.recv.at[i], device_id=dev, device_id_type=MESH
        )
        cp.start()
        self.open.append(cp)
        return cp

    def local(self, src, dst):
        i = self.n
        self.n += 1
        cp = pltpu.make_async_copy(src, dst, self.recv.at[i])
        cp.start()
        return cp

    def finish(self):
        for cp in self.open:
            cp.wait_send()
        self.open = []


def rows(i, n=1):
    return pl.ds(pl.multiple_of(i * BLOCK, BLOCK), n * BLOCK)


class Relay:
    def __init__(self, net, p, src, dst, rel):
        self.net, self.p, self.dst, self.rel = net, p, dst, rel
        y, c, oc = p.y, p.c, p.oc
        mine = dst.at[rows(2 * y + c)]
        self.ra = net.remote(src(2 * p.yab + c), rel.at[0], p.dev(y=p.ya))
        self.rb = net.remote(src(2 * p.yab + oc), rel.at[1], p.dev(y=p.yb))
        self.waits = [
            net.remote(src(2 * p.ya + c), mine, p.dev(y=p.ya)),
            net.remote(src(2 * p.yb + c), mine, p.dev(y=p.yb)),
            net.remote(src(2 * p.ya + oc), mine, p.dev(y=p.ya, c=oc)),
            net.remote(src(2 * p.yb + oc), mine, p.dev(y=p.yb, c=oc)),
            net.remote(src(2 * y + oc), mine, p.dev(c=oc)),
        ]
        self.own = net.local(src(2 * y + c), mine)

    def forward(self, way):
        p = self.p
        (self.ra, self.rb)[way].wait_recv()
        origin = (p.ya, p.yb)[way]
        to = (p.dev(y=p.yb), p.dev(y=p.ya, c=p.oc))[way]
        self.waits.append(
            self.net.remote(self.rel.at[way], self.dst.at[rows(2 * origin + p.c)], to)
        )

    def wait(self):
        self.own.wait()
        for cp in self.waits:
            cp.wait_recv()


def prefix(bits, o, k):
    total = 0
    for i in range(k):
        total = total + bits[o[i]] * (8 >> i)
    return total


def tables():
    inverse = np.power(np.float32(THETA), -2.0 * np.arange(64, dtype=np.float32) / HEAD)
    angles = np.arange(2048, dtype=np.float32)[:, None] * inverse.astype(np.float32)[None, :]
    angles = angles.astype(np.float64)
    cos, sin = np.cos(angles), np.sin(angles)
    cos = np.concatenate([cos, cos], axis=1).astype(np.float32)
    sin = np.concatenate([-sin, sin], axis=1).astype(np.float32)
    return cos, sin


QUERIES = {1: (0, 2), 2: (2, 2), 3: (4, 4), 4: (8, 4), 5: (12, 4)}
ORDER = (
    ("S",1), ("H","b1"), ("H","swap"), ("H","a1"), ("F",1,0), ("S",0), ("H","b2"),
    ("F",1,1), ("S",2), ("H","a2"), ("F",0,0), ("H","f1"), ("F",0,1), ("H","f2"), ("F",2,1),
    ("F",2,0), ("P",1), ("S",3), ("P",0), ("P",2), ("F",3,0), ("F",3,1), ("C",0,0), ("S",4),
    ("C",17,0), ("C",16,0), ("C",1,0), ("C",3,0), ("P",3), ("C",16,1), ("C",2,0), ("C",3,1),
    ("C",17,1), ("F",4,1), ("C",1,1), ("F",4,0), ("S",5), ("C",4,0), ("C",0,1), ("C",7,0),
    ("C",3,2), ("C",6,0), ("C",17,2), ("C",5,0), ("C",16,2), ("F",5,0), ("F",5,1),
    ("C",2,1), ("P",4), ("C",0,2), ("C",1,2), ("C",6,1), ("C",2,2), ("C",7,1), ("C",4,1),
    ("C",3,3), ("C",17,3), ("S",6), ("C",16,3), ("C",5,1), ("S",7), ("P",5), ("S",8),
    ("C",0,3), ("C",6,2), ("F",6,1), ("C",9,0), ("C",8,0), ("C",4,2), ("C",7,2), ("C",11,0),
    ("C",1,3), ("F",6,0), ("C",5,2), ("C",2,3), ("A",0), ("C",10,0), ("C",14,0), ("F",7,0),
    ("F",7,1), ("C",13,0), ("C",12,0), ("C",6,3), ("C",15,0), ("S",9), ("G",0,0,1),
    ("C",4,3), ("C",9,1), ("C",11,1), ("C",7,3), ("G",0,0,0), ("G",3,0,0), ("C",5,3),
    ("C",8,1), ("G",2,0,0), ("G",3,0,1), ("G",1,0,1), ("G",2,0,1), ("C",10,1), ("A",1),
    ("C",13,1), ("C",15,1), ("C",14,1), ("C",12,1), ("C",9,2), ("G",1,0,0), ("C",8,2),
    ("C",11,2), ("C",10,2), ("F",8,0), ("G",4,0,1), ("G",6,0,0), ("G",7,0,0), ("G",5,0,0),
    ("G",7,0,1), ("G",5,0,1), ("G",2,1,1), ("G",0,1,1), ("G",6,0,1), ("G",4,0,0),
    ("G",3,1,0), ("G",1,1,1), ("G",0,1,0), ("G",2,1,0), ("C",13,2), ("C",14,2), ("C",15,2),
    ("G",1,1,0), ("C",12,2), ("G",3,1,1), ("C",10,3), ("C",11,3), ("C",9,3), ("G",6,1,0),
    ("C",8,3), ("G",4,1,1), ("G",7,1,0), ("G",6,1,1), ("G",7,1,1), ("G",5,1,1), ("G",4,1,0),
    ("G",5,1,0), ("A",2), ("G",1,2,1), ("C",12,3), ("G",3,2,1), ("C",13,3), ("G",2,2,1),
    ("C",15,3), ("G",0,2,1), ("C",14,3), ("A",3), ("G",11,0,1), ("G",10,0,1), ("G",9,0,1),
    ("G",8,0,1), ("G",11,0,0), ("G",5,2,1), ("G",4,2,1), ("G",6,2,1), ("G",7,2,1),
    ("F",9,0), ("G",12,0,1), ("G",14,0,1), ("G",15,0,1), ("F",9,1), ("G",12,0,0),
    ("G",13,0,1), ("G",11,1,1), ("G",14,0,0), ("G",10,0,0), ("G",8,1,1), ("G",13,0,0),
    ("G",8,0,0), ("G",11,1,0), ("G",9,1,1), ("G",15,0,0), ("G",9,0,0), ("G",10,1,1),
    ("O",0,1), ("G",14,1,1), ("G",13,1,1), ("F",8,1), ("G",12,1,1), ("G",15,1,1),
    ("G",11,2,1), ("G",13,1,0), ("G",12,1,0), ("G",8,2,1), ("G",10,2,1), ("G",14,1,0),
    ("G",9,2,1), ("G",13,2,1), ("G",12,2,1), ("G",8,1,0), ("G",15,1,0), ("G",15,2,1),
    ("G",10,1,0), ("G",0,2,0), ("G",14,2,1), ("G",3,2,0), ("G",4,2,0), ("G",9,1,0),
    ("G",1,2,0), ("G",5,2,0), ("G",7,2,0), ("G",2,2,0), ("G",6,2,0), ("O",1,1), ("O",2,1),
    ("L",1,1), ("L",1,0), ("G",11,2,0), ("G",10,2,0), ("G",8,2,0), ("G",15,2,0),
    ("G",14,2,0), ("G",9,2,0), ("G",13,2,0), ("G",12,2,0), ("O",0,0), ("U",0,1,1),
    ("U",0,1,0), ("O",1,0), ("O",2,0), ("L",0,1), ("U",1,1,1), ("L",0,0), ("U",1,1,0),
    ("U",0,0,1), ("U",0,0,0), ("U",1,0,1), ("U",2,1,0), ("U",1,0,0), ("U",2,1,1),
    ("U",2,0,1), ("U",2,0,0),
)


def kernel(
    h_ref, seg_ref, cos_ref, sin_ref, q_ref, k_ref, v_ref, o_ref,
    out_ref,
    hx, xs, wkv, wq, relkv, relq, part, r0, r1, r2, r3, cos, sin, kv, bias,
    att, wo, relo, acc, po, rc, ry1, ry2, fin, send, recv,
):
    p = Place()
    net = Net(send, recv)
    recvs = (r0, r1, r2, r3)
    for z in range(2):
        for yy in range(4):
            hx[z, :, yy * 256 : (yy + 1) * 256] = h_ref[
                :, yy * 512 + z * 256 : yy * 512 + z * 256 + 256
            ]
    xs[rows(p.col)] = hx[p.zh]
    barrier(p.all_partners())

    flying = {}

    def arrive(*keys):
        for key in keys:
            flying.pop(key).wait_recv()

    def arrive_once(*keys):
        arrive(*[key for key in keys if key in flying])

    to_a, to_b, to_core = p.dev(y=p.ya), p.dev(y=p.yb), p.dev(c=p.oc)
    oz = 1 - p.zh

    def push(key, y, zh, dev):
        block = xs.at[rows(4 * y + 2 * zh + p.c)]
        flying[key] = net.remote(block, block, dev)

    flying["swap"] = net.remote(hx.at[oz], xs.at[rows(p.col)], p.dev(zh=oz))
    push("a1", p.y, p.zh, to_a)
    push("b1", p.y, p.zh, to_b)
    push("c1", p.y, p.zh, to_core)
    table_copies = [
        net.local(cos_ref.at[rows(p.token_block)], cos),
        net.local(sin_ref.at[rows(p.token_block)], sin),
    ]

    def act_h(name):
        arrive(name)
        if name == "a1":
            push("f1", p.ya, p.zh, to_b)
            push("h1", p.ya, p.zh, to_core)
        elif name == "b1":
            push("h2", p.yb, p.zh, to_core)
        elif name == "swap":
            push("a2", p.y, oz, to_a)
            push("b2", p.y, oz, to_b)
            push("c2", p.y, oz, to_core)
        elif name == "b2":
            push("f2", p.yb, oz, to_a)
            push("h3", p.yb, oz, to_core)
        elif name == "a2":
            push("h4", p.ya, oz, to_core)
        elif name == "f1":
            push("h5", p.yab, p.zh, to_core)
        elif name == "f2":
            push("h6", p.yab, oz, to_core)

    def columns(ref, width, j=0, chunk=None):
        chunk = chunk or width
        return lambda d: ref.at[:, pl.ds(pl.multiple_of(d * width + j * chunk, chunk), chunk)]

    weights = {}

    def query_weights(t):
        first, count = QUERIES[t]
        return first // 4, first % 4 * HEAD, count * HEAD

    def act_s(t):
        if t == 0:
            weights[t] = [
                Relay(net, p, columns(k_ref, HEAD), wkv.at[0], relkv.at[0]),
                Relay(net, p, columns(v_ref, HEAD), wkv.at[1], relkv.at[1]),
            ]
        elif t < 6:
            j, at, width = query_weights(t)
            weights[t] = [
                Relay(
                    net, p,
                    columns(q_ref, 2048, QUERIES[t][0] * HEAD // width, width),
                    wq.at[j, :, pl.ds(at, width)],
                    relq.at[j, :, :, pl.ds(at, width)],
                )
            ]
        else:
            j = t - 6
            weights[t] = [Relay(net, p, columns(o_ref, 2048, j, 512), wo.at[j], relo.at[j])]

    def act_f(t, way):
        for w in weights[t]:
            w.forward(way)

    def wait_weights(t):
        for w in weights.pop(t, ()):
            w.wait()

    def slot_order(slot):
        return order((0, 2)[slot - 16] if slot >= 16 else slot % 4)

    def place_in(o, nat):
        return 8 * nat[o[0]] + 4 * nat[o[1]] + 2 * nat[o[2]] + nat[o[3]]

    def scatter(slot, k):
        o, n = slot_order(slot), 8 >> k
        at = prefix(p.bits, o, k) + (1 - p.bits[o[k]]) * n
        flying["r", slot, k] = net.remote(
            part.at[slot, pl.ds(at, n)], recvs[k].at[slot], p.partners[o[k]]
        )

    def act_p(t):
        arrive_once("c1", "c2", "h1", "h2", "h3", "h4", "h5", "h6")
        wait_weights(t)
        slots = (16, 17) if t == 0 else range(QUERIES[t][0], sum(QUERIES[t]))

        def step(m, carry):
            x = xs[pl.ds(pl.multiple_of(m * 512, 512), 512), :]
            if t == 0:
                w = jnp.concatenate([wkv[0], wkv[1]], axis=1)
            else:
                j, at, width = query_weights(t)
                w = wq[j, :, at : at + width]
            y = jnp.dot(x, w, preferred_element_type=F32).astype(BF16)
            n0, n1 = lax.div(m, 2), lax.rem(m, 2)
            for i in range(4):
                nat = (n0, n1, i // 2, i % 2)
                for g, slot in enumerate(slots):
                    part[slot, place_in(slot_order(slot), nat)] = y[
                        i * BLOCK : (i + 1) * BLOCK, g * HEAD : (g + 1) * HEAD
                    ]
            return carry

        lax.fori_loop(0, 4, step, 0)
        for slot in slots:
            scatter(slot, 0)

    def rope(u):
        while table_copies:
            table_copies.pop().wait()
        return u * cos[...] + pltpu.roll(u, 64, 1) * sin[...]

    queries = {}

    def act_c(slot, k):
        arrive(("r", slot, k))
        o, n = slot_order(slot), 8 >> k
        at = prefix(p.bits, o, k + 1)
        if k < 3:
            for i in range(n):
                part[slot, at + i] = part[slot, at + i] + recvs[k][slot, i]
            scatter(slot, k + 1)
            return
        total = part[slot, at].astype(F32) + recvs[k][slot, 0].astype(F32)
        if slot < 16:
            queries[slot] = (rope(total) * (math.log2(math.e) / math.sqrt(HEAD))).astype(BF16)
        else:
            which = slot - 16
            kv[which, WINDOW - 1] = (total if which else rope(total)).astype(BF16)
            for d in range(1, WINDOW):
                flying["window", which, d] = net.remote(
                    kv.at[which, WINDOW - 1],
                    kv.at[which, WINDOW - 1 - d],
                    p.block_dev(p.token_block + d),
                )

    def gather(slot, i, half):
        o, k = slot_order(slot), 3 - i
        blocks = att.at[half, slot, pl.ds(prefix(p.bits, o, k + 1), 1 << i)]
        flying["g", slot, i, half] = net.remote(blocks, blocks, p.partners[o[k]])

    def act_a(u):
        arrive_once(*[("window", which, d) for which in range(2) for d in range(1, WINDOW)])
        slots = range(4 * u, 4 * u + 4)
        scores = lax.dot_general(
            jnp.concatenate([queries.pop(slot) for slot in slots], axis=0),
            kv[0].reshape(WINDOW * BLOCK, HEAD),
            (((1,), (1,)), ((), ())),
            preferred_element_type=F32,
        )
        scores = scores.reshape(4, BLOCK, WINDOW * BLOCK) + bias[...][None]
        scores = scores.reshape(4 * BLOCK, WINDOW * BLOCK)
        exponent = jnp.exp2(scores - jnp.max(scores, axis=-1, keepdims=True))
        denominator = jnp.sum(exponent, axis=-1, keepdims=True)
        attended = jnp.dot(
            exponent.astype(BF16),
            kv[1].reshape(WINDOW * BLOCK, HEAD),
            preferred_element_type=F32,
        )
        attended = (attended * (1.0 / denominator)).astype(BF16)
        for s, slot in enumerate(slots):
            at = prefix(p.bits, order(s), 4)
            for half in range(2):
                low = s * BLOCK + half * HALF
                att[half, slot, at] = attended[low : low + HALF]
                gather(slot, 0, half)

    def act_g(slot, i, half):
        arrive(("g", slot, i, half))
        gather(slot, i + 1, half)

    def attended_rows(u, half, m):
        blocks = []
        for i in range(8):
            nat = (m, i // 4, i // 2 % 2, i % 2)
            blocks.append(
                jnp.concatenate(
                    [att[half, 4 * u + s, place_in(order(s), nat)] for s in range(4)], axis=1
                )
            )
        return jnp.concatenate(blocks, axis=0)

    def act_o(u, half):
        wait_weights(6 + u)
        arrive(*[("g", 4 * u + s, 3, half) for s in range(4)])

        def step(m, carry):
            y = lax.dot_general(
                attended_rows(u, half, m), wo[u], (((1,), (1,)), ((), ())),
                preferred_element_type=F32,
            )
            for f in range(2):
                at = (half, f, pl.ds(pl.multiple_of(m * 512, 512), 512))
                term = y[:, f * 512 : (f + 1) * 512]
                acc[at] = term if u == 0 else acc[at] + term
            return carry

        lax.fori_loop(0, 2, step, 0)

    y, ya, yb, yab = p.y, p.ya, p.yb, p.yab

    def act_l(half, f):
        wait_weights(9)
        arrive_once(*[("g", 12 + s, 3, half) for s in range(4)])

        def step(m, carry):
            term = lax.dot_general(
                attended_rows(3, half, m), wo[3, f * 512 : (f + 1) * 512],
                (((1,), (1,)), ((), ())), preferred_element_type=F32,
            )
            total = acc[half, f, pl.ds(pl.multiple_of(m * 512, 512), 512)] + term
            total = total.astype(BF16)
            for i in range(8):
                po[half, f, i % 2, 4 * m + i // 2] = total[i * HALF : (i + 1) * HALF]
            return carry

        lax.fori_loop(0, 2, step, 0)
        flying["c", half, f] = net.remote(po.at[half, f, p.oc], rc.at[half, f], to_core)

    def act_u(stage, half, f):
        mine, key = po.at[half, f, p.c], ("u", stage, half, f)
        one, two = ry1.at[half, f], ry2.at[half, f]

        def add(at, other):
            mine[at] = mine[at] + other

        def hand(block, dst, dev):
            flying["u", stage + 1, half, f, len(flying)] = net.remote(mine.at[block], dst, dev)

        if stage == 0:
            arrive(("c", half, f))
            for i in range(8):
                add(i, rc[half, f, i])
            hand(2 * yab + p.zh, one.at[0, 0], to_a)
            hand(2 * yab + oz, one.at[1, 0], to_b)
            hand(2 * ya + p.zh, one.at[0, 1], to_a)
            hand(2 * yb + oz, one.at[1, 1], to_b)
            return
        arrive(*[k for k in flying if k[:4] == key])
        if stage == 1:
            add(2 * yb + p.zh, one[0, 0])
            hand(2 * yb + p.zh, two.at[0], to_b)
            add(2 * ya + oz, one[1, 0])
            hand(2 * ya + oz, two.at[1], p.dev(y=ya, zh=oz))
            add(2 * y + oz, one[1, 1])
            hand(2 * y + oz, two.at[2], p.dev(zh=oz))
            add(2 * y + p.zh, one[0, 1])
            return
        fin[half, f, p.zh] = mine[2 * y + p.zh] + two[0]
        fin[half, f, oz] = two[1] + two[2]
        for z in range(2):
            for e in range(2):
                at = (2 * f + e) * 512 + z * 256
                out_ref[half * HALF : (half + 1) * HALF, at : at + 256] = fin[
                    half, f, z, :, e * 256 : (e + 1) * 256
                ]

    seg_q = jnp.transpose(
        jnp.broadcast_to(seg_ref[pl.ds(p.token_block, 1), :], (BLOCK, BLOCK))
    )
    lane = lax.broadcasted_iota(jnp.int32, (BLOCK, BLOCK), 1)
    query = p.token_block * BLOCK + lax.broadcasted_iota(jnp.int32, (BLOCK, BLOCK), 0)
    for i in range(WINDOW):
        b = lax.rem(p.token_block + 16 - (WINDOW - 1) + i, 16)
        allowed = (b * BLOCK + lane <= query) & (seg_ref[pl.ds(b, 1), :] == seg_q)
        bias[:, i * BLOCK : (i + 1) * BLOCK] = jnp.where(allowed, F32(0), F32(NEGATIVE))

    actions = dict(
        H=act_h, S=act_s, F=act_f, P=act_p, C=act_c, A=act_a, G=act_g, O=act_o, L=act_l, U=act_u
    )
    for name, *arguments in ORDER:
        actions[name](*arguments)
    net.finish()


def body(hidden_in, segment_ids, q_weight, k_weight, value_weight, out_weight):
    vmem = pl.BlockSpec(memory_space=pltpu.VMEM)
    hbm = pl.BlockSpec(memory_space=pl.ANY)
    cos, sin = tables()
    blocks = lambda *shape: pltpu.VMEM(shape, BF16)
    return pl.pallas_call(
        kernel,
        out_shape=jax.ShapeDtypeStruct((BLOCK, 2048), BF16),
        in_specs=[vmem, vmem, hbm, hbm, hbm, hbm, hbm, hbm],
        out_specs=vmem,
        scratch_shapes=[
            blocks(2, BLOCK, 1024),
            blocks(2048, 1024),
            blocks(2, 1024, HEAD),
            blocks(4, 1024, 512),
            blocks(2, 2, BLOCK, HEAD),
            blocks(4, 2, BLOCK, 512),
            blocks(18, 16, BLOCK, HEAD),
            blocks(18, 8, BLOCK, HEAD),
            blocks(18, 4, BLOCK, HEAD),
            blocks(18, 2, BLOCK, HEAD),
            blocks(18, 1, BLOCK, HEAD),
            pltpu.VMEM((BLOCK, HEAD), F32),
            pltpu.VMEM((BLOCK, HEAD), F32),
            blocks(2, WINDOW, BLOCK, HEAD),
            pltpu.VMEM((BLOCK, WINDOW * BLOCK), F32),
            blocks(2, 16, 16, HALF, HEAD),
            blocks(4, 1024, 512),
            blocks(4, 2, BLOCK, 512),
            pltpu.VMEM((2, 2, 1024, 512), F32),
            blocks(2, 2, 2, 8, HALF, 512),
            blocks(2, 2, 8, HALF, 512),
            blocks(2, 2, 2, 2, HALF, 512),
            blocks(2, 2, 3, HALF, 512),
            blocks(2, 2, 2, HALF, 512),
            pltpu.SemaphoreType.DMA((SEMAPHORES,)),
            pltpu.SemaphoreType.DMA((SEMAPHORES,)),
        ],
        compiler_params=pltpu.CompilerParams(
            collective_id=0, has_side_effects=True, vmem_limit_bytes=63 << 20
        ),
    )(hidden_in, segment_ids.reshape(16, BLOCK), cos, sin, q_weight, k_weight, value_weight,
      out_weight)


def solution(mesh):
    placed = (
        P("col", "row"),
        P(),
        P(("row", "col"), None),
        P(("row", "col"), None),
        P(("row", "col"), None),
        P(("row", "col"), None),
    )
    return jax.shard_map(
        body, mesh=mesh, in_specs=placed, out_specs=P("col", "row"), check_vma=False
    )
```

```python
import math

import jax
import jax.numpy as jnp
import numpy as np
from jax import lax
from jax.experimental import pallas as pl
from jax.experimental.pallas import tpu as pltpu
from jax.sharding import PartitionSpec as P

HEAD = 128
BLOCK = 128
THETA = 500000.0
NEGATIVE = -1e30
SEMAPHORES = 400
WINDOW = 5
F32 = jnp.float32
BF16 = jnp.bfloat16
MESH = pl.DeviceIdType.MESH


class Place:
    def __init__(self):
        row, col = lax.axis_index("row"), lax.axis_index("col")
        self.x, self.zl = lax.div(row, 2), lax.rem(row, 2)
        self.y, self.zh, self.c = lax.div(col, 4), lax.rem(lax.div(col, 2), 2), lax.rem(col, 2)
        self.col = col
        self.oc = 1 - self.c
        x, y, zl, zh = self.x, self.y, self.zl, self.zh
        self.ya, self.yb = y + 1 - 2 * lax.rem(y, 2), 3 - y
        self.yab = 3 - self.ya
        self.xa, self.xb = x + 1 - 2 * lax.rem(x, 2), 3 - x
        self.bits = (lax.div(x, 2), lax.rem(x + lax.div(x, 2), 2), zh, lax.rem(zl + zh, 2))
        self.partners = (
            self.dev(x=self.xb),
            self.dev(x=self.xa),
            self.dev(zh=1 - zh, zl=1 - zl),
            self.dev(zl=1 - zl),
        )
        self.token_block = (
            8 * self.bits[0] + 4 * self.bits[1] + 2 * self.bits[2] + self.bits[3]
        )

    def dev(self, **k):
        g = lambda n: k.get(n, getattr(self, n))
        return (2 * g("x") + g("zl"), 4 * g("y") + 2 * g("zh") + g("c"))

    def ycore_partners(self):
        return [
            self.dev(c=self.oc),
            self.dev(y=self.ya),
            self.dev(y=self.ya, c=self.oc),
            self.dev(y=self.yb),
            self.dev(y=self.yb, c=self.oc),
        ]

    def block_dev(self, t):
        t = lax.rem(t + 16, 16)
        n0, n1 = lax.div(t, 8), lax.rem(lax.div(t, 4), 2)
        n2, n3 = lax.rem(lax.div(t, 2), 2), lax.rem(t, 2)
        return self.dev(x=2 * n0 + lax.rem(n0 + n1, 2), zh=n2, zl=lax.rem(n2 + n3, 2))

    def all_partners(self):
        window = [self.block_dev(self.token_block + d) for i in range(1, WINDOW) for d in (i, -i)]
        return (
            self.ycore_partners()
            + [self.dev(y=y, zh=1 - self.zh) for y in (self.y, self.ya, self.yb)]
            + list(self.partners)
            + window
        )


def order(s):
    return [(s + k) % 4 for k in range(4)]


def barrier(devices):
    sem = pltpu.get_barrier_semaphore()
    for d in devices:
        pl.semaphore_signal(sem, inc=1, device_id=d, device_id_type=MESH)
    pl.semaphore_wait(sem, len(devices))


class Net:
    def __init__(self, send, recv):
        self.send, self.recv, self.n, self.open = send, recv, 0, []

    def remote(self, src, dst, dev):
        i = self.n
        self.n += 1
        cp = pltpu.make_async_remote_copy(
            src, dst, self.send.at[i], self.recv.at[i], device_id=dev, device_id_type=MESH
        )
        cp.start()
        self.open.append(cp)
        return cp

    def local(self, src, dst):
        i = self.n
        self.n += 1
        cp = pltpu.make_async_copy(src, dst, self.recv.at[i])
        cp.start()
        return cp

    def finish(self):
        for cp in self.open:
            cp.wait_send()
        self.open = []


def rows(i, n=1):
    return pl.ds(pl.multiple_of(i * BLOCK, BLOCK), n * BLOCK)


class Relay:
    def __init__(self, net, p, src, dst, rel):
        self.net, self.p, self.src, self.dst, self.rel = net, p, src, dst, rel
        self.waits = []
        self.ra = net.remote(src(2 * p.yab + p.c), rel.at[0], p.dev(y=p.ya))
        self.rb = net.remote(src(2 * p.yab + p.oc), rel.at[1], p.dev(y=p.yb))

    def start(self):
        net, p, src = self.net, self.p, self.src
        y, c, oc = p.y, p.c, p.oc
        mine = self.dst.at[rows(2 * y + c)]
        self.waits += [
            net.remote(src(2 * p.ya + c), mine, p.dev(y=p.ya)),
            net.remote(src(2 * p.yb + c), mine, p.dev(y=p.yb)),
            net.remote(src(2 * p.ya + oc), mine, p.dev(y=p.ya, c=oc)),
            net.remote(src(2 * p.yb + oc), mine, p.dev(y=p.yb, c=oc)),
            net.remote(src(2 * y + oc), mine, p.dev(c=oc)),
        ]
        self.own = net.local(src(2 * y + c), mine)

    def forward(self, way):
        p = self.p
        (self.ra, self.rb)[way].wait_recv()
        origin = (p.ya, p.yb)[way]
        to = (p.dev(y=p.yb), p.dev(y=p.ya, c=p.oc))[way]
        self.waits.append(
            self.net.remote(self.rel.at[way], self.dst.at[rows(2 * origin + p.c)], to)
        )

    def wait(self):
        self.own.wait()
        for cp in self.waits:
            cp.wait_recv()


def prefix(bits, o, k):
    total = 0
    for i in range(k):
        total = total + bits[o[i]] * (8 >> i)
    return total


def tables():
    inverse = np.power(np.float32(THETA), -2.0 * np.arange(64, dtype=np.float32) / HEAD)
    angles = np.arange(2048, dtype=np.float32)[:, None] * inverse.astype(np.float32)[None, :]
    angles = angles.astype(np.float64)
    cos, sin = np.cos(angles), np.sin(angles)
    cos = np.concatenate([cos, cos], axis=1).astype(np.float32)
    sin = np.concatenate([-sin, sin], axis=1).astype(np.float32)
    return cos, sin


QUERIES = {1: (0, 2), 2: (2, 2), 3: (4, 4), 4: (8, 4), 5: (12, 4)}
HALVES = ((0, 48), (48, 80))
GATHER_HALVES = (0, 1)
WHOLE_STAGES = 0
ORDER = (
    ("S",1,0), ("S",0,0), ("S",2,0), ("H","b1"), ("H","swap"), ("F",0,0), ("F",0,1),
    ("F",1,1), ("H","a1"), ("F",1,0), ("H","a2"), ("H","b2"), ("S",1,1), ("S",0,1),
    ("H","f1"), ("F",2,1), ("H","f2"), ("S",2,1), ("F",2,0), ("S",3,0), ("P",1), ("S",3,1),
    ("P",0), ("P",2), ("F",3,0), ("C",0,0), ("C",1,0), ("F",3,1), ("C",17,0), ("S",4,0),
    ("C",16,0), ("S",4,1), ("C",3,0), ("P",3,0), ("C",2,0), ("C",0,1), ("F",4,1),
    ("C",16,1), ("C",1,1), ("P",3,1), ("F",4,0), ("C",17,1), ("S",5,0), ("C",3,1),
    ("C",1,2), ("S",5,1), ("C",4,0), ("C",0,2), ("C",16,2), ("C",5,0), ("C",2,1),
    ("C",17,2), ("P",4,0), ("C",6,0), ("C",3,2), ("P",4,1), ("F",5,0), ("F",5,1), ("C",4,1),
    ("S",6,0), ("S",7,0), ("C",1,3), ("S",8,0), ("S",7,1), ("C",2,2), ("C",16,3), ("C",0,3),
    ("S",6,1), ("C",3,3), ("C",7,0), ("C",17,3), ("S",8,1), ("C",8,0), ("C",5,1), ("C",9,0),
    ("C",6,1), ("P",5,0), ("C",10,0), ("C",7,1), ("P",5,1), ("C",2,3), ("C",4,2), ("C",6,2),
    ("C",5,2), ("S",9,0), ("A",0), ("C",9,1), ("F",6,1), ("C",11,0), ("C",10,1), ("C",12,0),
    ("F",7,0), ("C",7,2), ("C",13,0), ("C",5,3), ("C",6,3), ("C",14,0), ("C",8,1),
    ("G",3,0,0), ("G",3,0,1), ("G",2,0,0), ("C",15,0), ("F",6,0), ("G",1,0,1), ("G",2,0,1),
    ("C",4,3), ("C",11,1), ("C",7,3), ("G",0,0,1), ("A",1), ("C",13,1), ("C",10,2),
    ("G",0,0,0), ("C",9,2), ("C",12,1), ("C",15,1), ("C",14,1), ("C",8,2), ("C",11,2),
    ("G",4,0,0), ("G",5,0,0), ("G",0,1,1), ("F",7,1), ("G",6,0,1), ("G",5,0,1), ("G",1,0,0),
    ("G",7,0,0), ("G",3,1,0), ("F",8,1), ("G",7,0,1), ("G",4,0,1), ("G",3,1,1), ("G",2,1,0),
    ("G",1,1,1), ("G",0,1,0), ("C",13,2), ("C",10,3), ("C",12,2), ("G",6,0,0), ("C",9,3),
    ("G",5,1,0), ("C",11,3), ("G",2,1,1), ("C",15,2), ("C",8,3), ("C",14,2), ("G",5,1,1),
    ("G",6,1,1), ("G",1,1,0), ("G",4,1,1), ("G",0,2,1), ("G",4,1,0), ("A",2), ("G",3,2,1),
    ("G",7,1,1), ("C",13,3), ("G",2,2,1), ("C",15,3), ("C",12,3), ("G",1,2,1), ("C",14,3),
    ("A",3), ("G",10,0,1), ("G",9,0,1), ("G",4,2,1), ("G",8,0,1), ("G",9,0,0), ("G",10,0,0),
    ("G",11,0,1), ("G",5,2,1), ("G",7,2,1), ("F",8,0), ("G",12,0,0), ("F",9,1),
    ("G",12,0,1), ("G",13,0,1), ("S",9,1), ("G",10,1,1), ("G",6,1,0), ("G",9,1,1),
    ("G",14,0,1), ("G",6,2,1), ("G",14,0,0), ("G",11,1,1), ("G",13,0,0), ("G",7,1,0),
    ("G",8,0,0), ("G",15,0,1), ("G",8,1,1), ("O",0,1), ("G",12,1,1), ("G",14,1,1),
    ("G",11,0,0), ("G",15,0,0), ("G",15,1,1), ("G",13,1,1), ("G",11,2,1), ("F",9,0),
    ("G",8,2,1), ("G",9,2,1), ("G",10,2,1), ("O",1,1), ("G",12,2,1), ("G",13,2,1),
    ("G",14,2,1), ("G",15,2,1), ("G",10,1,0), ("G",9,1,0), ("G",3,2,0), ("G",15,1,0),
    ("G",8,1,0), ("G",11,1,0), ("G",13,1,0), ("G",0,2,0), ("G",12,1,0), ("G",2,2,0),
    ("G",1,2,0), ("G",14,1,0), ("G",7,2,0), ("O",2,1), ("G",6,2,0), ("G",4,2,0),
    ("G",5,2,0), ("L",1,0), ("G",8,2,0), ("G",12,2,0), ("L",1,1), ("G",9,2,0), ("G",13,2,0),
    ("G",11,2,0), ("G",15,2,0), ("G",10,2,0), ("O",0,0), ("G",14,2,0), ("U",0,1,0),
    ("O",1,0), ("U",0,1,1), ("O",2,0), ("L",0,0), ("U",1,1,0), ("L",0,1), ("U",0,0,0),
    ("U",1,1,1), ("U",0,0,1), ("U",1,0,0), ("U",1,0,1), ("U",2,1,1), ("U",2,0,0),
    ("U",2,1,0), ("U",2,0,1),
)


def kernel(
    h_ref, seg_ref, cos_ref, sin_ref, q_ref, k_ref, v_ref, o_ref,
    out_ref, more_ref,
    hx, xs, wkv, wq, relkv, relq, part, r0, r1, r2, r3, cos, sin, kv, bias,
    att, wo, relo, acc0, acc1, po0, po1, rc0, rc1, ones0, ones1, twos0, twos1, send, recv,
):
    p = Place()
    net = Net(send, recv)
    recvs = (r0, r1, r2, r3)
    acc, po, rc = (acc0, acc1), (po0, po1), (rc0, rc1)
    ones, twos = (ones0, ones1), (twos0, twos1)
    for z in range(2):
        for yy in range(4):
            hx[z, :, yy * 256 : (yy + 1) * 256] = h_ref[
                :, yy * 512 + z * 256 : yy * 512 + z * 256 + 256
            ]
    xs[rows(p.col)] = hx[p.zh]
    barrier(p.all_partners())

    flying = {}

    def arrive(*keys):
        for key in keys:
            flying.pop(key).wait_recv()

    def arrive_once(*keys):
        arrive(*[key for key in keys if key in flying])

    to_a, to_b, to_core = p.dev(y=p.ya), p.dev(y=p.yb), p.dev(c=p.oc)
    oz = 1 - p.zh

    def push(key, y, zh, dev):
        block = xs.at[rows(4 * y + 2 * zh + p.c)]
        flying[key] = net.remote(block, block, dev)

    flying["swap"] = net.remote(hx.at[oz], xs.at[rows(p.col)], p.dev(zh=oz))
    push("a1", p.y, p.zh, to_a)
    push("b1", p.y, p.zh, to_b)
    push("c1", p.y, p.zh, to_core)
    table_copies = [
        net.local(cos_ref.at[rows(p.token_block)], cos),
        net.local(sin_ref.at[rows(p.token_block)], sin),
    ]

    def act_h(name):
        arrive(name)
        if name == "a1":
            push("f1", p.ya, p.zh, to_b)
            push("h1", p.ya, p.zh, to_core)
        elif name == "b1":
            push("h2", p.yb, p.zh, to_core)
        elif name == "swap":
            push("a2", p.y, oz, to_a)
            push("b2", p.y, oz, to_b)
            push("c2", p.y, oz, to_core)
        elif name == "b2":
            push("f2", p.yb, oz, to_a)
            push("h3", p.yb, oz, to_core)
        elif name == "a2":
            push("h4", p.ya, oz, to_core)
        elif name == "f1":
            push("h5", p.yab, p.zh, to_core)
        elif name == "f2":
            push("h6", p.yab, oz, to_core)

    def columns(ref, width, j=0, chunk=None):
        chunk = chunk or width
        return lambda d: ref.at[:, pl.ds(pl.multiple_of(d * width + j * chunk, chunk), chunk)]

    weights = {}

    def query_weights(t):
        first, count = QUERIES[t]
        return first // 4, first % 4 * HEAD, count * HEAD

    def act_s(t, part):
        if part:
            for relay in weights[t]:
                relay.start()
        elif t == 0:
            weights[t] = [
                Relay(net, p, columns(k_ref, HEAD), wkv.at[0], relkv.at[0]),
                Relay(net, p, columns(v_ref, HEAD), wkv.at[1], relkv.at[1]),
            ]
        elif t < 6:
            j, at, width = query_weights(t)
            weights[t] = [
                Relay(
                    net, p,
                    columns(q_ref, 2048, QUERIES[t][0] * HEAD // width, width),
                    wq.at[j, :, pl.ds(at, width)],
                    relq.at[j, :, :, pl.ds(at, width)],
                )
            ]
        else:
            j = t - 6
            weights[t] = [Relay(net, p, columns(o_ref, 2048, j, 512), wo.at[j], relo.at[j])]

    def act_f(t, way):
        for w in weights[t]:
            w.forward(way)

    def wait_weights(t):
        for w in weights.pop(t, ()):
            w.wait()

    def slot_order(slot):
        return order((0, 2)[slot - 16] if slot >= 16 else slot % 4)

    def place_in(o, nat):
        return 8 * nat[o[0]] + 4 * nat[o[1]] + 2 * nat[o[2]] + nat[o[3]]

    def scatter(slot, k):
        o, n = slot_order(slot), 8 >> k
        at = prefix(p.bits, o, k) + (1 - p.bits[o[k]]) * n
        flying["r", slot, k] = net.remote(
            part.at[slot, pl.ds(at, n)], recvs[k].at[slot], p.partners[o[k]]
        )

    def act_p(t, pair=0):
        arrive_once("c1", "c2", "h1", "h2", "h3", "h4", "h5", "h6")
        wait_weights(t)
        if t == 0:
            slots = (16, 17)
        else:
            slots = range(QUERIES[t][0] + 2 * pair, QUERIES[t][0] + 2 * pair + 2)
            j, at, _ = query_weights(t)
            at = at + 256 * pair

        def step(m, carry):
            x = xs[pl.ds(pl.multiple_of(m * 512, 512), 512), :]
            if t == 0:
                w = jnp.concatenate([wkv[0], wkv[1]], axis=1)
            else:
                w = wq[j, :, at : at + 256]
            y = jnp.dot(x, w, preferred_element_type=F32).astype(BF16)
            n0, n1 = lax.div(m, 2), lax.rem(m, 2)
            for i in range(4):
                nat = (n0, n1, i // 2, i % 2)
                for g, slot in enumerate(slots):
                    part[slot, place_in(slot_order(slot), nat)] = y[
                        i * BLOCK : (i + 1) * BLOCK, g * HEAD : (g + 1) * HEAD
                    ]
            return carry

        lax.fori_loop(0, 4, step, 0)
        for slot in slots:
            scatter(slot, 0)

    def rope(u):
        while table_copies:
            table_copies.pop().wait()
        return u * cos[...] + pltpu.roll(u, 64, 1) * sin[...]

    queries = {}

    def act_c(slot, k):
        arrive(("r", slot, k))
        o, n = slot_order(slot), 8 >> k
        at = prefix(p.bits, o, k + 1)
        if k < 3:
            for i in range(n):
                part[slot, at + i] = part[slot, at + i] + recvs[k][slot, i]
            scatter(slot, k + 1)
            return
        total = part[slot, at].astype(F32) + recvs[k][slot, 0].astype(F32)
        if slot < 16:
            queries[slot] = (rope(total) * (math.log2(math.e) / math.sqrt(HEAD))).astype(BF16)
        else:
            which = slot - 16
            kv[which, WINDOW - 1] = (total if which else rope(total)).astype(BF16)
            for d in range(1, WINDOW):
                flying["window", which, d] = net.remote(
                    kv.at[which, WINDOW - 1],
                    kv.at[which, WINDOW - 1 - d],
                    p.block_dev(p.token_block + d),
                )

    def gather(slot, i):
        o, k = slot_order(slot), 3 - i
        at = pl.ds(prefix(p.bits, o, k + 1), 1 << i)
        if i < WHOLE_STAGES:
            blocks = att.at[slot, at]
            flying["g", slot, i] = net.remote(blocks, blocks, p.partners[o[k]])

    def gather_half(slot, i, half):
        o, k = slot_order(slot), 3 - i
        at = pl.ds(prefix(p.bits, o, k + 1), 1 << i)
        blocks = att.at[slot, at, pl.ds(*HALVES[half])]
        flying["g", slot, i, half] = net.remote(blocks, blocks, p.partners[o[k]])

    def gather_on(slot, i):
        if i < WHOLE_STAGES:
            gather(slot, i)
        else:
            for half in GATHER_HALVES:
                gather_half(slot, i, half)

    def act_a(u):
        arrive_once(*[("window", which, d) for which in range(2) for d in range(1, WINDOW)])
        slots = range(4 * u, 4 * u + 4)
        scores = lax.dot_general(
            jnp.concatenate([queries.pop(slot) for slot in slots], axis=0),
            kv[0].reshape(WINDOW * BLOCK, HEAD),
            (((1,), (1,)), ((), ())),
            preferred_element_type=F32,
        )
        scores = scores.reshape(4, BLOCK, WINDOW * BLOCK) + bias[...][None]
        scores = scores.reshape(4 * BLOCK, WINDOW * BLOCK)
        exponent = jnp.exp2(scores - jnp.max(scores, axis=-1, keepdims=True))
        denominator = jnp.sum(exponent, axis=-1, keepdims=True)
        attended = jnp.dot(
            exponent.astype(BF16),
            kv[1].reshape(WINDOW * BLOCK, HEAD),
            preferred_element_type=F32,
        )
        attended = (attended * (1.0 / denominator)).astype(BF16)
        for s, slot in enumerate(slots):
            att[slot, prefix(p.bits, order(s), 4)] = attended[s * BLOCK : (s + 1) * BLOCK]
            gather_on(slot, 0)

    def act_g(slot, i, *half):
        arrive(("g", slot, i, *half))
        if half:
            gather_half(slot, i + 1, *half)
        else:
            gather_on(slot, i + 1)

    def attended_rows(u, half, m):
        low, size = HALVES[half]
        blocks = []
        for i in range(8):
            nat = (m, i // 4, i // 2 % 2, i % 2)
            blocks.append(
                jnp.concatenate(
                    [att[4 * u + s, place_in(order(s), nat), low : low + size] for s in range(4)],
                    axis=1,
                )
            )
        return jnp.concatenate(blocks, axis=0)

    def act_o(u, half):
        wait_weights(6 + u)
        arrive(*[("g", 4 * u + s, 3, half) for s in range(4)])
        total, size = acc[half], HALVES[half][1]

        def step(m, carry):
            y = lax.dot_general(
                attended_rows(u, half, m), wo[u], (((1,), (1,)), ((), ())),
                preferred_element_type=F32,
            )
            for f in range(2):
                at = (f, pl.ds(pl.multiple_of(m * 8 * size, 8 * size), 8 * size))
                term = y[:, f * 512 : (f + 1) * 512]
                total[at] = term if u == 0 else total[at] + term
            return carry

        lax.fori_loop(0, 2, step, 0)

    y, ya, yb, yab = p.y, p.ya, p.yb, p.yab

    def act_l(half, f):
        wait_weights(9)
        arrive_once(*[("g", 12 + s, 3, half) for s in range(4)])
        size = HALVES[half][1]

        def step(m, carry):
            term = lax.dot_general(
                attended_rows(3, half, m), wo[3, f * 512 : (f + 1) * 512],
                (((1,), (1,)), ((), ())), preferred_element_type=F32,
            )
            at = pl.ds(pl.multiple_of(m * 8 * size, 8 * size), 8 * size)
            total = (acc[half][f, at] + term).astype(BF16)
            for i in range(8):
                po[half][f, i % 2, 4 * m + i // 2] = total[i * size : (i + 1) * size]
            return carry

        lax.fori_loop(0, 2, step, 0)
        flying["c", half, f] = net.remote(po[half].at[f, p.oc], rc[half].at[f], to_core)

    def act_u(stage, half, f):
        mine, key = po[half].at[f, p.c], ("u", stage, half, f)
        one, two = ones[half].at[f], twos[half].at[f]

        def add(at, other):
            mine[at] = mine[at] + other

        def hand(block, dst, dev):
            flying["u", stage + 1, half, f, len(flying)] = net.remote(mine.at[block], dst, dev)

        if stage == 0:
            arrive(("c", half, f))
            for i in range(8):
                add(i, rc[half][f, i])
            hand(2 * yab + p.zh, one.at[0, 0], to_a)
            hand(2 * yab + oz, one.at[1, 0], to_b)
            hand(2 * ya + p.zh, one.at[0, 1], to_a)
            hand(2 * yb + oz, one.at[1, 1], to_b)
            return
        arrive(*[k for k in flying if k[:4] == key])
        if stage == 1:
            add(2 * yb + p.zh, one[0, 0])
            hand(2 * yb + p.zh, two.at[0], to_b)
            add(2 * ya + oz, one[1, 0])
            hand(2 * ya + oz, two.at[1], p.dev(y=ya, zh=oz))
            add(2 * y + oz, one[1, 1])
            hand(2 * y + oz, two.at[2], p.dev(zh=oz))
            add(2 * y + p.zh, one[0, 1])
            return
        low, size = HALVES[half]
        here, there = (mine[2 * y + p.zh], two[0]), (two[1], two[2])
        for ref, mine_part, other_part in zip((out_ref, more_ref), here, there):
            for z in range(2):
                part_z = jnp.where(p.zh == z, mine_part, other_part)
                for e in range(2):
                    at = (2 * f + e) * 512 + z * 256
                    ref[low : low + size, at : at + 256] = part_z[:, e * 256 : (e + 1) * 256]

    seg_q = jnp.transpose(
        jnp.broadcast_to(seg_ref[pl.ds(p.token_block, 1), :], (BLOCK, BLOCK))
    )
    lane = lax.broadcasted_iota(jnp.int32, (BLOCK, BLOCK), 1)
    query = p.token_block * BLOCK + lax.broadcasted_iota(jnp.int32, (BLOCK, BLOCK), 0)
    for i in range(WINDOW):
        b = lax.rem(p.token_block + 16 - (WINDOW - 1) + i, 16)
        allowed = (b * BLOCK + lane <= query) & (seg_ref[pl.ds(b, 1), :] == seg_q)
        bias[:, i * BLOCK : (i + 1) * BLOCK] = jnp.where(allowed, F32(0), F32(NEGATIVE))

    actions = dict(
        H=act_h, S=act_s, F=act_f, P=act_p, C=act_c, A=act_a, G=act_g, O=act_o, L=act_l, U=act_u
    )
    for name, *arguments in ORDER:
        actions[name](*arguments)
    net.finish()


def body(hidden_in, segment_ids, q_weight, k_weight, value_weight, out_weight):
    vmem = pl.BlockSpec(memory_space=pltpu.VMEM)
    hbm = pl.BlockSpec(memory_space=pl.ANY)
    cos, sin = tables()
    blocks = lambda *shape: pltpu.VMEM(shape, BF16)
    sizes = [size for _, size in HALVES]
    one, two = pl.pallas_call(
        kernel,
        out_shape=(jax.ShapeDtypeStruct((BLOCK, 2048), BF16),) * 2,
        in_specs=[vmem, vmem, hbm, hbm, hbm, hbm, hbm, hbm],
        out_specs=(vmem, vmem),
        scratch_shapes=[
            blocks(2, BLOCK, 1024),
            blocks(2048, 1024),
            blocks(2, 1024, HEAD),
            blocks(4, 1024, 512),
            blocks(2, 2, BLOCK, HEAD),
            blocks(4, 2, BLOCK, 512),
            blocks(18, 16, BLOCK, HEAD),
            blocks(18, 8, BLOCK, HEAD),
            blocks(18, 4, BLOCK, HEAD),
            blocks(18, 2, BLOCK, HEAD),
            blocks(18, 1, BLOCK, HEAD),
            pltpu.VMEM((BLOCK, HEAD), F32),
            pltpu.VMEM((BLOCK, HEAD), F32),
            blocks(2, WINDOW, BLOCK, HEAD),
            pltpu.VMEM((BLOCK, WINDOW * BLOCK), F32),
            blocks(16, 16, BLOCK, HEAD),
            blocks(4, 1024, 512),
            blocks(4, 2, BLOCK, 512),
            *[pltpu.VMEM((2, 16 * size, 512), F32) for size in sizes],
            *[blocks(2, 2, 8, size, 512) for size in sizes],
            *[blocks(2, 8, size, 512) for size in sizes],
            *[blocks(2, 2, 2, size, 512) for size in sizes],
            *[blocks(2, 3, size, 512) for size in sizes],
            pltpu.SemaphoreType.DMA((SEMAPHORES,)),
            pltpu.SemaphoreType.DMA((SEMAPHORES,)),
        ],
        compiler_params=pltpu.CompilerParams(
            collective_id=0, has_side_effects=True, vmem_limit_bytes=63 << 20
        ),
    )(hidden_in, segment_ids.reshape(16, BLOCK), cos, sin, q_weight, k_weight, value_weight,
      out_weight)
    return (one.astype(F32) + two.astype(F32)).astype(BF16)


def solution(mesh):
    placed = (
        P("col", "row"),
        P(),
        P(("row", "col"), None),
        P(("row", "col"), None),
        P(("row", "col"), None),
        P(("row", "col"), None),
    )
    return jax.shard_map(
        body, mesh=mesh, in_specs=placed, out_specs=P("col", "row"), check_vma=False
    )
```

```python
import math

import jax
import jax.numpy as jnp
import numpy as np
from jax import lax
from jax.experimental import pallas as pl
from jax.experimental.pallas import tpu as pltpu
from jax.sharding import PartitionSpec as P

HEAD = 128
BLOCK = 128
THETA = 500000.0
NEGATIVE = -1e30
SEMAPHORES = 400
WINDOW = 5
F32 = jnp.float32
BF16 = jnp.bfloat16
MESH = pl.DeviceIdType.MESH


class Place:
    def __init__(self):
        row, col = lax.axis_index("row"), lax.axis_index("col")
        self.x, self.zl = lax.div(row, 2), lax.rem(row, 2)
        self.y, self.zh, self.c = lax.div(col, 4), lax.rem(lax.div(col, 2), 2), lax.rem(col, 2)
        self.col = col
        self.oc = 1 - self.c
        x, y, zl, zh = self.x, self.y, self.zl, self.zh
        self.ya, self.yb = y + 1 - 2 * lax.rem(y, 2), 3 - y
        self.yab = 3 - self.ya
        self.xa, self.xb = x + 1 - 2 * lax.rem(x, 2), 3 - x
        self.bits = (lax.div(x, 2), lax.rem(x + lax.div(x, 2), 2), zh, lax.rem(zl + zh, 2))
        self.partners = (
            self.dev(x=self.xb),
            self.dev(x=self.xa),
            self.dev(zh=1 - zh, zl=1 - zl),
            self.dev(zl=1 - zl),
        )
        self.token_block = (
            8 * self.bits[0] + 4 * self.bits[1] + 2 * self.bits[2] + self.bits[3]
        )

    def dev(self, **k):
        g = lambda n: k.get(n, getattr(self, n))
        return (2 * g("x") + g("zl"), 4 * g("y") + 2 * g("zh") + g("c"))

    def ycore_partners(self):
        return [
            self.dev(c=self.oc),
            self.dev(y=self.ya),
            self.dev(y=self.ya, c=self.oc),
            self.dev(y=self.yb),
            self.dev(y=self.yb, c=self.oc),
        ]

    def block_dev(self, t):
        t = lax.rem(t + 16, 16)
        n0, n1 = lax.div(t, 8), lax.rem(lax.div(t, 4), 2)
        n2, n3 = lax.rem(lax.div(t, 2), 2), lax.rem(t, 2)
        return self.dev(x=2 * n0 + lax.rem(n0 + n1, 2), zh=n2, zl=lax.rem(n2 + n3, 2))

    def all_partners(self):
        window = [self.block_dev(self.token_block + d) for i in range(1, WINDOW) for d in (i, -i)]
        return (
            self.ycore_partners()
            + [self.dev(y=y, zh=1 - self.zh) for y in (self.y, self.ya, self.yb)]
            + list(self.partners)
            + window
        )


def order(s):
    return [(s + k) % 4 for k in range(4)]


def barrier(devices):
    sem = pltpu.get_barrier_semaphore()
    for d in devices:
        pl.semaphore_signal(sem, inc=1, device_id=d, device_id_type=MESH)
    pl.semaphore_wait(sem, len(devices))


class Net:
    def __init__(self, send, recv):
        self.send, self.recv, self.n, self.open = send, recv, 0, []

    def remote(self, src, dst, dev, into=None):
        i = self.n
        self.n += 1
        cp = pltpu.make_async_remote_copy(
            src, dst, self.send.at[i], self.recv.at[i], device_id=dev, device_id_type=MESH
        )
        cp.start()
        (self.open if into is None else into).append(cp)
        return cp

    def local(self, src, dst):
        i = self.n
        self.n += 1
        cp = pltpu.make_async_copy(src, dst, self.recv.at[i])
        cp.start()
        return cp

    def finish(self):
        for cp in self.open:
            cp.wait_send()
        self.open = []


def rows(i, n=1):
    return pl.ds(pl.multiple_of(i * BLOCK, BLOCK), n * BLOCK)


class Relay:
    def __init__(self, net, p, src, dst, rel):
        self.net, self.p, self.src, self.dst, self.rel = net, p, src, dst, rel
        self.waits = []
        self.ra = net.remote(src(2 * p.yab + p.c), rel.at[0], p.dev(y=p.ya))
        self.rb = net.remote(src(2 * p.yab + p.oc), rel.at[1], p.dev(y=p.yb))

    def start(self):
        net, p, src = self.net, self.p, self.src
        y, c, oc = p.y, p.c, p.oc
        mine = self.dst.at[rows(2 * y + c)]
        self.waits += [
            net.remote(src(2 * p.ya + c), mine, p.dev(y=p.ya)),
            net.remote(src(2 * p.yb + c), mine, p.dev(y=p.yb)),
            net.remote(src(2 * p.ya + oc), mine, p.dev(y=p.ya, c=oc)),
            net.remote(src(2 * p.yb + oc), mine, p.dev(y=p.yb, c=oc)),
            net.remote(src(2 * y + oc), mine, p.dev(c=oc)),
        ]
        self.own = net.local(src(2 * y + c), mine)

    def forward(self, way):
        p = self.p
        (self.ra, self.rb)[way].wait_recv()
        origin = (p.ya, p.yb)[way]
        to = (p.dev(y=p.yb), p.dev(y=p.ya, c=p.oc))[way]
        self.waits.append(
            self.net.remote(self.rel.at[way], self.dst.at[rows(2 * origin + p.c)], to)
        )

    def wait(self):
        self.own.wait()
        for cp in self.waits:
            cp.wait_recv()


def prefix(bits, o, k):
    total = 0
    for i in range(k):
        total = total + bits[o[i]] * (8 >> i)
    return total


def tables():
    inverse = np.power(np.float32(THETA), -2.0 * np.arange(64, dtype=np.float32) / HEAD)
    angles = np.arange(2048, dtype=np.float32)[:, None] * inverse.astype(np.float32)[None, :]
    angles = angles.astype(np.float64)
    cos, sin = np.cos(angles), np.sin(angles)
    cos = np.concatenate([cos, cos], axis=1).astype(np.float32)
    sin = np.concatenate([-sin, sin], axis=1).astype(np.float32)
    return cos, sin


QUERIES = {1: (0, 2), 2: (2, 2), 3: (4, 4), 4: (8, 4), 5: (12, 4)}
HALVES = ((0, 48), (48, 80))
GATHER_HALVES = (0, 1)
WHOLE_STAGES = 0
ORDER = (
    ("S",1,0), ("S",0,0), ("S",2,0), ("H","b1"), ("H","swap"), ("F",0,0), ("F",0,1),
    ("F",1,1), ("H","a1"), ("F",1,0), ("H","a2"), ("H","b2"), ("S",1,1), ("S",0,1),
    ("H","f1"), ("F",2,1), ("H","f2"), ("S",2,1), ("F",2,0), ("S",3,0), ("P",1), ("S",3,1),
    ("P",0), ("P",2), ("F",3,0), ("C",0,0), ("C",1,0), ("F",3,1), ("C",17,0), ("S",4,0),
    ("C",16,0), ("S",4,1), ("C",3,0), ("P",3,0), ("C",2,0), ("C",0,1), ("F",4,1),
    ("C",16,1), ("C",1,1), ("P",3,1), ("F",4,0), ("C",17,1), ("S",5,0), ("C",3,1),
    ("C",1,2), ("S",5,1), ("C",4,0), ("C",0,2), ("C",16,2), ("C",5,0), ("C",2,1),
    ("C",17,2), ("P",4,0), ("C",6,0), ("C",3,2), ("P",4,1), ("F",5,0), ("F",5,1), ("C",4,1),
    ("S",6,0), ("S",7,0), ("C",1,3), ("S",8,0), ("S",7,1), ("C",2,2), ("C",16,3), ("C",0,3),
    ("S",6,1), ("C",3,3), ("C",7,0), ("C",17,3), ("S",8,1), ("C",8,0), ("C",5,1), ("C",9,0),
    ("C",6,1), ("P",5,0), ("C",10,0), ("C",7,1), ("P",5,1), ("C",2,3), ("C",4,2), ("C",6,2),
    ("C",5,2), ("S",9,0), ("A",0), ("C",9,1), ("F",6,1), ("C",11,0), ("C",10,1), ("C",12,0),
    ("F",7,0), ("C",7,2), ("C",13,0), ("C",5,3), ("C",6,3), ("C",14,0), ("C",8,1),
    ("G",3,0,0), ("G",3,0,1), ("G",2,0,0), ("C",15,0), ("F",6,0), ("G",1,0,1), ("G",2,0,1),
    ("C",4,3), ("C",11,1), ("C",7,3), ("G",0,0,1), ("A",1), ("C",13,1), ("C",10,2),
    ("G",0,0,0), ("C",9,2), ("C",12,1), ("C",15,1), ("C",14,1), ("C",8,2), ("C",11,2),
    ("G",4,0,0), ("G",5,0,0), ("G",0,1,1), ("F",7,1), ("G",6,0,1), ("G",5,0,1), ("G",1,0,0),
    ("G",7,0,0), ("G",3,1,0), ("F",8,1), ("G",7,0,1), ("G",4,0,1), ("G",3,1,1), ("G",2,1,0),
    ("G",1,1,1), ("G",0,1,0), ("C",13,2), ("C",10,3), ("C",12,2), ("G",6,0,0), ("C",9,3),
    ("G",5,1,0), ("C",11,3), ("G",2,1,1), ("C",15,2), ("C",8,3), ("C",14,2), ("G",5,1,1),
    ("G",6,1,1), ("G",1,1,0), ("G",4,1,1), ("G",0,2,1), ("G",4,1,0), ("A",2), ("G",3,2,1),
    ("G",7,1,1), ("C",13,3), ("G",2,2,1), ("C",15,3), ("C",12,3), ("G",1,2,1), ("C",14,3),
    ("A",3), ("G",10,0,1), ("G",9,0,1), ("G",4,2,1), ("G",8,0,1), ("G",9,0,0), ("G",10,0,0),
    ("G",11,0,1), ("G",5,2,1), ("G",7,2,1), ("F",8,0), ("G",12,0,0), ("F",9,1),
    ("G",12,0,1), ("G",13,0,1), ("S",9,1), ("G",10,1,1), ("G",6,1,0), ("G",9,1,1),
    ("G",14,0,1), ("G",6,2,1), ("G",14,0,0), ("G",11,1,1), ("G",13,0,0), ("G",7,1,0),
    ("G",8,0,0), ("G",15,0,1), ("G",8,1,1), ("O",0,1), ("G",12,1,1), ("G",14,1,1),
    ("G",11,0,0), ("G",15,0,0), ("G",15,1,1), ("G",13,1,1), ("G",11,2,1), ("F",9,0),
    ("G",8,2,1), ("G",9,2,1), ("G",10,2,1), ("O",1,1), ("G",12,2,1), ("G",13,2,1),
    ("G",14,2,1), ("G",15,2,1), ("G",10,1,0), ("G",9,1,0), ("G",3,2,0), ("G",15,1,0),
    ("G",8,1,0), ("G",11,1,0), ("G",13,1,0), ("G",0,2,0), ("G",12,1,0), ("G",2,2,0),
    ("G",1,2,0), ("G",14,1,0), ("G",7,2,0), ("O",2,1), ("G",6,2,0), ("G",4,2,0),
    ("G",5,2,0), ("L",1,0), ("G",8,2,0), ("G",12,2,0), ("L",1,1), ("G",9,2,0), ("G",13,2,0),
    ("G",11,2,0), ("G",15,2,0), ("G",10,2,0), ("O",0,0), ("G",14,2,0), ("U",0,1,0),
    ("O",1,0), ("U",0,1,1), ("O",2,0), ("L",0,0), ("U",1,1,0), ("L",0,1), ("U",0,0,0),
    ("U",1,1,1), ("U",0,0,1), ("U",1,0,0), ("U",1,0,1), ("U",2,1,1), ("U",2,0,0),
    ("U",2,1,0), ("U",2,0,1),
)


def kernel(
    h_ref, seg_ref, cos_ref, sin_ref, q_ref, k_ref, v_ref, o_ref,
    out_ref,
    hx, xs, wkv, wq, relkv, relq, part, r0, r1, r2, r3, cos, sin, kv, bias,
    att, wo, relo, acc0, acc1, po0, po1, rc0, rc1, ones0, ones1, twos0, twos1, fin, send, recv,
):
    p = Place()
    net = Net(send, recv)
    recvs = (r0, r1, r2, r3)
    acc, po, rc = (acc0, acc1), (po0, po1), (rc0, rc1)
    ones, twos = (ones0, ones1), (twos0, twos1)
    for z in range(2):
        for yy in range(4):
            hx[z, :, yy * 256 : (yy + 1) * 256] = h_ref[
                :, yy * 512 + z * 256 : yy * 512 + z * 256 + 256
            ]
    xs[rows(p.col)] = hx[p.zh]
    barrier(p.all_partners())

    flying = {}

    def arrive(*keys):
        for key in keys:
            flying.pop(key).wait_recv()

    def arrive_once(*keys):
        arrive(*[key for key in keys if key in flying])

    to_a, to_b, to_core = p.dev(y=p.ya), p.dev(y=p.yb), p.dev(c=p.oc)
    oz = 1 - p.zh

    def push(key, y, zh, dev):
        block = xs.at[rows(4 * y + 2 * zh + p.c)]
        flying[key] = net.remote(block, block, dev)

    flying["swap"] = net.remote(hx.at[oz], xs.at[rows(p.col)], p.dev(zh=oz))
    push("a1", p.y, p.zh, to_a)
    push("b1", p.y, p.zh, to_b)
    push("c1", p.y, p.zh, to_core)
    table_copies = [
        net.local(cos_ref.at[rows(p.token_block)], cos),
        net.local(sin_ref.at[rows(p.token_block)], sin),
    ]

    def act_h(name):
        arrive(name)
        if name == "a1":
            push("f1", p.ya, p.zh, to_b)
            push("h1", p.ya, p.zh, to_core)
        elif name == "b1":
            push("h2", p.yb, p.zh, to_core)
        elif name == "swap":
            push("a2", p.y, oz, to_a)
            push("b2", p.y, oz, to_b)
            push("c2", p.y, oz, to_core)
        elif name == "b2":
            push("f2", p.yb, oz, to_a)
            push("h3", p.yb, oz, to_core)
        elif name == "a2":
            push("h4", p.ya, oz, to_core)
        elif name == "f1":
            push("h5", p.yab, p.zh, to_core)
        elif name == "f2":
            push("h6", p.yab, oz, to_core)

    def columns(ref, width, j=0, chunk=None):
        chunk = chunk or width
        return lambda d: ref.at[:, pl.ds(pl.multiple_of(d * width + j * chunk, chunk), chunk)]

    weights = {}

    def query_weights(t):
        first, count = QUERIES[t]
        return first // 4, first % 4 * HEAD, count * HEAD

    def act_s(t, part):
        if part:
            for relay in weights[t]:
                relay.start()
        elif t == 0:
            weights[t] = [
                Relay(net, p, columns(k_ref, HEAD), wkv.at[0], relkv.at[0]),
                Relay(net, p, columns(v_ref, HEAD), wkv.at[1], relkv.at[1]),
            ]
        elif t < 6:
            j, at, width = query_weights(t)
            weights[t] = [
                Relay(
                    net, p,
                    columns(q_ref, 2048, QUERIES[t][0] * HEAD // width, width),
                    wq.at[j, :, pl.ds(at, width)],
                    relq.at[j, :, :, pl.ds(at, width)],
                )
            ]
        else:
            j = t - 6
            weights[t] = [Relay(net, p, columns(o_ref, 2048, j, 512), wo.at[j], relo.at[j])]

    def act_f(t, way):
        for w in weights[t]:
            w.forward(way)

    def wait_weights(t):
        for w in weights.pop(t, ()):
            w.wait()

    def slot_order(slot):
        return order((0, 2)[slot - 16] if slot >= 16 else slot % 4)

    def place_in(o, nat):
        return 8 * nat[o[0]] + 4 * nat[o[1]] + 2 * nat[o[2]] + nat[o[3]]

    def scatter(slot, k):
        o, n = slot_order(slot), 8 >> k
        at = prefix(p.bits, o, k) + (1 - p.bits[o[k]]) * n
        flying["r", slot, k] = net.remote(
            part.at[slot, pl.ds(at, n)], recvs[k].at[slot], p.partners[o[k]]
        )

    def act_p(t, pair=0):
        arrive_once("c1", "c2", "h1", "h2", "h3", "h4", "h5", "h6")
        wait_weights(t)
        if t == 0:
            slots = (16, 17)
        else:
            slots = range(QUERIES[t][0] + 2 * pair, QUERIES[t][0] + 2 * pair + 2)
            j, at, _ = query_weights(t)
            at = at + 256 * pair

        def step(m, carry):
            x = xs[pl.ds(pl.multiple_of(m * 512, 512), 512), :]
            if t == 0:
                w = jnp.concatenate([wkv[0], wkv[1]], axis=1)
            else:
                w = wq[j, :, at : at + 256]
            y = jnp.dot(x, w, preferred_element_type=F32).astype(BF16)
            n0, n1 = lax.div(m, 2), lax.rem(m, 2)
            for i in range(4):
                nat = (n0, n1, i // 2, i % 2)
                for g, slot in enumerate(slots):
                    part[slot, place_in(slot_order(slot), nat)] = y[
                        i * BLOCK : (i + 1) * BLOCK, g * HEAD : (g + 1) * HEAD
                    ]
            return carry

        lax.fori_loop(0, 4, step, 0)
        for slot in slots:
            scatter(slot, 0)

    def rope(u):
        while table_copies:
            table_copies.pop().wait()
        return u * cos[...] + pltpu.roll(u, 64, 1) * sin[...]

    queries = {}

    def act_c(slot, k):
        arrive(("r", slot, k))
        o, n = slot_order(slot), 8 >> k
        at = prefix(p.bits, o, k + 1)
        if k < 3:
            for i in range(n):
                part[slot, at + i] = part[slot, at + i] + recvs[k][slot, i]
            scatter(slot, k + 1)
            return
        total = part[slot, at].astype(F32) + recvs[k][slot, 0].astype(F32)
        if slot < 16:
            queries[slot] = (rope(total) * (math.log2(math.e) / math.sqrt(HEAD))).astype(BF16)
        else:
            which = slot - 16
            kv[which, WINDOW - 1] = (total if which else rope(total)).astype(BF16)
            for d in range(1, WINDOW):
                flying["window", which, d] = net.remote(
                    kv.at[which, WINDOW - 1],
                    kv.at[which, WINDOW - 1 - d],
                    p.block_dev(p.token_block + d),
                )

    def gather(slot, i):
        o, k = slot_order(slot), 3 - i
        at = pl.ds(prefix(p.bits, o, k + 1), 1 << i)
        if i < WHOLE_STAGES:
            blocks = att.at[slot, at]
            flying["g", slot, i] = net.remote(blocks, blocks, p.partners[o[k]])

    def gather_half(slot, i, half):
        o, k = slot_order(slot), 3 - i
        at = pl.ds(prefix(p.bits, o, k + 1), 1 << i)
        blocks = att.at[slot, at, pl.ds(*HALVES[half])]
        flying["g", slot, i, half] = net.remote(blocks, blocks, p.partners[o[k]])

    def gather_on(slot, i):
        if i < WHOLE_STAGES:
            gather(slot, i)
        else:
            for half in GATHER_HALVES:
                gather_half(slot, i, half)

    def act_a(u):
        arrive_once(*[("window", which, d) for which in range(2) for d in range(1, WINDOW)])
        slots = range(4 * u, 4 * u + 4)
        scores = lax.dot_general(
            jnp.concatenate([queries.pop(slot) for slot in slots], axis=0),
            kv[0].reshape(WINDOW * BLOCK, HEAD),
            (((1,), (1,)), ((), ())),
            preferred_element_type=F32,
        )
        scores = scores.reshape(4, BLOCK, WINDOW * BLOCK) + bias[...][None]
        scores = scores.reshape(4 * BLOCK, WINDOW * BLOCK)
        exponent = jnp.exp2(scores - jnp.max(scores, axis=-1, keepdims=True))
        denominator = jnp.sum(exponent, axis=-1, keepdims=True)
        attended = jnp.dot(
            exponent.astype(BF16),
            kv[1].reshape(WINDOW * BLOCK, HEAD),
            preferred_element_type=F32,
        )
        attended = (attended * (1.0 / denominator)).astype(BF16)
        for s, slot in enumerate(slots):
            att[slot, prefix(p.bits, order(s), 4)] = attended[s * BLOCK : (s + 1) * BLOCK]
            gather_on(slot, 0)

    def act_g(slot, i, *half):
        arrive(("g", slot, i, *half))
        if half:
            gather_half(slot, i + 1, *half)
        else:
            gather_on(slot, i + 1)

    def attended_rows(u, half, m):
        low, size = HALVES[half]
        blocks = []
        for i in range(8):
            nat = (m, i // 4, i // 2 % 2, i % 2)
            blocks.append(
                jnp.concatenate(
                    [att[4 * u + s, place_in(order(s), nat), low : low + size] for s in range(4)],
                    axis=1,
                )
            )
        return jnp.concatenate(blocks, axis=0)

    def act_o(u, half):
        wait_weights(6 + u)
        arrive(*[("g", 4 * u + s, 3, half) for s in range(4)])
        total, size = acc[half], HALVES[half][1]

        def step(m, carry):
            y = lax.dot_general(
                attended_rows(u, half, m), wo[u], (((1,), (1,)), ((), ())),
                preferred_element_type=F32,
            )
            for f in range(2):
                at = (f, pl.ds(pl.multiple_of(m * 8 * size, 8 * size), 8 * size))
                term = y[:, f * 512 : (f + 1) * 512]
                total[at] = term if u == 0 else total[at] + term
            return carry

        lax.fori_loop(0, 2, step, 0)

    y, ya, yb, yab = p.y, p.ya, p.yb, p.yab

    late, ready, results = [], [], []

    def act_l(half, f):
        wait_weights(9)
        arrive_once(*[("g", 12 + s, 3, half) for s in range(4)])
        size = HALVES[half][1]

        def step(m, carry):
            term = lax.dot_general(
                attended_rows(3, half, m), wo[3, f * 512 : (f + 1) * 512],
                (((1,), (1,)), ((), ())), preferred_element_type=F32,
            )
            at = pl.ds(pl.multiple_of(m * 8 * size, 8 * size), 8 * size)
            total = (acc[half][f, at] + term).astype(BF16)
            for i in range(8):
                po[half][f, i % 2, 4 * m + i // 2] = total[i * size : (i + 1) * size]
            return carry

        lax.fori_loop(0, 2, step, 0)
        flying["c", half, f] = net.remote(po[half].at[f, p.oc], rc[half].at[f], to_core, late)
        ready.append((half, f))
        if len(ready) == 4:
            net.finish()

    def act_u(stage, half, f):
        mine, key = po[half].at[f, p.c], ("u", stage, half, f)
        one, two = ones[half].at[f], twos[half].at[f]

        def add(at, other):
            mine[at] = mine[at] + other

        def hand(block, dst, dev):
            flying["u", stage + 1, half, f, len(flying)] = net.remote(
                mine.at[block], dst, dev, late
            )

        if stage == 0:
            arrive(("c", half, f))
            for i in range(8):
                add(i, rc[half][f, i])
            hand(2 * yab + p.zh, one.at[0, 0], to_a)
            hand(2 * yab + oz, one.at[1, 0], to_b)
            hand(2 * ya + p.zh, one.at[0, 1], to_a)
            hand(2 * yb + oz, one.at[1, 1], to_b)
            return
        arrive(*[k for k in flying if k[:4] == key])
        if stage == 1:
            add(2 * yb + p.zh, one[0, 0])
            hand(2 * yb + p.zh, two.at[0], to_b)
            add(2 * ya + oz, one[1, 0])
            hand(2 * ya + oz, two.at[1], p.dev(y=ya, zh=oz))
            add(2 * y + oz, one[1, 1])
            hand(2 * y + oz, two.at[2], p.dev(zh=oz))
            add(2 * y + p.zh, one[0, 1])
            return
        low, size = HALVES[half]
        here, there = mine[2 * y + p.zh] + two[0], two[1] + two[2]
        for z in range(2):
            part_z = jnp.where(p.zh == z, here, there)
            for e in range(2):
                at = (2 * f + e) * 512 + z * 256
                fin[low : low + size, at : at + 256] = part_z[:, e * 256 : (e + 1) * 256]
        piece = (pl.ds(low, size), pl.ds(f * 1024, 1024))
        results.append(net.local(fin.at[piece], out_ref.at[piece]))

    seg_q = jnp.transpose(
        jnp.broadcast_to(seg_ref[pl.ds(p.token_block, 1), :], (BLOCK, BLOCK))
    )
    lane = lax.broadcasted_iota(jnp.int32, (BLOCK, BLOCK), 1)
    query = p.token_block * BLOCK + lax.broadcasted_iota(jnp.int32, (BLOCK, BLOCK), 0)
    for i in range(WINDOW):
        b = lax.rem(p.token_block + 16 - (WINDOW - 1) + i, 16)
        allowed = (b * BLOCK + lane <= query) & (seg_ref[pl.ds(b, 1), :] == seg_q)
        bias[:, i * BLOCK : (i + 1) * BLOCK] = jnp.where(allowed, F32(0), F32(NEGATIVE))

    actions = dict(
        H=act_h, S=act_s, F=act_f, P=act_p, C=act_c, A=act_a, G=act_g, O=act_o, L=act_l, U=act_u
    )
    for name, *arguments in ORDER:
        actions[name](*arguments)
    for cp in late:
        cp.wait_send()
    for cp in results:
        cp.wait()


def body(hidden_in, segment_ids, q_weight, k_weight, value_weight, out_weight):
    vmem = pl.BlockSpec(memory_space=pltpu.VMEM)
    hbm = pl.BlockSpec(memory_space=pl.ANY)
    cos, sin = tables()
    blocks = lambda *shape: pltpu.VMEM(shape, BF16)
    sizes = [size for _, size in HALVES]
    return pl.pallas_call(
        kernel,
        out_shape=jax.ShapeDtypeStruct((BLOCK, 2048), BF16),
        in_specs=[vmem, vmem, hbm, hbm, hbm, hbm, hbm, hbm],
        out_specs=hbm,
        scratch_shapes=[
            blocks(2, BLOCK, 1024),
            blocks(2048, 1024),
            blocks(2, 1024, HEAD),
            blocks(4, 1024, 512),
            blocks(2, 2, BLOCK, HEAD),
            blocks(4, 2, BLOCK, 512),
            blocks(18, 16, BLOCK, HEAD),
            blocks(18, 8, BLOCK, HEAD),
            blocks(18, 4, BLOCK, HEAD),
            blocks(18, 2, BLOCK, HEAD),
            blocks(18, 1, BLOCK, HEAD),
            pltpu.VMEM((BLOCK, HEAD), F32),
            pltpu.VMEM((BLOCK, HEAD), F32),
            blocks(2, WINDOW, BLOCK, HEAD),
            pltpu.VMEM((BLOCK, WINDOW * BLOCK), F32),
            blocks(16, 16, BLOCK, HEAD),
            blocks(4, 1024, 512),
            blocks(4, 2, BLOCK, 512),
            *[pltpu.VMEM((2, 16 * size, 512), F32) for size in sizes],
            *[blocks(2, 2, 8, size, 512) for size in sizes],
            *[blocks(2, 8, size, 512) for size in sizes],
            *[blocks(2, 2, 2, size, 512) for size in sizes],
            *[blocks(2, 3, size, 512) for size in sizes],
            blocks(BLOCK, 2048),
            pltpu.SemaphoreType.DMA((SEMAPHORES,)),
            pltpu.SemaphoreType.DMA((SEMAPHORES,)),
        ],
        compiler_params=pltpu.CompilerParams(
            collective_id=0, has_side_effects=True, vmem_limit_bytes=63 << 20
        ),
    )(hidden_in, segment_ids.reshape(16, BLOCK), cos, sin, q_weight, k_weight, value_weight,
      out_weight)


def solution(mesh):
    placed = (
        P("col", "row"),
        P(),
        P(("row", "col"), None),
        P(("row", "col"), None),
        P(("row", "col"), None),
        P(("row", "col"), None),
    )
    return jax.shard_map(
        body, mesh=mesh, in_specs=placed, out_specs=P("col", "row"), check_vma=False
    )
```

```python
import math

import jax
import jax.numpy as jnp
import numpy as np
from jax import lax
from jax.experimental import pallas as pl
from jax.experimental.pallas import tpu as pltpu
from jax.sharding import PartitionSpec as P

HEAD = 128
BLOCK = 128
THETA = 500000.0
NEGATIVE = -1e30
SEMAPHORES = 400
WINDOW = 5
F32 = jnp.float32
BF16 = jnp.bfloat16
MESH = pl.DeviceIdType.MESH


class Place:
    def __init__(self):
        row, col = lax.axis_index("row"), lax.axis_index("col")
        self.x, self.zl = lax.div(row, 2), lax.rem(row, 2)
        self.y, self.zh, self.c = lax.div(col, 4), lax.rem(lax.div(col, 2), 2), lax.rem(col, 2)
        self.col = col
        self.oc = 1 - self.c
        x, y, zl, zh = self.x, self.y, self.zl, self.zh
        self.ya, self.yb = y + 1 - 2 * lax.rem(y, 2), 3 - y
        self.yab = 3 - self.ya
        self.xa, self.xb = x + 1 - 2 * lax.rem(x, 2), 3 - x
        self.bits = (lax.div(x, 2), lax.rem(x + lax.div(x, 2), 2), zh, lax.rem(zl + zh, 2))
        self.partners = (
            self.dev(x=self.xb),
            self.dev(x=self.xa),
            self.dev(zh=1 - zh, zl=1 - zl),
            self.dev(zl=1 - zl),
        )
        self.token_block = (
            8 * self.bits[0] + 4 * self.bits[1] + 2 * self.bits[2] + self.bits[3]
        )

    def dev(self, **k):
        g = lambda n: k.get(n, getattr(self, n))
        return (2 * g("x") + g("zl"), 4 * g("y") + 2 * g("zh") + g("c"))

    def ycore_partners(self):
        return [
            self.dev(c=self.oc),
            self.dev(y=self.ya),
            self.dev(y=self.ya, c=self.oc),
            self.dev(y=self.yb),
            self.dev(y=self.yb, c=self.oc),
        ]

    def block_dev(self, t):
        t = lax.rem(t + 16, 16)
        n0, n1 = lax.div(t, 8), lax.rem(lax.div(t, 4), 2)
        n2, n3 = lax.rem(lax.div(t, 2), 2), lax.rem(t, 2)
        return self.dev(x=2 * n0 + lax.rem(n0 + n1, 2), zh=n2, zl=lax.rem(n2 + n3, 2))

    def all_partners(self):
        window = [self.block_dev(self.token_block + d) for i in range(1, WINDOW) for d in (i, -i)]
        return (
            self.ycore_partners()
            + [self.dev(y=y, zh=1 - self.zh) for y in (self.y, self.ya, self.yb)]
            + list(self.partners)
            + window
        )


def order(s):
    return [(s + k) % 4 for k in range(4)]


def barrier(devices):
    sem = pltpu.get_barrier_semaphore()
    for d in devices:
        pl.semaphore_signal(sem, inc=1, device_id=d, device_id_type=MESH)
    pl.semaphore_wait(sem, len(devices))


class Net:
    def __init__(self, send, recv):
        self.send, self.recv, self.n, self.open = send, recv, 0, []

    def remote(self, src, dst, dev, into=None):
        i = self.n
        self.n += 1
        cp = pltpu.make_async_remote_copy(
            src, dst, self.send.at[i], self.recv.at[i], device_id=dev, device_id_type=MESH
        )
        cp.start()
        (self.open if into is None else into).append(cp)
        return cp

    def local(self, src, dst):
        i = self.n
        self.n += 1
        cp = pltpu.make_async_copy(src, dst, self.recv.at[i])
        cp.start()
        return cp

    def finish(self):
        for cp in self.open:
            cp.wait_send()
        self.open = []


def rows(i, n=1):
    return pl.ds(pl.multiple_of(i * BLOCK, BLOCK), n * BLOCK)


class Relay:
    def __init__(self, net, p, src, dst, rel):
        self.net, self.p, self.src, self.dst, self.rel = net, p, src, dst, rel
        self.waits = []
        self.ra = net.remote(src(2 * p.yab + p.c), rel.at[0], p.dev(y=p.ya))
        self.rb = net.remote(src(2 * p.yab + p.oc), rel.at[1], p.dev(y=p.yb))

    def start(self):
        net, p, src = self.net, self.p, self.src
        y, c, oc = p.y, p.c, p.oc
        mine = self.dst.at[rows(2 * y + c)]
        self.waits += [
            net.remote(src(2 * p.ya + c), mine, p.dev(y=p.ya)),
            net.remote(src(2 * p.yb + c), mine, p.dev(y=p.yb)),
            net.remote(src(2 * p.ya + oc), mine, p.dev(y=p.ya, c=oc)),
            net.remote(src(2 * p.yb + oc), mine, p.dev(y=p.yb, c=oc)),
            net.remote(src(2 * y + oc), mine, p.dev(c=oc)),
        ]
        self.own = net.local(src(2 * y + c), mine)

    def forward(self, way):
        p = self.p
        (self.ra, self.rb)[way].wait_recv()
        origin = (p.ya, p.yb)[way]
        to = (p.dev(y=p.yb), p.dev(y=p.ya, c=p.oc))[way]
        self.waits.append(
            self.net.remote(self.rel.at[way], self.dst.at[rows(2 * origin + p.c)], to)
        )

    def wait(self):
        self.own.wait()
        for cp in self.waits:
            cp.wait_recv()


def prefix(bits, o, k):
    total = 0
    for i in range(k):
        total = total + bits[o[i]] * (8 >> i)
    return total


def tables():
    inverse = np.power(np.float32(THETA), -2.0 * np.arange(64, dtype=np.float32) / HEAD)
    angles = np.arange(2048, dtype=np.float32)[:, None] * inverse.astype(np.float32)[None, :]
    angles = angles.astype(np.float64)
    cos, sin = np.cos(angles), np.sin(angles)
    cos = np.concatenate([cos, cos], axis=1).astype(np.float32)
    sin = np.concatenate([-sin, sin], axis=1).astype(np.float32)
    return cos, sin


QUERIES = {1: (0, 2), 2: (2, 2), 3: (4, 4), 4: (8, 4), 5: (12, 4)}
HALVES = ((0, 48), (48, 80))
GATHER_HALVES = (0, 1)
WHOLE_STAGES = 0
ORDER = (
    ("S",1,0), ("S",0,0), ("S",2,0), ("H","swap"), ("H","a1"), ("F",0,1), ("F",1,1),
    ("F",1,0), ("F",0,0), ("H","b2"), ("H","b1"), ("S",1,1), ("S",0,1), ("F",2,0),
    ("F",2,1), ("H","a2"), ("S",2,1), ("S",3,0), ("S",3,1), ("H","f1"), ("H","f2"), ("P",1),
    ("P",0), ("P",2), ("C",0,0), ("F",3,1), ("F",3,0), ("C",1,0), ("S",4,0), ("C",17,0),
    ("C",16,0), ("C",3,0), ("C",0,1), ("S",4,1), ("C",2,0), ("P",3,0), ("P",3,1),
    ("C",17,1), ("C",16,1), ("C",2,1), ("C",3,1), ("F",4,1), ("F",4,0), ("S",5,0),
    ("C",1,1), ("S",5,1), ("C",0,2), ("C",4,0), ("C",5,0), ("C",6,0), ("C",7,0), ("C",17,2),
    ("C",3,2), ("P",4,0), ("C",16,2), ("P",4,1), ("C",5,1), ("F",5,1), ("F",5,0), ("S",6,0),
    ("C",7,1), ("S",7,0), ("C",17,3), ("S",8,0), ("C",2,2), ("C",3,3), ("C",1,2), ("S",9,0),
    ("S",6,1), ("C",6,1), ("C",4,1), ("C",0,3), ("C",16,3), ("C",8,0), ("C",9,0), ("C",7,2),
    ("C",10,0), ("C",11,0), ("P",5,0), ("C",4,2), ("P",5,1), ("C",1,3), ("F",6,1),
    ("S",8,1), ("C",2,3), ("C",6,2), ("F",6,0), ("A",0), ("C",7,3), ("C",9,1), ("C",5,2),
    ("F",7,0), ("C",10,1), ("C",11,1), ("C",8,1), ("C",4,3), ("F",7,1), ("C",13,0),
    ("F",8,1), ("C",12,0), ("F",8,0), ("G",2,0,0), ("C",6,3), ("G",1,0,0), ("F",9,1),
    ("G",2,0,1), ("C",14,0), ("C",15,0), ("C",5,3), ("G",3,0,1), ("G",0,0,1), ("A",1),
    ("G",1,0,1), ("C",11,2), ("G",3,0,0), ("C",9,2), ("C",8,2), ("C",10,2), ("G",0,0,0),
    ("C",13,1), ("C",12,1), ("C",14,1), ("G",0,1,1), ("G",2,1,0), ("G",3,1,1), ("G",1,1,0),
    ("G",4,0,1), ("G",6,0,0), ("G",5,0,0), ("C",15,1), ("G",7,0,1), ("G",6,0,1),
    ("G",2,1,1), ("G",5,0,1), ("G",4,0,0), ("G",3,1,0), ("C",9,3), ("G",1,1,1), ("C",11,3),
    ("C",10,3), ("G",7,0,0), ("C",8,3), ("G",0,1,0), ("A",2), ("C",12,2), ("C",13,2),
    ("G",4,1,0), ("C",15,2), ("G",5,1,0), ("G",3,2,1), ("G",7,1,1), ("C",14,2), ("G",4,1,1),
    ("G",5,1,1), ("G",0,2,1), ("G",8,0,0), ("G",7,1,0), ("S",7,1), ("G",9,0,0), ("G",2,2,1),
    ("G",11,0,1), ("C",13,3), ("G",1,2,1), ("C",12,3), ("G",9,0,1), ("C",15,3), ("F",9,0),
    ("C",14,3), ("G",6,1,1), ("A",3), ("G",10,0,1), ("G",7,2,1), ("G",8,0,1), ("G",9,1,1),
    ("G",5,2,1), ("G",11,0,0), ("G",10,0,0), ("S",9,1), ("G",11,1,1), ("G",12,0,0),
    ("G",15,0,1), ("G",14,0,0), ("G",14,0,1), ("G",12,0,1), ("G",13,0,1), ("G",13,0,0),
    ("G",4,2,1), ("G",8,1,1), ("G",10,1,1), ("G",15,0,0), ("G",6,2,1), ("O",0,1),
    ("G",14,1,1), ("G",13,1,1), ("G",12,1,1), ("G",6,1,0), ("G",15,1,1), ("G",9,2,1),
    ("G",11,2,1), ("G",10,2,1), ("G",8,2,1), ("G",14,2,1), ("G",9,1,0), ("G",15,2,1),
    ("G",12,2,1), ("G",15,1,0), ("G",10,1,0), ("G",13,1,0), ("G",2,2,0), ("G",14,1,0),
    ("G",6,2,0), ("G",13,2,1), ("G",8,1,0), ("G",3,2,0), ("G",12,1,0), ("G",11,1,0),
    ("G",1,2,0), ("G",5,2,0), ("G",0,2,0), ("O",1,1), ("G",4,2,0), ("O",2,1), ("G",7,2,0),
    ("L",1,1), ("G",9,2,0), ("G",10,2,0), ("G",14,2,0), ("G",13,2,0), ("L",1,0),
    ("G",8,2,0), ("G",12,2,0), ("G",11,2,0), ("O",0,0), ("G",15,2,0), ("U",0,1,1),
    ("O",1,0), ("U",0,1,0), ("O",2,0), ("L",0,1), ("U",1,1,1), ("L",0,0), ("U",0,0,1),
    ("U",1,1,0), ("U",0,0,0), ("U",2,1,1), ("U",1,0,1), ("U",1,0,0), ("U",2,1,0),
    ("U",2,0,1), ("U",2,0,0),
)


def kernel(
    h_ref, seg_ref, cos_ref, sin_ref, q_ref, k_ref, v_ref, o_ref,
    out_ref,
    hx, xs, wkv, wq, relkv, relq, part, r0, r1, r2, r3, cos, sin, kv, bias,
    att, wo, relo, acc0, acc1, po0, po1, rc0, rc1, ones0, ones1, twos0, twos1, fin, send, recv,
):
    p = Place()
    net = Net(send, recv)
    recvs = (r0, r1, r2, r3)
    acc, po, rc = (acc0, acc1), (po0, po1), (rc0, rc1)
    ones, twos = (ones0, ones1), (twos0, twos1)
    for z in range(2):
        for yy in range(4):
            hx[z, :, yy * 256 : (yy + 1) * 256] = h_ref[
                :, yy * 512 + z * 256 : yy * 512 + z * 256 + 256
            ]
    xs[rows(p.col)] = hx[p.zh]
    barrier(p.all_partners())

    flying = {}

    def arrive(*keys):
        for key in keys:
            flying.pop(key).wait_recv()

    def arrive_once(*keys):
        arrive(*[key for key in keys if key in flying])

    to_a, to_b, to_core = p.dev(y=p.ya), p.dev(y=p.yb), p.dev(c=p.oc)
    oz = 1 - p.zh

    def push(key, y, zh, dev):
        block = xs.at[rows(4 * y + 2 * zh + p.c)]
        flying[key] = net.remote(block, block, dev)

    flying["swap"] = net.remote(hx.at[oz], xs.at[rows(p.col)], p.dev(zh=oz))
    push("a1", p.y, p.zh, to_a)
    push("b1", p.y, p.zh, to_b)
    push("c1", p.y, p.zh, to_core)
    table_copies = [
        net.local(cos_ref.at[rows(p.token_block)], cos),
        net.local(sin_ref.at[rows(p.token_block)], sin),
    ]

    def act_h(name):
        arrive(name)
        if name == "a1":
            push("f1", p.ya, p.zh, to_b)
            push("h1", p.ya, p.zh, to_core)
        elif name == "b1":
            push("h2", p.yb, p.zh, to_core)
        elif name == "swap":
            push("a2", p.y, oz, to_a)
            push("b2", p.y, oz, to_b)
            push("c2", p.y, oz, to_core)
        elif name == "b2":
            push("f2", p.yb, oz, to_a)
            push("h3", p.yb, oz, to_core)
        elif name == "a2":
            push("h4", p.ya, oz, to_core)
        elif name == "f1":
            push("h5", p.yab, p.zh, to_core)
        elif name == "f2":
            push("h6", p.yab, oz, to_core)

    def columns(ref, width, j=0, chunk=None):
        chunk = chunk or width
        return lambda d: ref.at[:, pl.ds(pl.multiple_of(d * width + j * chunk, chunk), chunk)]

    weights = {}

    def query_weights(t):
        first, count = QUERIES[t]
        return first // 4, first % 4 * HEAD, count * HEAD

    def act_s(t, part):
        if part:
            for relay in weights[t]:
                relay.start()
        elif t == 0:
            weights[t] = [
                Relay(net, p, columns(k_ref, HEAD), wkv.at[0], relkv.at[0]),
                Relay(net, p, columns(v_ref, HEAD), wkv.at[1], relkv.at[1]),
            ]
        elif t < 6:
            j, at, width = query_weights(t)
            weights[t] = [
                Relay(
                    net, p,
                    columns(q_ref, 2048, QUERIES[t][0] * HEAD // width, width),
                    wq.at[j, :, pl.ds(at, width)],
                    relq.at[j, :, :, pl.ds(at, width)],
                )
            ]
        else:
            j = t - 6
            weights[t] = [Relay(net, p, columns(o_ref, 2048, j, 512), wo.at[j], relo.at[j])]

    def act_f(t, way):
        for w in weights[t]:
            w.forward(way)

    def wait_weights(t):
        for w in weights.pop(t, ()):
            w.wait()

    def slot_order(slot):
        return order((0, 2)[slot - 16] if slot >= 16 else slot % 4)

    def place_in(o, nat):
        return 8 * nat[o[0]] + 4 * nat[o[1]] + 2 * nat[o[2]] + nat[o[3]]

    def scatter(slot, k):
        o, n = slot_order(slot), 8 >> k
        at = prefix(p.bits, o, k) + (1 - p.bits[o[k]]) * n
        flying["r", slot, k] = net.remote(
            part.at[slot, pl.ds(at, n)], recvs[k].at[slot], p.partners[o[k]]
        )

    def act_p(t, pair=0):
        arrive_once("c1", "c2", "h1", "h2", "h3", "h4", "h5", "h6")
        wait_weights(t)
        if t == 0:
            slots = (16, 17)
        else:
            slots = range(QUERIES[t][0] + 2 * pair, QUERIES[t][0] + 2 * pair + 2)
            j, at, _ = query_weights(t)
            at = at + 256 * pair

        def step(m, carry):
            x = xs[pl.ds(pl.multiple_of(m * 512, 512), 512), :]
            if t == 0:
                w = jnp.concatenate([wkv[0], wkv[1]], axis=1)
            else:
                w = wq[j, :, at : at + 256]
            y = jnp.dot(x, w, preferred_element_type=F32).astype(BF16)
            n0, n1 = lax.div(m, 2), lax.rem(m, 2)
            for i in range(4):
                nat = (n0, n1, i // 2, i % 2)
                for g, slot in enumerate(slots):
                    part[slot, place_in(slot_order(slot), nat)] = y[
                        i * BLOCK : (i + 1) * BLOCK, g * HEAD : (g + 1) * HEAD
                    ]
            return carry

        lax.fori_loop(0, 4, step, 0)
        for slot in slots:
            scatter(slot, 0)

    def rope(u):
        while table_copies:
            table_copies.pop().wait()
        return u * cos[...] + pltpu.roll(u, 64, 1) * sin[...]

    queries = {}

    def act_c(slot, k):
        arrive(("r", slot, k))
        o, n = slot_order(slot), 8 >> k
        at = prefix(p.bits, o, k + 1)
        if k < 3:
            for i in range(n):
                part[slot, at + i] = part[slot, at + i] + recvs[k][slot, i]
            scatter(slot, k + 1)
            return
        total = part[slot, at].astype(F32) + recvs[k][slot, 0].astype(F32)
        if slot < 16:
            queries[slot] = (rope(total) * (math.log2(math.e) / math.sqrt(HEAD))).astype(BF16)
        else:
            which = slot - 16
            kv[which, WINDOW - 1] = (total if which else rope(total)).astype(BF16)
            for d in range(1, WINDOW):
                flying["window", which, d] = net.remote(
                    kv.at[which, WINDOW - 1],
                    kv.at[which, WINDOW - 1 - d],
                    p.block_dev(p.token_block + d),
                )

    def gather(slot, i):
        o, k = slot_order(slot), 3 - i
        at = pl.ds(prefix(p.bits, o, k + 1), 1 << i)
        if i < WHOLE_STAGES:
            blocks = att.at[slot, at]
            flying["g", slot, i] = net.remote(blocks, blocks, p.partners[o[k]])

    def gather_half(slot, i, half):
        o, k = slot_order(slot), 3 - i
        at = pl.ds(prefix(p.bits, o, k + 1), 1 << i)
        blocks = att.at[slot, at, pl.ds(*HALVES[half])]
        flying["g", slot, i, half] = net.remote(blocks, blocks, p.partners[o[k]])

    def gather_on(slot, i):
        if i < WHOLE_STAGES:
            gather(slot, i)
        else:
            for half in GATHER_HALVES:
                gather_half(slot, i, half)

    def act_a(u):
        arrive_once(*[("window", which, d) for which in range(2) for d in range(1, WINDOW)])
        slots = range(4 * u, 4 * u + 4)
        scores = lax.dot_general(
            jnp.concatenate([queries.pop(slot) for slot in slots], axis=0),
            kv[0].reshape(WINDOW * BLOCK, HEAD),
            (((1,), (1,)), ((), ())),
            preferred_element_type=F32,
        )
        scores = scores.reshape(4, BLOCK, WINDOW * BLOCK) + bias[...][None]
        scores = scores.reshape(4 * BLOCK, WINDOW * BLOCK)
        exponent = jnp.exp2(scores - jnp.max(scores, axis=-1, keepdims=True))
        denominator = jnp.sum(exponent, axis=-1, keepdims=True)
        attended = jnp.dot(
            exponent.astype(BF16),
            kv[1].reshape(WINDOW * BLOCK, HEAD),
            preferred_element_type=F32,
        )
        attended = (attended * (1.0 / denominator)).astype(BF16)
        for s, slot in enumerate(slots):
            att[slot, prefix(p.bits, order(s), 4)] = attended[s * BLOCK : (s + 1) * BLOCK]
            gather_on(slot, 0)

    def act_g(slot, i, *half):
        arrive(("g", slot, i, *half))
        if half:
            gather_half(slot, i + 1, *half)
        else:
            gather_on(slot, i + 1)

    def attended_rows(u, half, m):
        low, size = HALVES[half]
        blocks = []
        for i in range(8):
            nat = (m, i // 4, i // 2 % 2, i % 2)
            blocks.append(
                jnp.concatenate(
                    [att[4 * u + s, place_in(order(s), nat), low : low + size] for s in range(4)],
                    axis=1,
                )
            )
        return jnp.concatenate(blocks, axis=0)

    def act_o(u, half):
        wait_weights(6 + u)
        arrive(*[("g", 4 * u + s, 3, half) for s in range(4)])
        total, size = acc[half], HALVES[half][1]

        def step(m, carry):
            y = lax.dot_general(
                attended_rows(u, half, m), wo[u], (((1,), (1,)), ((), ())),
                preferred_element_type=F32,
            )
            for f in range(2):
                at = (f, pl.ds(pl.multiple_of(m * 8 * size, 8 * size), 8 * size))
                term = y[:, f * 512 : (f + 1) * 512]
                total[at] = term if u == 0 else total[at] + term
            return carry

        lax.fori_loop(0, 2, step, 0)

    y, ya, yb, yab = p.y, p.ya, p.yb, p.yab

    late, ready, results = [], [], []

    def act_l(half, f):
        wait_weights(9)
        arrive_once(*[("g", 12 + s, 3, half) for s in range(4)])
        size = HALVES[half][1]

        def step(m, carry):
            term = lax.dot_general(
                attended_rows(3, half, m), wo[3, f * 512 : (f + 1) * 512],
                (((1,), (1,)), ((), ())), preferred_element_type=F32,
            )
            at = pl.ds(pl.multiple_of(m * 8 * size, 8 * size), 8 * size)
            total = (acc[half][f, at] + term).astype(BF16)
            for i in range(8):
                po[half][f, i % 2, 4 * m + i // 2] = total[i * size : (i + 1) * size]
            return carry

        lax.fori_loop(0, 2, step, 0)
        flying["c", half, f] = net.remote(po[half].at[f, p.oc], rc[half].at[f], to_core, late)
        ready.append((half, f))
        if len(ready) == 4:
            net.finish()

    def act_u(stage, half, f):
        mine, key = po[half].at[f, p.c], ("u", stage, half, f)
        one, two = ones[half].at[f], twos[half].at[f]

        def add(at, other):
            mine[at] = mine[at] + other

        def hand(block, dst, dev):
            flying["u", stage + 1, half, f, len(flying)] = net.remote(
                mine.at[block], dst, dev, late
            )

        if stage == 0:
            arrive(("c", half, f))
            for i in range(8):
                add(i, rc[half][f, i])
            hand(2 * yab + p.zh, one.at[0, 0], to_a)
            hand(2 * yab + oz, one.at[1, 0], to_b)
            hand(2 * ya + p.zh, one.at[0, 1], to_a)
            hand(2 * yb + oz, one.at[1, 1], to_b)
            return
        arrive(*[k for k in flying if k[:4] == key])
        if stage == 1:
            add(2 * yb + p.zh, one[0, 0])
            hand(2 * yb + p.zh, two.at[0], to_b)
            add(2 * ya + oz, one[1, 0])
            hand(2 * ya + oz, two.at[1], p.dev(y=ya, zh=oz))
            add(2 * y + oz, one[1, 1])
            hand(2 * y + oz, two.at[2], p.dev(zh=oz))
            add(2 * y + p.zh, one[0, 1])
            return
        low, size = HALVES[half]
        here, there = mine[2 * y + p.zh] + two[0], two[1] + two[2]
        for z in range(2):
            part_z = jnp.where(p.zh == z, here, there)
            for e in range(2):
                at = (2 * f + e) * 512 + z * 256
                fin[low : low + size, at : at + 256] = part_z[:, e * 256 : (e + 1) * 256]
        piece = (pl.ds(low, size), pl.ds(f * 1024, 1024))
        results.append(net.local(fin.at[piece], out_ref.at[piece]))

    seg_q = jnp.transpose(
        jnp.broadcast_to(seg_ref[pl.ds(p.token_block, 1), :], (BLOCK, BLOCK))
    )
    lane = lax.broadcasted_iota(jnp.int32, (BLOCK, BLOCK), 1)
    query = p.token_block * BLOCK + lax.broadcasted_iota(jnp.int32, (BLOCK, BLOCK), 0)
    for i in range(WINDOW):
        b = lax.rem(p.token_block + 16 - (WINDOW - 1) + i, 16)
        allowed = (b * BLOCK + lane <= query) & (seg_ref[pl.ds(b, 1), :] == seg_q)
        bias[:, i * BLOCK : (i + 1) * BLOCK] = jnp.where(allowed, F32(0), F32(NEGATIVE))

    actions = dict(
        H=act_h, S=act_s, F=act_f, P=act_p, C=act_c, A=act_a, G=act_g, O=act_o, L=act_l, U=act_u
    )
    for name, *arguments in ORDER:
        actions[name](*arguments)
    for cp in late:
        cp.wait_send()
    for cp in results:
        cp.wait()


def body(hidden_in, segment_ids, q_weight, k_weight, value_weight, out_weight):
    vmem = pl.BlockSpec(memory_space=pltpu.VMEM)
    hbm = pl.BlockSpec(memory_space=pl.ANY)
    cos, sin = tables()
    blocks = lambda *shape: pltpu.VMEM(shape, BF16)
    sizes = [size for _, size in HALVES]
    return pl.pallas_call(
        kernel,
        out_shape=jax.ShapeDtypeStruct((BLOCK, 2048), BF16),
        in_specs=[vmem, vmem, hbm, hbm, hbm, hbm, hbm, hbm],
        out_specs=hbm,
        scratch_shapes=[
            blocks(2, BLOCK, 1024),
            blocks(2048, 1024),
            blocks(2, 1024, HEAD),
            blocks(4, 1024, 512),
            blocks(2, 2, BLOCK, HEAD),
            blocks(4, 2, BLOCK, 512),
            blocks(18, 16, BLOCK, HEAD),
            blocks(18, 8, BLOCK, HEAD),
            blocks(18, 4, BLOCK, HEAD),
            blocks(18, 2, BLOCK, HEAD),
            blocks(18, 1, BLOCK, HEAD),
            pltpu.VMEM((BLOCK, HEAD), F32),
            pltpu.VMEM((BLOCK, HEAD), F32),
            blocks(2, WINDOW, BLOCK, HEAD),
            pltpu.VMEM((BLOCK, WINDOW * BLOCK), F32),
            blocks(16, 16, BLOCK, HEAD),
            blocks(4, 1024, 512),
            blocks(4, 2, BLOCK, 512),
            *[pltpu.VMEM((2, 16 * size, 512), F32) for size in sizes],
            *[blocks(2, 2, 8, size, 512) for size in sizes],
            *[blocks(2, 8, size, 512) for size in sizes],
            *[blocks(2, 2, 2, size, 512) for size in sizes],
            *[blocks(2, 3, size, 512) for size in sizes],
            blocks(BLOCK, 2048),
            pltpu.SemaphoreType.DMA((SEMAPHORES,)),
            pltpu.SemaphoreType.DMA((SEMAPHORES,)),
        ],
        compiler_params=pltpu.CompilerParams(
            collective_id=0, has_side_effects=True, vmem_limit_bytes=63 << 20
        ),
    )(hidden_in, segment_ids.reshape(16, BLOCK), cos, sin, q_weight, k_weight, value_weight,
      out_weight)


def solution(mesh):
    placed = (
        P("col", "row"),
        P(),
        P(("row", "col"), None),
        P(("row", "col"), None),
        P(("row", "col"), None),
        P(("row", "col"), None),
    )
    return jax.shard_map(
        body, mesh=mesh, in_specs=placed, out_specs=P("col", "row"), check_vma=False
    )
```

```python
import math

import jax
import jax.numpy as jnp
import numpy as np
from jax import lax
from jax.experimental import pallas as pl
from jax.experimental.pallas import tpu as pltpu
from jax.sharding import PartitionSpec as P

HEAD = 128
BLOCK = 128
THETA = 500000.0
NEGATIVE = -1e30
SEMAPHORES = 400
WINDOW = 5
F32 = jnp.float32
BF16 = jnp.bfloat16
MESH = pl.DeviceIdType.MESH


class Place:
    def __init__(self):
        row, col = lax.axis_index("row"), lax.axis_index("col")
        self.x, self.zl = lax.div(row, 2), lax.rem(row, 2)
        self.y, self.zh, self.c = lax.div(col, 4), lax.rem(lax.div(col, 2), 2), lax.rem(col, 2)
        self.col = col
        self.oc = 1 - self.c
        x, y, zl, zh = self.x, self.y, self.zl, self.zh
        self.ya, self.yb = y + 1 - 2 * lax.rem(y, 2), 3 - y
        self.yab = 3 - self.ya
        self.xa, self.xb = x + 1 - 2 * lax.rem(x, 2), 3 - x
        self.bits = (lax.div(x, 2), lax.rem(x + lax.div(x, 2), 2), zh, lax.rem(zl + zh, 2))
        self.partners = (
            self.dev(x=self.xb),
            self.dev(x=self.xa),
            self.dev(zh=1 - zh, zl=1 - zl),
            self.dev(zl=1 - zl),
        )
        self.token_block = (
            8 * self.bits[0] + 4 * self.bits[1] + 2 * self.bits[2] + self.bits[3]
        )

    def dev(self, **k):
        g = lambda n: k.get(n, getattr(self, n))
        return (2 * g("x") + g("zl"), 4 * g("y") + 2 * g("zh") + g("c"))

    def ycore_partners(self):
        return [
            self.dev(c=self.oc),
            self.dev(y=self.ya),
            self.dev(y=self.ya, c=self.oc),
            self.dev(y=self.yb),
            self.dev(y=self.yb, c=self.oc),
        ]

    def block_dev(self, t):
        t = lax.rem(t + 16, 16)
        n0, n1 = lax.div(t, 8), lax.rem(lax.div(t, 4), 2)
        n2, n3 = lax.rem(lax.div(t, 2), 2), lax.rem(t, 2)
        return self.dev(x=2 * n0 + lax.rem(n0 + n1, 2), zh=n2, zl=lax.rem(n2 + n3, 2))

    def all_partners(self):
        window = [self.block_dev(self.token_block + d) for i in range(1, WINDOW) for d in (i, -i)]
        return (
            self.ycore_partners()
            + [self.dev(y=y, zh=1 - self.zh) for y in (self.y, self.ya, self.yb)]
            + list(self.partners)
            + window
        )


def order(s):
    return [(s + k) % 4 for k in range(4)]


def barrier(devices):
    sem = pltpu.get_barrier_semaphore()
    for d in devices:
        pl.semaphore_signal(sem, inc=1, device_id=d, device_id_type=MESH)
    pl.semaphore_wait(sem, len(devices))


class Net:
    def __init__(self, send, recv):
        self.send, self.recv, self.n, self.open = send, recv, 0, []

    def remote(self, src, dst, dev, into=None):
        i = self.n
        self.n += 1
        cp = pltpu.make_async_remote_copy(
            src, dst, self.send.at[i], self.recv.at[i], device_id=dev, device_id_type=MESH
        )
        cp.start()
        (self.open if into is None else into).append(cp)
        return cp

    def local(self, src, dst):
        i = self.n
        self.n += 1
        cp = pltpu.make_async_copy(src, dst, self.recv.at[i])
        cp.start()
        return cp

    def finish(self):
        for cp in self.open:
            cp.wait_send()
        self.open = []


def rows(i, n=1):
    return pl.ds(pl.multiple_of(i * BLOCK, BLOCK), n * BLOCK)


class Relay:
    def __init__(self, net, p, src, dst, rel):
        self.net, self.p, self.src, self.dst, self.rel = net, p, src, dst, rel
        self.waits = []
        self.ra = net.remote(src(2 * p.yab + p.c), rel.at[0], p.dev(y=p.ya))
        self.rb = net.remote(src(2 * p.yab + p.oc), rel.at[1], p.dev(y=p.yb))

    def start(self):
        net, p, src = self.net, self.p, self.src
        y, c, oc = p.y, p.c, p.oc
        mine = self.dst.at[rows(2 * y + c)]
        self.waits += [
            net.remote(src(2 * p.ya + c), mine, p.dev(y=p.ya)),
            net.remote(src(2 * p.yb + c), mine, p.dev(y=p.yb)),
            net.remote(src(2 * p.ya + oc), mine, p.dev(y=p.ya, c=oc)),
            net.remote(src(2 * p.yb + oc), mine, p.dev(y=p.yb, c=oc)),
            net.remote(src(2 * y + oc), mine, p.dev(c=oc)),
        ]
        self.own = net.local(src(2 * y + c), mine)

    def forward(self, way):
        p = self.p
        (self.ra, self.rb)[way].wait_recv()
        origin = (p.ya, p.yb)[way]
        to = (p.dev(y=p.yb), p.dev(y=p.ya, c=p.oc))[way]
        self.waits.append(
            self.net.remote(self.rel.at[way], self.dst.at[rows(2 * origin + p.c)], to)
        )

    def wait(self):
        self.own.wait()
        for cp in self.waits:
            cp.wait_recv()


def prefix(bits, o, k):
    total = 0
    for i in range(k):
        total = total + bits[o[i]] * (8 >> i)
    return total


def tables():
    inverse = np.power(np.float32(THETA), -2.0 * np.arange(64, dtype=np.float32) / HEAD)
    angles = np.arange(2048, dtype=np.float32)[:, None] * inverse.astype(np.float32)[None, :]
    angles = angles.astype(np.float64)
    cos, sin = np.cos(angles), np.sin(angles)
    cos = np.concatenate([cos, cos], axis=1).astype(np.float32)
    sin = np.concatenate([-sin, sin], axis=1).astype(np.float32)
    return cos, sin


QUERIES = {1: (0, 2), 2: (2, 2), 3: (4, 4), 4: (8, 4), 5: (12, 4)}
HALVES = ((0, 48), (48, 80))
GATHER_HALVES = (0, 1)
WHOLE_STAGES = 0
ORDER = (
    ("S",1,0), ("S",0,0), ("S",2,0), ("H","z0"), ("H","z1"), ("H","swap"), ("H","a1"),
    ("F",0,1), ("F",1,1), ("F",1,0), ("F",0,0), ("H","b2"), ("H","b1"), ("S",1,1),
    ("S",0,1), ("F",2,0), ("F",2,1), ("H","a2"), ("S",2,1), ("S",3,0), ("S",3,1),
    ("H","f1"), ("H","f2"), ("P",1), ("P",0), ("P",2), ("C",0,0), ("F",3,1), ("F",3,0),
    ("C",1,0), ("S",4,0), ("C",17,0), ("C",16,0), ("C",3,0), ("C",0,1), ("S",4,1),
    ("C",2,0), ("P",3,0), ("P",3,1), ("C",17,1), ("C",16,1), ("C",2,1), ("C",3,1),
    ("F",4,1), ("F",4,0), ("S",5,0), ("C",1,1), ("S",5,1), ("C",0,2), ("C",4,0), ("C",5,0),
    ("C",6,0), ("C",7,0), ("C",17,2), ("C",3,2), ("P",4,0), ("C",16,2), ("P",4,1),
    ("C",5,1), ("F",5,1), ("F",5,0), ("S",6,0), ("C",7,1), ("S",7,0), ("C",17,3), ("S",8,0),
    ("C",2,2), ("C",3,3), ("C",1,2), ("S",9,0), ("S",6,1), ("C",6,1), ("C",4,1), ("C",0,3),
    ("C",16,3), ("C",8,0), ("C",9,0), ("C",7,2), ("C",10,0), ("C",11,0), ("P",5,0),
    ("C",4,2), ("P",5,1), ("C",1,3), ("F",6,1), ("S",8,1), ("C",2,3), ("C",6,2), ("F",6,0),
    ("A",0), ("C",7,3), ("C",9,1), ("C",5,2), ("F",7,0), ("C",10,1), ("C",11,1), ("C",8,1),
    ("C",4,3), ("F",7,1), ("C",13,0), ("F",8,1), ("C",12,0), ("F",8,0), ("G",2,0,0),
    ("C",6,3), ("G",1,0,0), ("F",9,1), ("G",2,0,1), ("C",14,0), ("C",15,0), ("C",5,3),
    ("G",3,0,1), ("G",0,0,1), ("A",1), ("G",1,0,1), ("C",11,2), ("G",3,0,0), ("C",9,2),
    ("C",8,2), ("C",10,2), ("G",0,0,0), ("C",13,1), ("C",12,1), ("C",14,1), ("G",0,1,1),
    ("G",2,1,0), ("G",3,1,1), ("G",1,1,0), ("G",4,0,1), ("G",6,0,0), ("G",5,0,0),
    ("C",15,1), ("G",7,0,1), ("G",6,0,1), ("G",2,1,1), ("G",5,0,1), ("G",4,0,0),
    ("G",3,1,0), ("C",9,3), ("G",1,1,1), ("C",11,3), ("C",10,3), ("G",7,0,0), ("C",8,3),
    ("G",0,1,0), ("A",2), ("C",12,2), ("C",13,2), ("G",4,1,0), ("C",15,2), ("G",5,1,0),
    ("G",3,2,1), ("G",7,1,1), ("C",14,2), ("G",4,1,1), ("G",5,1,1), ("G",0,2,1),
    ("G",8,0,0), ("G",7,1,0), ("S",7,1), ("G",9,0,0), ("G",2,2,1), ("G",11,0,1), ("C",13,3),
    ("G",1,2,1), ("C",12,3), ("G",9,0,1), ("C",15,3), ("F",9,0), ("C",14,3), ("G",6,1,1),
    ("A",3), ("G",10,0,1), ("G",7,2,1), ("G",8,0,1), ("G",9,1,1), ("G",5,2,1), ("G",11,0,0),
    ("G",10,0,0), ("S",9,1), ("G",11,1,1), ("G",12,0,0), ("G",15,0,1), ("G",14,0,0),
    ("G",14,0,1), ("G",12,0,1), ("G",13,0,1), ("G",13,0,0), ("G",4,2,1), ("G",8,1,1),
    ("G",10,1,1), ("G",15,0,0), ("G",6,2,1), ("O",0,1), ("G",14,1,1), ("G",13,1,1),
    ("G",12,1,1), ("G",6,1,0), ("G",15,1,1), ("G",9,2,1), ("G",11,2,1), ("G",10,2,1),
    ("G",8,2,1), ("G",14,2,1), ("G",9,1,0), ("G",15,2,1), ("G",12,2,1), ("G",15,1,0),
    ("G",10,1,0), ("G",13,1,0), ("G",2,2,0), ("G",14,1,0), ("G",6,2,0), ("G",13,2,1),
    ("G",8,1,0), ("G",3,2,0), ("G",12,1,0), ("G",11,1,0), ("G",1,2,0), ("G",5,2,0),
    ("G",0,2,0), ("O",1,1), ("G",4,2,0), ("O",2,1), ("G",7,2,0), ("L",1,1), ("G",9,2,0),
    ("G",10,2,0), ("G",14,2,0), ("G",13,2,0), ("L",1,0), ("G",8,2,0), ("G",12,2,0),
    ("G",11,2,0), ("O",0,0), ("G",15,2,0), ("U",0,1,1), ("O",1,0), ("U",0,1,0), ("O",2,0),
    ("L",0,1), ("U",1,1,1), ("L",0,0), ("U",0,0,1), ("U",1,1,0), ("U",0,0,0), ("U",2,1,1),
    ("U",1,0,1), ("U",1,0,0), ("U",2,1,0), ("U",2,0,1), ("U",2,0,0),
)


def kernel(
    h_ref, seg_ref, cos_ref, sin_ref, q_ref, k_ref, v_ref, o_ref,
    out_ref,
    hx, hop, xs, wkv, wq, relkv, relq, part, r0, r1, r2, r3, cos, sin, kv, bias,
    att, wo, relo, acc0, acc1, po0, po1, rc0, rc1, ones0, ones1, twos0, twos1, fin, send, recv,
):
    p = Place()
    net = Net(send, recv)
    recvs = (r0, r1, r2, r3)
    acc, po, rc = (acc0, acc1), (po0, po1), (rc0, rc1)
    ones, twos = (ones0, ones1), (twos0, twos1)
    for z in range(2):
        for yy in range(4):
            hx[z, :, yy * 256 : (yy + 1) * 256] = h_ref[
                :, yy * 512 + z * 256 : yy * 512 + z * 256 + 256
            ]
    xs[rows(p.col)] = hx[p.zh]
    barrier(p.all_partners())

    flying = {}

    def arrive(*keys):
        for key in keys:
            flying.pop(key).wait_recv()

    def arrive_once(*keys):
        arrive(*[key for key in keys if key in flying])

    to_a, to_b, to_core = p.dev(y=p.ya), p.dev(y=p.yb), p.dev(c=p.oc)
    oz = 1 - p.zh

    def push(key, y, zh, dev):
        block = xs.at[rows(4 * y + 2 * zh + p.c)]
        flying[key] = net.remote(block, block, dev)

    (to_zb, to_za), low, high = p.partners[2:], pl.ds(0, 64), pl.ds(64, 64)
    flying["z0"] = net.remote(hx.at[oz, low], hop.at[0], to_za)
    flying["z1"] = net.remote(hx.at[oz, high], hop.at[1], to_zb)
    push("a1", p.y, p.zh, to_a)
    push("b1", p.y, p.zh, to_b)
    push("c1", p.y, p.zh, to_core)
    table_copies = [
        net.local(cos_ref.at[rows(p.token_block)], cos),
        net.local(sin_ref.at[rows(p.token_block)], sin),
    ]

    def half_rows(zh, first):
        return xs.at[pl.ds(pl.multiple_of((4 * p.y + 2 * zh + p.c) * BLOCK + first, 64), 64)]

    def act_h(name):
        if name == "swap":
            arrive("swap0", "swap1")
        else:
            arrive(name)
        if name == "z0":
            flying["swap0"] = net.remote(hop.at[0], half_rows(p.zh, 0), to_zb)
        elif name == "z1":
            flying["swap1"] = net.remote(hop.at[1], half_rows(oz, 64), to_za)
        elif name == "a1":
            push("f1", p.ya, p.zh, to_b)
            push("h1", p.ya, p.zh, to_core)
        elif name == "b1":
            push("h2", p.yb, p.zh, to_core)
        elif name == "swap":
            push("a2", p.y, oz, to_a)
            push("b2", p.y, oz, to_b)
            push("c2", p.y, oz, to_core)
        elif name == "b2":
            push("f2", p.yb, oz, to_a)
            push("h3", p.yb, oz, to_core)
        elif name == "a2":
            push("h4", p.ya, oz, to_core)
        elif name == "f1":
            push("h5", p.yab, p.zh, to_core)
        elif name == "f2":
            push("h6", p.yab, oz, to_core)

    def columns(ref, width, j=0, chunk=None):
        chunk = chunk or width
        return lambda d: ref.at[:, pl.ds(pl.multiple_of(d * width + j * chunk, chunk), chunk)]

    weights = {}

    def query_weights(t):
        first, count = QUERIES[t]
        return first // 4, first % 4 * HEAD, count * HEAD

    def act_s(t, part):
        if part:
            for relay in weights[t]:
                relay.start()
        elif t == 0:
            weights[t] = [
                Relay(net, p, columns(k_ref, HEAD), wkv.at[0], relkv.at[0]),
                Relay(net, p, columns(v_ref, HEAD), wkv.at[1], relkv.at[1]),
            ]
        elif t < 6:
            j, at, width = query_weights(t)
            weights[t] = [
                Relay(
                    net, p,
                    columns(q_ref, 2048, QUERIES[t][0] * HEAD // width, width),
                    wq.at[j, :, pl.ds(at, width)],
                    relq.at[j, :, :, pl.ds(at, width)],
                )
            ]
        else:
            j = t - 6
            weights[t] = [Relay(net, p, columns(o_ref, 2048, j, 512), wo.at[j], relo.at[j])]

    def act_f(t, way):
        for w in weights[t]:
            w.forward(way)

    def wait_weights(t):
        for w in weights.pop(t, ()):
            w.wait()

    def slot_order(slot):
        return order((0, 2)[slot - 16] if slot >= 16 else slot % 4)

    def place_in(o, nat):
        return 8 * nat[o[0]] + 4 * nat[o[1]] + 2 * nat[o[2]] + nat[o[3]]

    def scatter(slot, k):
        o, n = slot_order(slot), 8 >> k
        at = prefix(p.bits, o, k) + (1 - p.bits[o[k]]) * n
        flying["r", slot, k] = net.remote(
            part.at[slot, pl.ds(at, n)], recvs[k].at[slot], p.partners[o[k]]
        )

    def act_p(t, pair=0):
        arrive_once("c1", "c2", "h1", "h2", "h3", "h4", "h5", "h6")
        wait_weights(t)
        if t == 0:
            slots = (16, 17)
        else:
            slots = range(QUERIES[t][0] + 2 * pair, QUERIES[t][0] + 2 * pair + 2)
            j, at, _ = query_weights(t)
            at = at + 256 * pair

        def step(m, carry):
            x = xs[pl.ds(pl.multiple_of(m * 1024, 1024), 1024), :]
            if t == 0:
                w = jnp.concatenate([wkv[0], wkv[1]], axis=1)
            else:
                w = wq[j, :, at : at + 256]
            y = jnp.dot(x, w, preferred_element_type=F32).astype(BF16)
            for i in range(8):
                nat = (m, i // 4, i // 2 % 2, i % 2)
                for g, slot in enumerate(slots):
                    part[slot, place_in(slot_order(slot), nat)] = y[
                        i * BLOCK : (i + 1) * BLOCK, g * HEAD : (g + 1) * HEAD
                    ]
            return carry

        lax.fori_loop(0, 2, step, 0)
        for slot in slots:
            scatter(slot, 0)

    def rope(u):
        while table_copies:
            table_copies.pop().wait()
        return u * cos[...] + pltpu.roll(u, 64, 1) * sin[...]

    queries = {}

    def act_c(slot, k):
        arrive(("r", slot, k))
        o, n = slot_order(slot), 8 >> k
        at = prefix(p.bits, o, k + 1)
        if k < 3:
            for i in range(n):
                part[slot, at + i] = part[slot, at + i] + recvs[k][slot, i]
            scatter(slot, k + 1)
            return
        total = part[slot, at].astype(F32) + recvs[k][slot, 0].astype(F32)
        if slot < 16:
            queries[slot] = (rope(total) * (math.log2(math.e) / math.sqrt(HEAD))).astype(BF16)
        else:
            which = slot - 16
            kv[which, WINDOW - 1] = (total if which else rope(total)).astype(BF16)
            for d in range(1, WINDOW):
                flying["window", which, d] = net.remote(
                    kv.at[which, WINDOW - 1],
                    kv.at[which, WINDOW - 1 - d],
                    p.block_dev(p.token_block + d),
                )

    def gather(slot, i):
        o, k = slot_order(slot), 3 - i
        at = pl.ds(prefix(p.bits, o, k + 1), 1 << i)
        if i < WHOLE_STAGES:
            blocks = att.at[slot, at]
            flying["g", slot, i] = net.remote(blocks, blocks, p.partners[o[k]])

    def gather_half(slot, i, half):
        o, k = slot_order(slot), 3 - i
        at = pl.ds(prefix(p.bits, o, k + 1), 1 << i)
        blocks = att.at[slot, at, pl.ds(*HALVES[half])]
        flying["g", slot, i, half] = net.remote(blocks, blocks, p.partners[o[k]])

    def gather_on(slot, i):
        if i < WHOLE_STAGES:
            gather(slot, i)
        else:
            for half in GATHER_HALVES:
                gather_half(slot, i, half)

    def act_a(u):
        arrive_once(*[("window", which, d) for which in range(2) for d in range(1, WINDOW)])
        slots = range(4 * u, 4 * u + 4)
        scores = lax.dot_general(
            jnp.concatenate([queries.pop(slot) for slot in slots], axis=0),
            kv[0].reshape(WINDOW * BLOCK, HEAD),
            (((1,), (1,)), ((), ())),
            preferred_element_type=F32,
        )
        scores = scores.reshape(4, BLOCK, WINDOW * BLOCK) + bias[...][None]
        scores = scores.reshape(4 * BLOCK, WINDOW * BLOCK)
        exponent = jnp.exp2(scores - jnp.max(scores, axis=-1, keepdims=True))
        denominator = jnp.sum(exponent, axis=-1, keepdims=True)
        attended = jnp.dot(
            exponent.astype(BF16),
            kv[1].reshape(WINDOW * BLOCK, HEAD),
            preferred_element_type=F32,
        )
        attended = (attended * (1.0 / denominator)).astype(BF16)
        for s, slot in enumerate(slots):
            att[slot, prefix(p.bits, order(s), 4)] = attended[s * BLOCK : (s + 1) * BLOCK]
            gather_on(slot, 0)

    def act_g(slot, i, *half):
        arrive(("g", slot, i, *half))
        if half:
            gather_half(slot, i + 1, *half)
        else:
            gather_on(slot, i + 1)

    def attended_rows(u, half):
        low, size = HALVES[half]
        blocks = []
        for i in range(16):
            nat = (i // 8, i // 4 % 2, i // 2 % 2, i % 2)
            blocks.append(
                jnp.concatenate(
                    [att[4 * u + s, place_in(order(s), nat), low : low + size] for s in range(4)],
                    axis=1,
                )
            )
        return jnp.concatenate(blocks, axis=0)

    def act_o(u, half):
        wait_weights(6 + u)
        arrive(*[("g", 4 * u + s, 3, half) for s in range(4)])
        total = acc[half]

        def step(f, carry):
            term = lax.dot_general(
                attended_rows(u, half), wo[u, rows(4 * f, 4)], (((1,), (1,)), ((), ())),
                preferred_element_type=F32,
            )
            total[f] = term if u == 0 else total[f] + term
            return carry

        lax.fori_loop(0, 2, step, 0)

    y, ya, yb, yab = p.y, p.ya, p.yb, p.yab

    late, ready, results = [], [], []

    def act_l(half, f):
        wait_weights(9)
        arrive_once(*[("g", 12 + s, 3, half) for s in range(4)])
        size = HALVES[half][1]

        term = lax.dot_general(
            attended_rows(3, half), wo[3, f * 512 : (f + 1) * 512], (((1,), (1,)), ((), ())),
            preferred_element_type=F32,
        )
        total = (acc[half][f] + term).astype(BF16)
        for i in range(16):
            po[half][f, i % 2, i // 2] = total[i * size : (i + 1) * size]
        flying["c", half, f] = net.remote(po[half].at[f, p.oc], rc[half].at[f], to_core, late)
        ready.append((half, f))
        if len(ready) == 4:
            net.finish()

    def act_u(stage, half, f):
        mine, key = po[half].at[f, p.c], ("u", stage, half, f)
        one, two = ones[half].at[f], twos[half].at[f]

        def add(at, other):
            mine[at] = mine[at] + other

        def hand(block, dst, dev):
            flying["u", stage + 1, half, f, len(flying)] = net.remote(
                mine.at[block], dst, dev, late
            )

        if stage == 0:
            arrive(("c", half, f))
            for i in range(8):
                add(i, rc[half][f, i])
            hand(2 * yab + p.zh, one.at[0, 0], to_a)
            hand(2 * yab + oz, one.at[1, 0], to_b)
            hand(2 * ya + p.zh, one.at[0, 1], to_a)
            hand(2 * yb + oz, one.at[1, 1], to_b)
            return
        arrive(*[k for k in flying if k[:4] == key])
        if stage == 1:
            add(2 * yb + p.zh, one[0, 0])
            hand(2 * yb + p.zh, two.at[0], to_b)
            add(2 * ya + oz, one[1, 0])
            hand(2 * ya + oz, two.at[1], p.dev(y=ya, zh=oz))
            add(2 * y + oz, one[1, 1])
            hand(2 * y + oz, two.at[2], p.dev(zh=oz))
            add(2 * y + p.zh, one[0, 1])
            return
        low, size = HALVES[half]
        here, there = mine[2 * y + p.zh] + two[0], two[1] + two[2]
        for z in range(2):
            part_z = jnp.where(p.zh == z, here, there)
            for e in range(2):
                at = (2 * f + e) * 512 + z * 256
                fin[low : low + size, at : at + 256] = part_z[:, e * 256 : (e + 1) * 256]
        piece = (pl.ds(low, size), pl.ds(f * 1024, 1024))
        results.append(net.local(fin.at[piece], out_ref.at[piece]))

    seg_q = jnp.transpose(
        jnp.broadcast_to(seg_ref[pl.ds(p.token_block, 1), :], (BLOCK, BLOCK))
    )
    lane = lax.broadcasted_iota(jnp.int32, (BLOCK, BLOCK), 1)
    query = p.token_block * BLOCK + lax.broadcasted_iota(jnp.int32, (BLOCK, BLOCK), 0)
    for i in range(WINDOW):
        b = lax.rem(p.token_block + 16 - (WINDOW - 1) + i, 16)
        allowed = (b * BLOCK + lane <= query) & (seg_ref[pl.ds(b, 1), :] == seg_q)
        bias[:, i * BLOCK : (i + 1) * BLOCK] = jnp.where(allowed, F32(0), F32(NEGATIVE))

    actions = dict(
        H=act_h, S=act_s, F=act_f, P=act_p, C=act_c, A=act_a, G=act_g, O=act_o, L=act_l, U=act_u
    )
    for name, *arguments in ORDER:
        actions[name](*arguments)
    for cp in late:
        cp.wait_send()
    for cp in results:
        cp.wait()


def body(hidden_in, segment_ids, q_weight, k_weight, value_weight, out_weight):
    vmem = pl.BlockSpec(memory_space=pltpu.VMEM)
    hbm = pl.BlockSpec(memory_space=pl.ANY)
    cos, sin = tables()
    blocks = lambda *shape: pltpu.VMEM(shape, BF16)
    sizes = [size for _, size in HALVES]
    return pl.pallas_call(
        kernel,
        out_shape=jax.ShapeDtypeStruct((BLOCK, 2048), BF16),
        in_specs=[vmem, vmem, hbm, hbm, hbm, hbm, hbm, hbm],
        out_specs=hbm,
        scratch_shapes=[
            blocks(2, BLOCK, 1024),
            blocks(2, 64, 1024),
            blocks(2048, 1024),
            blocks(2, 1024, HEAD),
            blocks(4, 1024, 512),
            blocks(2, 2, BLOCK, HEAD),
            blocks(4, 2, BLOCK, 512),
            blocks(18, 16, BLOCK, HEAD),
            blocks(18, 8, BLOCK, HEAD),
            blocks(18, 4, BLOCK, HEAD),
            blocks(18, 2, BLOCK, HEAD),
            blocks(18, 1, BLOCK, HEAD),
            pltpu.VMEM((BLOCK, HEAD), F32),
            pltpu.VMEM((BLOCK, HEAD), F32),
            blocks(2, WINDOW, BLOCK, HEAD),
            pltpu.VMEM((BLOCK, WINDOW * BLOCK), F32),
            blocks(16, 16, BLOCK, HEAD),
            blocks(4, 1024, 512),
            blocks(4, 2, BLOCK, 512),
            *[pltpu.VMEM((2, 16 * size, 512), F32) for size in sizes],
            *[blocks(2, 2, 8, size, 512) for size in sizes],
            *[blocks(2, 8, size, 512) for size in sizes],
            *[blocks(2, 2, 2, size, 512) for size in sizes],
            *[blocks(2, 3, size, 512) for size in sizes],
            blocks(BLOCK, 2048),
            pltpu.SemaphoreType.DMA((SEMAPHORES,)),
            pltpu.SemaphoreType.DMA((SEMAPHORES,)),
        ],
        compiler_params=pltpu.CompilerParams(
            collective_id=0, has_side_effects=True, vmem_limit_bytes=63 << 20
        ),
    )(hidden_in, segment_ids.reshape(16, BLOCK), cos, sin, q_weight, k_weight, value_weight,
      out_weight)


def solution(mesh):
    placed = (
        P("col", "row"),
        P(),
        P(("row", "col"), None),
        P(("row", "col"), None),
        P(("row", "col"), None),
        P(("row", "col"), None),
    )
    return jax.shard_map(
        body, mesh=mesh, in_specs=placed, out_specs=P("col", "row"), check_vma=False
    )
```

```python
import math

import jax
import jax.numpy as jnp
import numpy as np
from jax import lax
from jax.experimental import pallas as pl
from jax.experimental.pallas import tpu as pltpu
from jax.sharding import PartitionSpec as P

HEAD = 128
BLOCK = 128
THETA = 500000.0
NEGATIVE = -1e30
SEMAPHORES = 400
WINDOW = 5
F32 = jnp.float32
BF16 = jnp.bfloat16
MESH = pl.DeviceIdType.MESH


class Place:
    def __init__(self):
        row, col = lax.axis_index("row"), lax.axis_index("col")
        self.x, self.zl = lax.div(row, 2), lax.rem(row, 2)
        self.y, self.zh, self.c = lax.div(col, 4), lax.rem(lax.div(col, 2), 2), lax.rem(col, 2)
        self.col = col
        self.oc = 1 - self.c
        x, y, zl, zh = self.x, self.y, self.zl, self.zh
        self.ya, self.yb = y + 1 - 2 * lax.rem(y, 2), 3 - y
        self.yab = 3 - self.ya
        self.xa, self.xb = x + 1 - 2 * lax.rem(x, 2), 3 - x
        self.bits = (lax.div(x, 2), lax.rem(x + lax.div(x, 2), 2), zh, lax.rem(zl + zh, 2))
        self.partners = (
            self.dev(x=self.xb),
            self.dev(x=self.xa),
            self.dev(zh=1 - zh, zl=1 - zl),
            self.dev(zl=1 - zl),
        )
        self.token_block = (
            8 * self.bits[0] + 4 * self.bits[1] + 2 * self.bits[2] + self.bits[3]
        )

    def dev(self, **k):
        g = lambda n: k.get(n, getattr(self, n))
        return (2 * g("x") + g("zl"), 4 * g("y") + 2 * g("zh") + g("c"))

    def ycore_partners(self):
        return [
            self.dev(c=self.oc),
            self.dev(y=self.ya),
            self.dev(y=self.ya, c=self.oc),
            self.dev(y=self.yb),
            self.dev(y=self.yb, c=self.oc),
        ]

    def block_dev(self, t):
        t = lax.rem(t + 16, 16)
        n0, n1 = lax.div(t, 8), lax.rem(lax.div(t, 4), 2)
        n2, n3 = lax.rem(lax.div(t, 2), 2), lax.rem(t, 2)
        return self.dev(x=2 * n0 + lax.rem(n0 + n1, 2), zh=n2, zl=lax.rem(n2 + n3, 2))

    def all_partners(self):
        window = [self.block_dev(self.token_block + d) for i in range(1, WINDOW) for d in (i, -i)]
        return (
            self.ycore_partners()
            + [self.dev(y=y, zh=1 - self.zh) for y in (self.y, self.ya, self.yb)]
            + list(self.partners)
            + window
        )


def order(s):
    return [(s + k) % 4 for k in range(4)]


def barrier(devices):
    sem = pltpu.get_barrier_semaphore()
    for d in devices:
        pl.semaphore_signal(sem, inc=1, device_id=d, device_id_type=MESH)
    pl.semaphore_wait(sem, len(devices))


class Net:
    def __init__(self, send, recv):
        self.send, self.recv, self.n, self.open = send, recv, 0, []

    def remote(self, src, dst, dev, into=None):
        i = self.n
        self.n += 1
        cp = pltpu.make_async_remote_copy(
            src, dst, self.send.at[i], self.recv.at[i], device_id=dev, device_id_type=MESH
        )
        cp.start()
        (self.open if into is None else into).append(cp)
        return cp

    def local(self, src, dst):
        i = self.n
        self.n += 1
        cp = pltpu.make_async_copy(src, dst, self.recv.at[i])
        cp.start()
        return cp

    def finish(self):
        for cp in self.open:
            cp.wait_send()
        self.open = []


def rows(i, n=1):
    return pl.ds(pl.multiple_of(i * BLOCK, BLOCK), n * BLOCK)


class Relay:
    def __init__(self, net, p, src, dst, rel):
        self.net, self.p, self.src, self.dst, self.rel = net, p, src, dst, rel
        self.waits = []
        self.ra = net.remote(src(2 * p.yab + p.c), rel.at[0], p.dev(y=p.ya))
        self.rb = net.remote(src(2 * p.yab + p.oc), rel.at[1], p.dev(y=p.yb))

    def start(self):
        net, p, src = self.net, self.p, self.src
        y, c, oc = p.y, p.c, p.oc
        mine = self.dst.at[rows(2 * y + c)]
        self.waits += [
            net.remote(src(2 * p.ya + c), mine, p.dev(y=p.ya)),
            net.remote(src(2 * p.yb + c), mine, p.dev(y=p.yb)),
            net.remote(src(2 * p.ya + oc), mine, p.dev(y=p.ya, c=oc)),
            net.remote(src(2 * p.yb + oc), mine, p.dev(y=p.yb, c=oc)),
            net.remote(src(2 * y + oc), mine, p.dev(c=oc)),
        ]
        self.own = net.local(src(2 * y + c), mine)

    def forward(self, way):
        p = self.p
        (self.ra, self.rb)[way].wait_recv()
        origin = (p.ya, p.yb)[way]
        to = (p.dev(y=p.yb), p.dev(y=p.ya, c=p.oc))[way]
        self.waits.append(
            self.net.remote(self.rel.at[way], self.dst.at[rows(2 * origin + p.c)], to)
        )

    def wait(self):
        self.own.wait()
        for cp in self.waits:
            cp.wait_recv()


def prefix(bits, o, k):
    total = 0
    for i in range(k):
        total = total + bits[o[i]] * (8 >> i)
    return total


def tables():
    inverse = np.power(np.float32(THETA), -2.0 * np.arange(64, dtype=np.float32) / HEAD)
    angles = np.arange(2048, dtype=np.float32)[:, None] * inverse.astype(np.float32)[None, :]
    angles = angles.astype(np.float64)
    cos, sin = np.cos(angles), np.sin(angles)
    cos = np.concatenate([cos, cos], axis=1).astype(np.float32)
    sin = np.concatenate([-sin, sin], axis=1).astype(np.float32)
    return cos, sin


QUERIES = {1: (0, 2), 2: (2, 2), 3: (4, 4), 4: (8, 4), 5: (12, 4)}
HALVES = ((0, 48), (48, 80))
GATHER_HALVES = (0, 1)
WHOLE_STAGES = 0
ORDER = (
    ("S",1,0), ("S",0,0), ("S",2,0), ("H","z0"), ("H","z1"), ("H","swap"), ("H","a1"),
    ("F",0,1), ("F",1,1), ("F",1,0), ("F",0,0), ("H","b2"), ("H","b1"), ("S",1,1),
    ("S",0,1), ("F",2,0), ("F",2,1), ("H","a2"), ("S",2,1), ("S",3,0), ("S",3,1),
    ("H","f1"), ("H","f2"), ("P",1), ("P",0), ("P",2), ("C",0,0), ("F",3,1), ("F",3,0),
    ("C",1,0), ("S",4,0), ("C",17,0), ("C",16,0), ("C",3,0), ("C",0,1), ("S",4,1),
    ("C",2,0), ("P",3,0), ("P",3,1), ("C",17,1), ("C",16,1), ("C",2,1), ("C",3,1),
    ("F",4,1), ("F",4,0), ("S",5,0), ("C",1,1), ("S",5,1), ("C",0,2), ("C",4,0), ("C",5,0),
    ("C",6,0), ("C",7,0), ("C",17,2), ("C",3,2), ("P",4,0), ("C",16,2), ("P",4,1),
    ("C",5,1), ("F",5,1), ("F",5,0), ("S",6,0), ("C",7,1), ("S",7,0), ("C",17,3), ("S",8,0),
    ("C",2,2), ("C",3,3), ("C",1,2), ("S",9,0), ("S",6,1), ("C",6,1), ("C",4,1), ("C",0,3),
    ("C",16,3), ("C",8,0), ("C",9,0), ("C",7,2), ("C",10,0), ("C",11,0), ("P",5,0),
    ("C",4,2), ("P",5,1), ("C",1,3), ("F",6,1), ("S",8,1), ("C",2,3), ("C",6,2), ("F",6,0),
    ("A",0), ("C",7,3), ("C",9,1), ("C",5,2), ("F",7,0), ("C",10,1), ("C",11,1), ("C",8,1),
    ("C",4,3), ("F",7,1), ("C",13,0), ("F",8,1), ("C",12,0), ("F",8,0), ("G",2,0,0),
    ("C",6,3), ("G",1,0,0), ("F",9,1), ("G",2,0,1), ("C",14,0), ("C",15,0), ("C",5,3),
    ("G",3,0,1), ("G",0,0,1), ("A",1), ("G",1,0,1), ("C",11,2), ("G",3,0,0), ("C",9,2),
    ("C",8,2), ("C",10,2), ("G",0,0,0), ("C",13,1), ("C",12,1), ("C",14,1), ("G",0,1,1),
    ("G",2,1,0), ("G",3,1,1), ("G",1,1,0), ("G",4,0,1), ("G",6,0,0), ("G",5,0,0),
    ("C",15,1), ("G",7,0,1), ("G",6,0,1), ("G",2,1,1), ("G",5,0,1), ("G",4,0,0),
    ("G",3,1,0), ("C",9,3), ("G",1,1,1), ("C",11,3), ("C",10,3), ("G",7,0,0), ("C",8,3),
    ("G",0,1,0), ("A",2), ("C",12,2), ("C",13,2), ("G",4,1,0), ("C",15,2), ("G",5,1,0),
    ("G",3,2,1), ("G",7,1,1), ("C",14,2), ("G",4,1,1), ("G",5,1,1), ("G",0,2,1),
    ("G",8,0,0), ("G",7,1,0), ("S",7,1), ("G",9,0,0), ("G",2,2,1), ("G",11,0,1), ("C",13,3),
    ("G",1,2,1), ("C",12,3), ("G",9,0,1), ("C",15,3), ("F",9,0), ("C",14,3), ("G",6,1,1),
    ("A",3), ("G",10,0,1), ("G",7,2,1), ("G",8,0,1), ("G",9,1,1), ("G",5,2,1), ("G",11,0,0),
    ("G",10,0,0), ("S",9,1), ("G",11,1,1), ("G",12,0,0), ("G",15,0,1), ("G",14,0,0),
    ("G",14,0,1), ("G",12,0,1), ("G",13,0,1), ("G",13,0,0), ("G",4,2,1), ("G",8,1,1),
    ("G",10,1,1), ("G",15,0,0), ("G",6,2,1), ("O",0,1), ("G",14,1,1), ("G",13,1,1),
    ("G",12,1,1), ("G",6,1,0), ("G",15,1,1), ("G",9,2,1), ("G",11,2,1), ("G",10,2,1),
    ("G",8,2,1), ("G",14,2,1), ("G",9,1,0), ("G",15,2,1), ("G",12,2,1), ("G",15,1,0),
    ("G",10,1,0), ("G",13,1,0), ("G",2,2,0), ("G",14,1,0), ("G",6,2,0), ("G",13,2,1),
    ("G",8,1,0), ("G",3,2,0), ("G",12,1,0), ("G",11,1,0), ("G",1,2,0), ("G",5,2,0),
    ("G",0,2,0), ("O",1,1), ("G",4,2,0), ("O",2,1), ("G",7,2,0), ("L",1,1), ("G",9,2,0),
    ("G",10,2,0), ("G",14,2,0), ("G",13,2,0), ("L",1,0), ("G",8,2,0), ("G",12,2,0),
    ("G",11,2,0), ("O",0,0), ("G",15,2,0), ("U",0,1,1), ("O",1,0), ("U",0,1,0), ("O",2,0),
    ("L",0,1), ("U",1,1,1), ("L",0,0), ("U",0,0,1), ("U",1,1,0), ("U",0,0,0), ("U",2,1,1),
    ("U",1,0,1), ("U",1,0,0), ("U",2,1,0), ("U",2,0,1), ("U",2,0,0),
)


def kernel(
    h_ref, seg_ref, cos_ref, sin_ref, q_ref, k_ref, v_ref, o_ref,
    out_ref,
    hx, hop, xs, wkv, wq, relkv, relq, part, r0, r1, r2, r3, cos, sin, kv, bias,
    att, wo, relo, acc0, acc1, po0, po1, rc0, rc1, ones0, ones1, twos0, twos1, fin, send, recv,
):
    p = Place()
    net = Net(send, recv)
    recvs = (r0, r1, r2, r3)
    acc, po, rc = (acc0, acc1), (po0, po1), (rc0, rc1)
    ones, twos = (ones0, ones1), (twos0, twos1)
    inputs = []
    for z, dst in ((1 - p.zh, hx), (p.zh, xs.at[rows(p.col)])):
        for yy in range(4):
            at = pl.ds(pl.multiple_of(yy * 512 + z * 256, 256), 256)
            inputs.append(net.local(h_ref.at[:, at], dst.at[:, pl.ds(yy * 256, 256)]))
    barrier(p.all_partners())
    for cp in inputs:
        cp.wait()

    flying = {}

    def arrive(*keys):
        for key in keys:
            flying.pop(key).wait_recv()

    def arrive_once(*keys):
        arrive(*[key for key in keys if key in flying])

    to_a, to_b, to_core = p.dev(y=p.ya), p.dev(y=p.yb), p.dev(c=p.oc)
    oz = 1 - p.zh

    def push(key, y, zh, dev):
        block = xs.at[rows(4 * y + 2 * zh + p.c)]
        flying[key] = net.remote(block, block, dev)

    (to_zb, to_za), low, high = p.partners[2:], pl.ds(0, 64), pl.ds(64, 64)
    flying["z0"] = net.remote(hx.at[low], hop.at[0], to_za)
    flying["z1"] = net.remote(hx.at[high], hop.at[1], to_zb)
    push("a1", p.y, p.zh, to_a)
    push("b1", p.y, p.zh, to_b)
    push("c1", p.y, p.zh, to_core)
    table_copies = [
        net.local(cos_ref.at[rows(p.token_block)], cos),
        net.local(sin_ref.at[rows(p.token_block)], sin),
    ]

    def half_rows(zh, first):
        return xs.at[pl.ds(pl.multiple_of((4 * p.y + 2 * zh + p.c) * BLOCK + first, 64), 64)]

    def act_h(name):
        if name == "swap":
            arrive("swap0", "swap1")
        else:
            arrive(name)
        if name == "z0":
            flying["swap0"] = net.remote(hop.at[0], half_rows(p.zh, 0), to_zb)
        elif name == "z1":
            flying["swap1"] = net.remote(hop.at[1], half_rows(oz, 64), to_za)
        elif name == "a1":
            push("f1", p.ya, p.zh, to_b)
            push("h1", p.ya, p.zh, to_core)
        elif name == "b1":
            push("h2", p.yb, p.zh, to_core)
        elif name == "swap":
            push("a2", p.y, oz, to_a)
            push("b2", p.y, oz, to_b)
            push("c2", p.y, oz, to_core)
        elif name == "b2":
            push("f2", p.yb, oz, to_a)
            push("h3", p.yb, oz, to_core)
        elif name == "a2":
            push("h4", p.ya, oz, to_core)
        elif name == "f1":
            push("h5", p.yab, p.zh, to_core)
        elif name == "f2":
            push("h6", p.yab, oz, to_core)

    def columns(ref, width, j=0, chunk=None):
        chunk = chunk or width
        return lambda d: ref.at[:, pl.ds(pl.multiple_of(d * width + j * chunk, chunk), chunk)]

    weights = {}

    def query_weights(t):
        first, count = QUERIES[t]
        return first // 4, first % 4 * HEAD, count * HEAD

    def act_s(t, part):
        if part:
            for relay in weights[t]:
                relay.start()
        elif t == 0:
            weights[t] = [
                Relay(net, p, columns(k_ref, HEAD), wkv.at[0], relkv.at[0]),
                Relay(net, p, columns(v_ref, HEAD), wkv.at[1], relkv.at[1]),
            ]
        elif t < 6:
            j, at, width = query_weights(t)
            weights[t] = [
                Relay(
                    net, p,
                    columns(q_ref, 2048, QUERIES[t][0] * HEAD // width, width),
                    wq.at[j, :, pl.ds(at, width)],
                    relq.at[j, :, :, pl.ds(at, width)],
                )
            ]
        else:
            j = t - 6
            weights[t] = [Relay(net, p, columns(o_ref, 2048, j, 512), wo.at[j], relo.at[j])]

    def act_f(t, way):
        for w in weights[t]:
            w.forward(way)

    def wait_weights(t):
        for w in weights.pop(t, ()):
            w.wait()

    def slot_order(slot):
        return order((0, 2)[slot - 16] if slot >= 16 else slot % 4)

    def place_in(o, nat):
        return 8 * nat[o[0]] + 4 * nat[o[1]] + 2 * nat[o[2]] + nat[o[3]]

    def scatter(slot, k):
        o, n = slot_order(slot), 8 >> k
        at = prefix(p.bits, o, k) + (1 - p.bits[o[k]]) * n
        flying["r", slot, k] = net.remote(
            part.at[slot, pl.ds(at, n)], recvs[k].at[slot], p.partners[o[k]]
        )

    def act_p(t, pair=0):
        arrive_once("c1", "c2", "h1", "h2", "h3", "h4", "h5", "h6")
        wait_weights(t)
        if t == 0:
            slots = (16, 17)
        else:
            slots = range(QUERIES[t][0] + 2 * pair, QUERIES[t][0] + 2 * pair + 2)
            j, at, _ = query_weights(t)
            at = at + 256 * pair

        def step(m, carry):
            x = xs[pl.ds(pl.multiple_of(m * 1024, 1024), 1024), :]
            if t == 0:
                w = jnp.concatenate([wkv[0], wkv[1]], axis=1)
            else:
                w = wq[j, :, at : at + 256]
            y = jnp.dot(x, w, preferred_element_type=F32).astype(BF16)
            for i in range(8):
                nat = (m, i // 4, i // 2 % 2, i % 2)
                for g, slot in enumerate(slots):
                    part[slot, place_in(slot_order(slot), nat)] = y[
                        i * BLOCK : (i + 1) * BLOCK, g * HEAD : (g + 1) * HEAD
                    ]
            return carry

        lax.fori_loop(0, 2, step, 0)
        for slot in slots:
            scatter(slot, 0)

    def rope(u):
        while table_copies:
            table_copies.pop().wait()
        return u * cos[...] + pltpu.roll(u, 64, 1) * sin[...]

    queries = {}

    def act_c(slot, k):
        arrive(("r", slot, k))
        o, n = slot_order(slot), 8 >> k
        at = prefix(p.bits, o, k + 1)
        if k < 3:
            for i in range(n):
                part[slot, at + i] = part[slot, at + i] + recvs[k][slot, i]
            scatter(slot, k + 1)
            return
        total = part[slot, at].astype(F32) + recvs[k][slot, 0].astype(F32)
        if slot < 16:
            queries[slot] = (rope(total) * (math.log2(math.e) / math.sqrt(HEAD))).astype(BF16)
        else:
            which = slot - 16
            kv[which, WINDOW - 1] = (total if which else rope(total)).astype(BF16)
            for d in range(1, WINDOW):
                flying["window", which, d] = net.remote(
                    kv.at[which, WINDOW - 1],
                    kv.at[which, WINDOW - 1 - d],
                    p.block_dev(p.token_block + d),
                )

    def gather(slot, i):
        o, k = slot_order(slot), 3 - i
        at = pl.ds(prefix(p.bits, o, k + 1), 1 << i)
        if i < WHOLE_STAGES:
            blocks = att.at[slot, at]
            flying["g", slot, i] = net.remote(blocks, blocks, p.partners[o[k]])

    def gather_half(slot, i, half):
        o, k = slot_order(slot), 3 - i
        at = pl.ds(prefix(p.bits, o, k + 1), 1 << i)
        blocks = att.at[slot, at, pl.ds(*HALVES[half])]
        flying["g", slot, i, half] = net.remote(blocks, blocks, p.partners[o[k]])

    def gather_on(slot, i):
        if i < WHOLE_STAGES:
            gather(slot, i)
        else:
            for half in GATHER_HALVES:
                gather_half(slot, i, half)

    def act_a(u):
        arrive_once(*[("window", which, d) for which in range(2) for d in range(1, WINDOW)])
        slots = range(4 * u, 4 * u + 4)
        scores = lax.dot_general(
            jnp.concatenate([queries.pop(slot) for slot in slots], axis=0),
            kv[0].reshape(WINDOW * BLOCK, HEAD),
            (((1,), (1,)), ((), ())),
            preferred_element_type=F32,
        )
        scores = scores.reshape(4, BLOCK, WINDOW * BLOCK) + bias[...][None]
        scores = scores.reshape(4 * BLOCK, WINDOW * BLOCK)
        exponent = jnp.exp2(scores - jnp.max(scores, axis=-1, keepdims=True))
        denominator = jnp.sum(exponent, axis=-1, keepdims=True)
        attended = jnp.dot(
            exponent.astype(BF16),
            kv[1].reshape(WINDOW * BLOCK, HEAD),
            preferred_element_type=F32,
        )
        attended = (attended * (1.0 / denominator)).astype(BF16)
        for s, slot in enumerate(slots):
            att[slot, prefix(p.bits, order(s), 4)] = attended[s * BLOCK : (s + 1) * BLOCK]
            gather_on(slot, 0)

    def act_g(slot, i, *half):
        arrive(("g", slot, i, *half))
        if half:
            gather_half(slot, i + 1, *half)
        else:
            gather_on(slot, i + 1)

    def attended_rows(u, half):
        low, size = HALVES[half]
        blocks = []
        for i in range(16):
            nat = (i // 8, i // 4 % 2, i // 2 % 2, i % 2)
            blocks.append(
                jnp.concatenate(
                    [att[4 * u + s, place_in(order(s), nat), low : low + size] for s in range(4)],
                    axis=1,
                )
            )
        return jnp.concatenate(blocks, axis=0)

    def act_o(u, half):
        wait_weights(6 + u)
        arrive(*[("g", 4 * u + s, 3, half) for s in range(4)])
        total = acc[half]

        def step(f, carry):
            term = lax.dot_general(
                attended_rows(u, half), wo[u, rows(4 * f, 4)], (((1,), (1,)), ((), ())),
                preferred_element_type=F32,
            )
            total[f] = term if u == 0 else total[f] + term
            return carry

        lax.fori_loop(0, 2, step, 0)

    y, ya, yb, yab = p.y, p.ya, p.yb, p.yab

    late, ready, results = [], [], []

    def act_l(half, f):
        wait_weights(9)
        arrive_once(*[("g", 12 + s, 3, half) for s in range(4)])
        size = HALVES[half][1]

        term = lax.dot_general(
            attended_rows(3, half), wo[3, f * 512 : (f + 1) * 512], (((1,), (1,)), ((), ())),
            preferred_element_type=F32,
        )
        total = (acc[half][f] + term).astype(BF16)
        for i in range(16):
            po[half][f, i % 2, i // 2] = total[i * size : (i + 1) * size]
        flying["c", half, f] = net.remote(po[half].at[f, p.oc], rc[half].at[f], to_core, late)
        ready.append((half, f))
        if len(ready) == 4:
            net.finish()

    def act_u(stage, half, f):
        mine, key = po[half].at[f, p.c], ("u", stage, half, f)
        one, two = ones[half].at[f], twos[half].at[f]

        def add(at, other):
            mine[at] = mine[at] + other

        def hand(block, dst, dev):
            flying["u", stage + 1, half, f, len(flying)] = net.remote(
                mine.at[block], dst, dev, late
            )

        if stage == 0:
            arrive(("c", half, f))
            for i in range(8):
                add(i, rc[half][f, i])
            hand(2 * yab + p.zh, one.at[0, 0], to_a)
            hand(2 * yab + oz, one.at[1, 0], to_b)
            hand(2 * ya + p.zh, one.at[0, 1], to_a)
            hand(2 * yb + oz, one.at[1, 1], to_b)
            return
        arrive(*[k for k in flying if k[:4] == key])
        if stage == 1:
            add(2 * yb + p.zh, one[0, 0])
            hand(2 * yb + p.zh, two.at[0], to_b)
            add(2 * ya + oz, one[1, 0])
            hand(2 * ya + oz, two.at[1], p.dev(y=ya, zh=oz))
            add(2 * y + oz, one[1, 1])
            hand(2 * y + oz, two.at[2], p.dev(zh=oz))
            add(2 * y + p.zh, one[0, 1])
            return
        low, size = HALVES[half]
        here, there = mine[2 * y + p.zh] + two[0], two[1] + two[2]
        for z in range(2):
            part_z = jnp.where(p.zh == z, here, there)
            for e in range(2):
                at = (2 * f + e) * 512 + z * 256
                fin[low : low + size, at : at + 256] = part_z[:, e * 256 : (e + 1) * 256]
        piece = (pl.ds(low, size), pl.ds(f * 1024, 1024))
        results.append(net.local(fin.at[piece], out_ref.at[piece]))

    seg_q = jnp.transpose(
        jnp.broadcast_to(seg_ref[pl.ds(p.token_block, 1), :], (BLOCK, BLOCK))
    )
    lane = lax.broadcasted_iota(jnp.int32, (BLOCK, BLOCK), 1)
    query = p.token_block * BLOCK + lax.broadcasted_iota(jnp.int32, (BLOCK, BLOCK), 0)
    for i in range(WINDOW):
        b = lax.rem(p.token_block + 16 - (WINDOW - 1) + i, 16)
        allowed = (b * BLOCK + lane <= query) & (seg_ref[pl.ds(b, 1), :] == seg_q)
        bias[:, i * BLOCK : (i + 1) * BLOCK] = jnp.where(allowed, F32(0), F32(NEGATIVE))

    actions = dict(
        H=act_h, S=act_s, F=act_f, P=act_p, C=act_c, A=act_a, G=act_g, O=act_o, L=act_l, U=act_u
    )
    for name, *arguments in ORDER:
        actions[name](*arguments)
    for cp in late:
        cp.wait_send()
    for cp in results:
        cp.wait()


def body(hidden_in, segment_ids, q_weight, k_weight, value_weight, out_weight):
    vmem = pl.BlockSpec(memory_space=pltpu.VMEM)
    hbm = pl.BlockSpec(memory_space=pl.ANY)
    cos, sin = tables()
    blocks = lambda *shape: pltpu.VMEM(shape, BF16)
    sizes = [size for _, size in HALVES]
    return pl.pallas_call(
        kernel,
        out_shape=jax.ShapeDtypeStruct((BLOCK, 2048), BF16),
        in_specs=[hbm, vmem, hbm, hbm, hbm, hbm, hbm, hbm],
        out_specs=hbm,
        scratch_shapes=[
            blocks(BLOCK, 1024),
            blocks(2, 64, 1024),
            blocks(2048, 1024),
            blocks(2, 1024, HEAD),
            blocks(4, 1024, 512),
            blocks(2, 2, BLOCK, HEAD),
            blocks(4, 2, BLOCK, 512),
            blocks(18, 16, BLOCK, HEAD),
            blocks(18, 8, BLOCK, HEAD),
            blocks(18, 4, BLOCK, HEAD),
            blocks(18, 2, BLOCK, HEAD),
            blocks(18, 1, BLOCK, HEAD),
            pltpu.VMEM((BLOCK, HEAD), F32),
            pltpu.VMEM((BLOCK, HEAD), F32),
            blocks(2, WINDOW, BLOCK, HEAD),
            pltpu.VMEM((BLOCK, WINDOW * BLOCK), F32),
            blocks(16, 16, BLOCK, HEAD),
            blocks(4, 1024, 512),
            blocks(4, 2, BLOCK, 512),
            *[pltpu.VMEM((2, 16 * size, 512), F32) for size in sizes],
            *[blocks(2, 2, 8, size, 512) for size in sizes],
            *[blocks(2, 8, size, 512) for size in sizes],
            *[blocks(2, 2, 2, size, 512) for size in sizes],
            *[blocks(2, 3, size, 512) for size in sizes],
            blocks(BLOCK, 2048),
            pltpu.SemaphoreType.DMA((SEMAPHORES,)),
            pltpu.SemaphoreType.DMA((SEMAPHORES,)),
        ],
        compiler_params=pltpu.CompilerParams(
            collective_id=0, has_side_effects=True, vmem_limit_bytes=63 << 20
        ),
    )(hidden_in, segment_ids.reshape(16, BLOCK), cos, sin, q_weight, k_weight, value_weight,
      out_weight)


def solution(mesh):
    placed = (
        P("col", "row"),
        P(),
        P(("row", "col"), None),
        P(("row", "col"), None),
        P(("row", "col"), None),
        P(("row", "col"), None),
    )
    return jax.shard_map(
        body, mesh=mesh, in_specs=placed, out_specs=P("col", "row"), check_vma=False
    )
```
